512 devices in a mesh: blk: 256 (over z, x, y), rep: 2 (over core).
Axes of the slice: x: 4, y: 8, z: 8, core: 2. Of those that a mesh axis runs over, the one named last changes fastest.
Arguments:
- node_feat: bfloat16 [65536, 128], P('blk'), may hold values from -1 to 1.09375
- tile_values: bfloat16 [6144, 128, 128], P('blk'), may hold values from 0 to 0.049804688
- tile_rows: int32 [6144], P('blk'), may hold values from 0 to 1
- tile_cols: int32 [6144], P('blk'), may hold values from 0 to 511, as said below
- tile_count: int32 [256], P('blk'), may hold values from 7 to 24, as said below
- comp_ids: int32 [65536], P('blk'), may hold values from 0 to 255, as said below
- weight_in: bfloat16 [128, 256], replicated, may hold values from -0.5 to 0.5
- weight_hidden: bfloat16 [256, 256], replicated, may hold values from -0.375 to 0.375
- norm_params: float32 [2, 3, 256], replicated, may hold values from 0.5 to 1.5
- cotangent: bfloat16 [65536, 256], P('blk'), may hold values from -6 to 6
Outputs:
- node_out: bfloat16 [65536, 256], P('blk')
- grad_w1: float32 [128, 256], replicated
- grad_w2: float32 [256, 256], replicated
- grad_norm: float32 [2, 3, 256], replicated
The draws below stay inside these ranges and needn't reach their ends.
Inputs may be any that keep to these rules, and one draw needn't show every extreme that they name: `tile_cols`: slot k of block b names a column tile of node blocks b - 3 to b + 3, counted cyclically over the blocks; for k <= 6 it is a tile of block b + k - 3; column tile j covers nodes 128 * j onward. Slots from tile_count on are ignored. `comp_ids`: the nodes of each node block form four runs of consecutive nodes, each run of one component and at least 32 nodes long; every component has four runs.
All inputs are finite; a program needn't handle non-finite values.
Results may differ from the reference program's by a relative error of at most 0.009.
Values may be sent and summed in bfloat16 or wider, within the bound.
No kernel may reach another device: no remote copies, remote signals or barrier semaphores. Data moves between devices by JAX's collectives and lax.ppermute only.
A program may use at most 64 MiB of HBM per device.

```python
import jax
import jax.numpy as jnp
from jax import lax

F_IN = 128
HID = 256
TILE = 128
BAND = 3
NB = 256
TCAP = 24
RT = 2
NODES = 65536
NCOMP = 256
N_BLK = 256


def draw_tile_cols(key, part):
    key = jax.random.fold_in(key, 11)
    first_key, second_key = jax.random.split(key)
    slots = N_BLK * TCAP
    position = jnp.arange(slots, dtype=jnp.int32)
    block = position // TCAP
    within_block = position % TCAP
    random_offset = jax.random.randint(first_key, (slots,), -BAND, BAND + 1)
    offset = jnp.where(within_block <= 2 * BAND, within_block - BAND, random_offset)
    within = jax.random.randint(second_key, (slots,), 0, RT)
    return ((block + offset) % N_BLK * RT + within).astype(jnp.int32)


def draw_tile_count(key, part):
    key = jax.random.fold_in(key, 12)
    first_key, second_key = jax.random.split(key)
    least = max(TCAP // 16, 2 * BAND + 1)
    picks = jax.random.randint(first_key, (N_BLK,), 0, 17)
    counts = least + picks * picks * (TCAP - least) // 256
    fullest = jax.random.randint(second_key, (), 0, N_BLK)
    counts = counts.at[fullest].set(TCAP)
    return counts.astype(jnp.int32)


def draw_comp_ids(key, part):
    key = jax.random.fold_in(key, 13)
    first_key, second_key = jax.random.split(key)
    order = jax.random.permutation(first_key, 4 * N_BLK).astype(jnp.int32)
    cuts = jnp.sort(jax.random.randint(second_key, (N_BLK, 3), 0, NB // 2 + 1), axis=1)
    starts = jnp.arange(1, 4, dtype=jnp.int32)[None, :] * (NB // 8) + cuts
    nodes = jnp.arange(NB, dtype=jnp.int32)
    runs = jnp.sum((nodes[None, :, None] >= starts[:, None, :]).astype(jnp.int32), axis=2)
    table = order.reshape(N_BLK, 4)
    components = table[jnp.arange(N_BLK, dtype=jnp.int32)[:, None], runs] // 4
    return components.reshape(-1).astype(jnp.int32)


def set_ends(array, stream_key, low, high):
    shape = array.shape
    index_at = [jax.random.randint(jax.random.fold_in(stream_key, axis), (), 0, shape[axis]) for axis in range(len(shape))]
    array = array.at[tuple(index_at)].set(low)
    longest = shape.index(max(shape))
    index_at[longest] = (index_at[longest] + 1) % shape[longest]
    return array.at[tuple(index_at)].set(high)


def level_of(own_key, extent, shards, low, top_value):
    gain = 1.0
    for axis_at, blocks in shards:
        heights = jax.random.uniform(jax.random.fold_in(jax.random.fold_in(own_key, 6), axis_at), (blocks,), jnp.float32, low / len(shards), top_value / len(shards))
        gain = gain * jnp.repeat(jnp.exp(heights), extent[axis_at] // blocks).reshape((-1,) + (1,) * (len(extent) - 1 - axis_at))
    return gain


def bell_draw(rng, shape, scale, bound, cuts=(), kind=jnp.bfloat16):
    result = jax.random.normal(rng, shape, jnp.float32) * scale
    if len(cuts) > 0:
        result = level_of(rng, shape, cuts, -0.22, 0.18) * result
    return jnp.clip(result, min=-bound, max=bound).astype(kind)


def setup_inputs(seed: int = 0) -> dict:
    seeds = jax.random.split(jax.random.key(seed), 11)
    node_feat = jnp.clip(-1.0 + 2.09375 * jax.random.uniform(seeds[0], (NODES, F_IN), jnp.float32) ** level_of(seeds[0], (NODES, F_IN), ((0, 256),), -0.2, 0.2), -1.0, 1.09375).astype(jnp.bfloat16)
    tile_values = jnp.clip(0.049804688 * jax.random.uniform(seeds[1], (N_BLK * TCAP, TILE, TILE), jnp.float32) ** level_of(seeds[1], (N_BLK * TCAP, TILE, TILE), ((0, 256),), -0.2, 0.2), 0.0, 0.049804688).astype(jnp.bfloat16)
    tile_rows = set_ends(jax.random.randint(seeds[2], (N_BLK * TCAP,), 0, RT), jax.random.fold_in(seeds[2], 1), 0, RT - 1).astype(jnp.int32)
    tile_cols = draw_tile_cols(jax.random.fold_in(seeds[10], 71), 0)
    tile_count = draw_tile_count(jax.random.fold_in(seeds[10], 71), 0)
    comp_ids = draw_comp_ids(jax.random.fold_in(seeds[10], 71), 0)
    weight_in = bell_draw(seeds[6], (F_IN, HID), F_IN ** -0.5, 0.5)
    weight_hidden = bell_draw(seeds[7], (HID, HID), HID ** -0.5, 0.375)
    norm_params = jnp.clip(jax.random.uniform(seeds[8], (2, 3, HID), jnp.float32, 0.5, 1.5), 0.5, 1.5)
    cotangent = bell_draw(seeds[9], (NODES, HID), 1.0, 6.0, ((0, 256),))
    return {"node_feat": node_feat, "tile_values": tile_values, "tile_rows": tile_rows, "tile_cols": tile_cols, "tile_count": tile_count, "comp_ids": comp_ids, "weight_in": weight_in, "weight_hidden": weight_hidden, "norm_params": norm_params, "cotangent": cotangent}


EPSILON = 1e-05

def aggregate(tile_values, tile_rows, tile_cols, tile_count, features):
    width = features.shape[1]
    feature_tiles = features.reshape(NODES // TILE, TILE, width)

    def one_block(inputs):
        values, rows, columns, count = inputs
        valid = jnp.arange(TCAP, dtype=jnp.int32) < count
        picked = feature_tiles[columns].astype(jnp.float32)
        product = jnp.einsum('sij,sjw->siw', values.astype(jnp.float32), picked, precision=lax.Precision.HIGHEST)
        selector = ((rows[None, :] == jnp.arange(RT, dtype=jnp.int32)[:, None]) & valid[None, :]).astype(jnp.float32)
        return jnp.einsum('rs,siw->riw', selector, product, precision=lax.Precision.HIGHEST)
    stacked = lax.map(one_block, (tile_values.reshape(N_BLK, TCAP, TILE, TILE), tile_rows.reshape(N_BLK, TCAP), tile_cols.reshape(N_BLK, TCAP), tile_count))
    return stacked.reshape(NODES, width)

def aggregate_transposed(tile_values, tile_rows, tile_cols, tile_count, grads):
    width = grads.shape[1]
    grad_tiles = grads.reshape(NODES // TILE, TILE, width)

    def one_block(carry, inputs):
        values, rows, columns, count, block = inputs
        valid = jnp.arange(TCAP, dtype=jnp.int32) < count
        picked = grad_tiles[block * RT + rows].astype(jnp.float32)
        product = jnp.einsum('sji,sjw->siw', values.astype(jnp.float32), picked, precision=lax.Precision.HIGHEST)
        product = jnp.where(valid[:, None, None], product, jnp.zeros_like(product))
        return (carry.at[columns].add(product), None)
    start = jnp.zeros((NODES // TILE, TILE, width), jnp.float32)
    total, unused = lax.scan(one_block, start, (tile_values.reshape(N_BLK, TCAP, TILE, TILE), tile_rows.reshape(N_BLK, TCAP), tile_cols.reshape(N_BLK, TCAP), tile_count, jnp.arange(N_BLK, dtype=jnp.int32)))
    return total.reshape(NODES, width)

def graph_norm(values, comp_ids, params):
    gamma, beta, alpha = (params[0], params[1], params[2])
    count = jax.ops.segment_sum(jnp.ones((NODES,), jnp.float32), comp_ids, NCOMP)
    means = jax.ops.segment_sum(values, comp_ids, NCOMP) / count[:, None]
    centred = values - alpha * means[comp_ids]
    spread = jnp.sqrt(jax.ops.segment_sum(centred * centred, comp_ids, NCOMP) / count[:, None] + EPSILON)
    normed = centred / spread[comp_ids]
    return (gamma * normed + beta, (count, means, spread, normed))

def norm_backward(grads, comp_ids, params, saved):
    gamma, alpha = (params[0], params[2])
    count, means, spread, normed = saved
    row_sums = jax.ops.segment_sum(grads, comp_ids, NCOMP)
    projections = jax.ops.segment_sum(grads * normed, comp_ids, NCOMP)
    d_gamma = lax.optimization_barrier(jnp.sum(projections, axis=0))
    d_beta = lax.optimization_barrier(jnp.sum(row_sums, axis=0))
    total = gamma / spread * (row_sums - (1.0 - alpha) * means * projections / spread)
    d_alpha = -lax.optimization_barrier(jnp.sum(means * total, axis=0))
    d_centred = (gamma / spread)[comp_ids] * (grads - normed * (projections / count[:, None])[comp_ids])
    d_input = d_centred - alpha * (total / count[:, None])[comp_ids]
    return (d_input, jnp.stack([d_gamma, d_beta, d_alpha]))

def silu_grad(values):
    logistic = jax.nn.sigmoid(values)
    return logistic * (1.0 + values * (1.0 - logistic))

def reference(node_feat, tile_values, tile_rows, tile_cols, tile_count, comp_ids, weight_in, weight_hidden, norm_params, cotangent):
    agg_in = aggregate(tile_values, tile_rows, tile_cols, tile_count, node_feat).astype(jnp.bfloat16)
    z_first = jnp.dot(agg_in, weight_in, preferred_element_type=jnp.float32)
    y_first, saved_first = graph_norm(z_first, comp_ids, norm_params[0])
    hidden = jax.nn.silu(y_first).astype(jnp.bfloat16)
    projected = jnp.dot(hidden, weight_hidden, preferred_element_type=jnp.float32).astype(jnp.bfloat16)
    z_second = aggregate(tile_values, tile_rows, tile_cols, tile_count, projected)
    y_second, saved_second = graph_norm(z_second, comp_ids, norm_params[1])
    node_out = y_second.astype(jnp.bfloat16)
    d_out = cotangent.astype(jnp.float32) / jnp.sqrt(jnp.float32(NODES))
    d_second, grads_second = norm_backward(d_out, comp_ids, norm_params[1], saved_second)
    d_projected = aggregate_transposed(tile_values, tile_rows, tile_cols, tile_count, d_second.astype(jnp.bfloat16)).astype(jnp.bfloat16)
    grad_w2 = lax.dot_general(hidden, d_projected, (((0,), (0,)), ((), ())), preferred_element_type=jnp.float32)
    d_hidden = lax.dot_general(d_projected, weight_hidden, (((1,), (1,)), ((), ())), preferred_element_type=jnp.float32)
    d_first_y = d_hidden * silu_grad(y_first)
    d_first, grads_first = norm_backward(d_first_y, comp_ids, norm_params[0], saved_first)
    grad_w1 = lax.dot_general(agg_in, d_first.astype(jnp.bfloat16), (((0,), (0,)), ((), ())), preferred_element_type=jnp.float32)
    return (node_out, grad_w1, grad_w2, jnp.stack([grads_first, grads_second]))
```

```python
import jax
import jax.numpy as jnp
from jax import lax
from jax.sharding import PartitionSpec as P

BAND = 3
RUNS = 4
EPSILON = 1e-05
F32 = jnp.float32
BF16 = jnp.bfloat16
HIGH = lax.Precision.HIGHEST
AXES = ("blk", "rep")


def dot(a, b, contract):
    return lax.dot_general(a, b, (contract, ((), ())), precision=HIGH)


def other_core(x):
    return lax.ppermute(x, "rep", [(0, 1), (1, 0)])


def side_routes(blocks, distance, outward):
    routes = []
    for i in range(blocks):
        low, high = (i - distance) % blocks, (i + distance) % blocks
        if outward:
            routes += [(i * 2, low * 2), (i * 2 + 1, high * 2 + 1)]
        else:
            routes += [(low * 2, i * 2), (high * 2 + 1, i * 2 + 1)]
    return routes


def exchange(x):
    return lax.all_to_all(x, "blk", 0, 0, tiled=True)


def tile_products(pieces, values, rows, places, valid, row_tiles):
    tile = values.shape[1]
    width = pieces.shape[1]
    picked = pieces.reshape(-1, tile, width)[places]
    zero = jnp.zeros((), picked.dtype)
    masked = [
        jnp.where((valid & (rows == r))[:, None, None], picked, zero) for r in range(row_tiles)
    ]
    product = lax.dot_general(
        values,
        jnp.concatenate(masked, axis=2),
        (((0, 2), (0, 1)), ((), ())),
        preferred_element_type=F32,
    )
    return jnp.concatenate(
        [product[:, r * width : (r + 1) * width] for r in range(row_tiles)], axis=0
    )


def tile_transposed(grads, values, rows, places, valid, row_tiles, targets):
    tile = values.shape[1]
    width = grads.shape[1]
    picked = grads.reshape(row_tiles, tile, width)[rows]
    product = jnp.einsum("sji,sjw->siw", values, picked, preferred_element_type=F32)
    selector = (
        (places[None, :] == jnp.arange(targets, dtype=jnp.int32)[:, None]) & valid[None, :]
    ).astype(F32)
    summed = jnp.einsum("ps,siw->piw", selector, product, precision=HIGH)
    return summed.reshape(targets // row_tiles, row_tiles * tile, width)


def silu_grad(values):
    logistic = jax.nn.sigmoid(values)
    return logistic * (1.0 + values * (1.0 - logistic))


def shards(
    node_feat,
    tile_values,
    tile_rows,
    tile_cols,
    tile_count,
    comp_ids,
    weight_in,
    weight_hidden,
    norm_params,
    cotangent,
):
    nodes_here, features = node_feat.shape
    hidden_units = weight_hidden.shape[0]
    tile = tile_values.shape[1]
    row_tiles = nodes_here // tile
    blocks = lax.axis_size("blk")
    b = lax.axis_index("blk")
    r = lax.axis_index("rep")
    half = hidden_units // 2
    items = 2 * half // blocks
    f_half = features // 2
    h_half = hidden_units // 2

    valid = jnp.arange(tile_values.shape[0], dtype=jnp.int32) < tile_count[0]
    distance = (tile_cols // row_tiles - b) % blocks
    signed = jnp.where(distance > blocks // 2, distance - blocks, distance)
    own_side = (signed < 0) == (r == 0)
    slot_block = jnp.where(
        signed == 0, 0, jnp.where(own_side, jnp.abs(signed), BAND + jnp.abs(signed))
    )
    places = slot_block * row_tiles + tile_cols % row_tiles
    side_valid = valid & jnp.where(signed == 0, r == 0, own_side)
    side_places = jnp.where(side_valid, places, 0)

    node = jnp.arange(nodes_here, dtype=jnp.int32)
    changed = jnp.concatenate(
        [jnp.zeros((1,), jnp.int32), (comp_ids[1:] != comp_ids[:-1]).astype(jnp.int32)]
    )
    run_of = jnp.sum(
        jnp.where(node[None, :] <= node[:, None], changed[None, :], 0), axis=1
    )
    run_ids = jnp.arange(RUNS, dtype=jnp.int32)
    run_hot = run_of[:, None] == run_ids[None, :]
    sel = run_hot.astype(F32)
    n_run = jnp.sum(sel, axis=0)
    comp_run = jnp.max(jnp.where(run_hot, comp_ids[:, None], -1), axis=0).astype(F32)
    n_safe = jnp.maximum(n_run, 1.0)[:, None]

    def run_sums(x):
        return dot(sel, x, ((0,), (0,)))

    def at_nodes(table):
        return dot(sel, table, ((1,), (0,)))

    def to_owners(columns):
        k = columns.shape[1]
        doubled = jnp.broadcast_to(columns[:, None, :], (half, 2, k))
        return doubled.reshape(blocks, items, k)

    def from_owners(x):
        k = x.shape[-1]
        return x.reshape(half, 2, k)[:, 0, :]

    def mine(x, axis):
        return lax.dynamic_slice_in_dim(x, r * half, half, axis)

    params = mine(norm_params, 2)
    column = (b * items + jnp.arange(items, dtype=jnp.int32)) // 2
    column_hot = (
        jnp.arange(half, dtype=jnp.int32)[:, None] == column[None, :]
    ).astype(F32)
    owned = dot(params.reshape(6, half), column_hot, ((1,), (0,))).reshape(2, 3, items)

    near = [
        lax.ppermute(node_feat, AXES, side_routes(blocks, d, False)) for d in range(1, BAND + 1)
    ]
    near = jnp.concatenate(near, axis=0)
    extended = jnp.concatenate([node_feat, near, other_core(near)], axis=0)
    agg_in = tile_products(extended, tile_values, tile_rows, places, valid, row_tiles).astype(BF16)
    z_first = jnp.dot(agg_in, mine(weight_in, 1), preferred_element_type=F32)

    sums = run_sums(z_first)
    run_means = sums / n_safe
    offset = z_first - at_nodes(run_means)
    squares = run_sums(offset * offset)
    agg_wide = agg_in.astype(F32)
    run_info = jnp.concatenate([n_run, comp_run])
    message = jnp.concatenate(
        [sums.T, squares.T, jnp.broadcast_to(run_info[None, :], (half, 2 * RUNS))], axis=1
    )
    got = exchange(to_owners(message))

    def per_run(x):
        return jnp.transpose(x, (0, 2, 1)).reshape(blocks * RUNS, items)

    def per_block(x):
        return jnp.transpose(x.reshape(blocks, RUNS, items), (0, 2, 1))

    all_n = per_run(got[:, :, 2 * RUNS : 3 * RUNS])
    all_comp = got[:, 0, 3 * RUNS :].reshape(1, blocks * RUNS)
    comp_hot = (jnp.arange(blocks, dtype=jnp.int32)[:, None].astype(F32) == all_comp).astype(F32)

    def by_comp(x):
        return dot(comp_hot, x, ((1,), (0,)))

    def at_runs(x):
        return dot(comp_hot, x, ((0,), (0,)))

    def owner_norm(all_sums, all_squares, alpha, extra=None):
        first = by_comp(jnp.concatenate([all_sums, all_n] + (extra or []), axis=1))
        count = first[:, items : 2 * items]
        mean = first[:, :items] / count
        wide = at_runs(jnp.concatenate([mean, count], axis=1))
        mean_r, count_r = wide[:, :items], wide[:, items:]
        run_mean = all_sums / jnp.maximum(all_n, 1.0)
        apart = run_mean - mean_r
        return count, mean, mean_r, count_r, apart, first[:, 2 * items :]

    all_sums, all_squares = per_run(got[:, :, :RUNS]), per_run(got[:, :, RUNS : 2 * RUNS])
    alpha0, gamma0 = owned[0, 2], owned[0, 0]
    count, mean0, mean0_r, count_r, apart, _ = owner_norm(all_sums, all_squares, alpha0)
    kept = (1.0 - alpha0) * mean0
    spread0 = jnp.sqrt(
        by_comp(all_squares + all_n * apart * apart) / count + kept * kept + EPSILON
    )
    spread0_r = at_runs(spread0)
    back = exchange(
        jnp.concatenate([per_block(mean0_r), per_block(spread0_r), per_block(count_r)], axis=2)
    )
    back = from_owners(back).T
    mean_first, spread_first = back[:RUNS], back[RUNS : 2 * RUNS]
    n_comp = jnp.maximum(back[2 * RUNS :, :1], 1.0)
    spread_first = jnp.where(n_run[:, None] > 0, spread_first, 1.0)
    looked = at_nodes(
        jnp.concatenate([params[0, 2] * mean_first, 1.0 / spread_first], axis=1)
    )
    normed_first = (z_first - looked[:, :half]) * looked[:, half:]
    slope_first = params[0, 0] * looked[:, half:]
    y_first = params[0, 0] * normed_first + params[0, 1]
    hidden_mine = jax.nn.silu(y_first).astype(BF16)
    hidden_other = other_core(hidden_mine)

    def in_order(own, other, axis):
        return jnp.where(
            r == 0,
            jnp.concatenate([own, other], axis=axis),
            jnp.concatenate([other, own], axis=axis),
        )

    hidden = in_order(hidden_mine, hidden_other, 1)
    projected = jnp.dot(hidden, weight_hidden, preferred_element_type=F32).astype(BF16)

    near = [
        lax.ppermute(projected, AXES, side_routes(blocks, d, False)) for d in range(1, BAND + 1)
    ]
    part = tile_products(
        jnp.concatenate([projected] + near, axis=0),
        tile_values,
        tile_rows,
        side_places,
        side_valid,
        row_tiles,
    )
    theirs = lax.dynamic_slice_in_dim(part, (1 - r) * half, half, 1)
    z_second = mine(part, 1) + other_core(theirs)

    d_out = mine(cotangent, 1).astype(F32) / jnp.sqrt(F32(nodes_here * blocks))
    sums = run_sums(jnp.concatenate([z_second, d_out], axis=1))
    run_means = sums[:, :half] / n_safe
    offset = z_second - at_nodes(run_means)
    more = run_sums(jnp.concatenate([offset * offset, offset * d_out], axis=1))
    message = jnp.concatenate(
        [sums[:, :half].T, more[:, :half].T, sums[:, half:].T, more[:, half:].T], axis=1
    )
    by_run = (sel[:, :, None] * agg_wide[:, None, :]).reshape(nodes_here, RUNS * features)
    cross = dot(normed_first, by_run, ((0,), (0,)))
    cross = jnp.transpose(cross.reshape(half, RUNS, 2, f_half), (0, 2, 1, 3))
    run_feat = jnp.transpose(run_sums(agg_wide).reshape(RUNS, 2, f_half), (1, 0, 2))
    run_feat = jnp.broadcast_to(run_feat[None], (half, 2, RUNS, f_half))
    got = exchange(
        jnp.concatenate(
            [
                cross.reshape(blocks, items, RUNS * f_half),
                run_feat.reshape(blocks, items, RUNS * f_half),
                to_owners(message),
            ],
            axis=2,
        )
    )
    all_cross = got[:, :, : RUNS * f_half].reshape(blocks, items, RUNS, f_half)
    all_feat = got[:, :, RUNS * f_half : 2 * RUNS * f_half].reshape(blocks, items, RUNS, f_half)
    stats = [
        per_run(got[:, :, 2 * RUNS * f_half + i * RUNS : 2 * RUNS * f_half + (i + 1) * RUNS])
        for i in range(4)
    ]
    alpha1, gamma1 = owned[1, 2], owned[1, 0]
    count, mean1, mean1_r, count_r, apart, rows1 = owner_norm(
        stats[0], stats[1], alpha1, [stats[2]]
    )
    second = by_comp(
        jnp.concatenate([stats[1] + all_n * apart * apart, stats[3] + apart * stats[2]], axis=1)
    )
    kept = (1.0 - alpha1) * mean1
    spread1 = jnp.sqrt(second[:, :items] / count + kept * kept + EPSILON)
    proj1 = (second[:, items:] + kept * rows1) / spread1
    total1 = gamma1 / spread1 * (rows1 - kept * proj1 / spread1)
    grads1 = jnp.stack(
        [jnp.sum(proj1, axis=0), jnp.sum(rows1, axis=0), -jnp.sum(mean1 * total1, axis=0)], axis=1
    )
    wide = at_runs(jnp.concatenate([spread1, proj1 / count, total1 / count], axis=1))
    back = exchange(
        jnp.concatenate(
            [per_block(mean1_r)]
            + [per_block(wide[:, i * items : (i + 1) * items]) for i in range(3)],
            axis=2,
        )
    )
    back = from_owners(back).T
    mean_second = back[:RUNS]
    spread_second = jnp.where(n_run[:, None] > 0, back[RUNS : 2 * RUNS], 1.0)
    gamma, beta, alpha = params[1, 0], params[1, 1], params[1, 2]
    looked = at_nodes(
        jnp.concatenate(
            [
                alpha * mean_second,
                1.0 / spread_second,
                back[2 * RUNS : 3 * RUNS],
                alpha * back[3 * RUNS :],
            ],
            axis=1,
        )
    )
    inverse = looked[:, half : 2 * half]
    normed = (z_second - looked[:, :half]) * inverse
    out_mine = (gamma * normed + beta).astype(BF16)
    d_second = gamma * inverse * (d_out - normed * looked[:, 2 * half : 3 * half])
    d_second = (d_second - looked[:, 3 * half :]).astype(BF16)
    swapped = other_core(jnp.concatenate([out_mine, d_second], axis=1))
    node_out = in_order(out_mine, swapped[:, :half], 1)
    d_second = in_order(d_second, swapped[:, half:], 1)

    pieces = tile_transposed(
        d_second,
        tile_values,
        tile_rows,
        side_places,
        side_valid,
        row_tiles,
        (BAND + 1) * row_tiles,
    )
    gathered = pieces[0]
    for d in range(1, BAND + 1):
        gathered = gathered + lax.ppermute(
            pieces[d].astype(BF16), AXES, side_routes(blocks, d, True)
        ).astype(F32)
    d_projected = (gathered + other_core(gathered)).astype(BF16)

    d_hidden = lax.dot_general(
        d_projected,
        mine(weight_hidden, 0),
        (((1,), (1,)), ((), ())),
        preferred_element_type=F32,
    )
    d_first_y = d_hidden * silu_grad(y_first)
    sums = run_sums(jnp.concatenate([d_first_y, d_first_y * normed_first], axis=1))
    direct = dot(slope_first * d_first_y, agg_wide, ((0,), (0,)))
    w2_part = lax.dot_general(
        mine(d_projected, 1), hidden, (((0,), (0,)), ((), ())), preferred_element_type=F32
    )
    message = jnp.concatenate([sums[:, :half].T, sums[:, half:].T], axis=1)
    got = exchange(
        jnp.concatenate(
            [
                w2_part.reshape(blocks, items, h_half),
                direct.reshape(blocks, items, f_half),
                to_owners(message),
            ],
            axis=2,
        )
    )
    w2_owned = jnp.sum(got[:, :, :h_half], axis=0)
    w1_owned = jnp.sum(got[:, :, h_half : h_half + f_half], axis=0)
    base = h_half + f_half
    run_rows, run_proj = per_run(got[:, :, base : base + RUNS]), per_run(got[:, :, base + RUNS :])
    both = by_comp(jnp.concatenate([run_rows, run_proj], axis=1))
    rows0, proj0 = both[:, :items], both[:, items:]
    total0 = gamma0 / spread0 * (rows0 - (1.0 - alpha0) * mean0 * proj0 / spread0)
    grads0 = jnp.stack(
        [jnp.sum(proj0, axis=0), jnp.sum(rows0, axis=0), -jnp.sum(mean0 * total0, axis=0)], axis=1
    )
    wide = at_runs(
        jnp.concatenate([gamma0 / spread0 * proj0 / count, alpha0 * total0 / count], axis=1)
    )
    coef_cross, coef_feat = per_block(wide[:, :items]), per_block(wide[:, items:])
    w1_owned = w1_owned - jnp.sum(
        coef_cross[..., None] * all_cross + coef_feat[..., None] * all_feat, axis=(0, 2)
    )
    final = jnp.concatenate([w2_owned, w1_owned, grads0, grads1], axis=1)
    width = final.shape[1]
    final = exchange(jnp.broadcast_to(final[None], (blocks, items, width)))
    final = final.reshape(half, 2, width)
    final = in_order(final, other_core(final), 0)
    grad_w2 = final[:, :, :h_half].reshape(hidden_units, hidden_units).T
    grad_w1 = final[:, :, h_half:base].reshape(hidden_units, features).T
    grad_norm = final[:, 0, base:].T.reshape(2, 3, hidden_units)
    return (node_out, grad_w1, grad_w2, grad_norm)


def solution(mesh):
    in_specs = (
        P("blk", None),
        P("blk", None, None),
        P("blk"),
        P("blk"),
        P("blk"),
        P("blk"),
        P(),
        P(),
        P(),
        P("blk", None),
    )
    out_specs = (P("blk", None), P(), P(), P())
    return jax.shard_map(shards, mesh=mesh, in_specs=in_specs, out_specs=out_specs, check_vma=False)
```

```python
import jax
import jax.numpy as jnp
from jax import lax
from jax.experimental import pallas as pl
from jax.experimental.pallas import tpu as pltpu
from jax.sharding import PartitionSpec as P

BAND = 3
RUNS = 4
EPSILON = 1e-05
F32 = jnp.float32
BF16 = jnp.bfloat16
HIGH = lax.Precision.HIGHEST
AXES = ("blk", "rep")


def dot(a, b, contract):
    return lax.dot_general(a, b, (contract, ((), ())), precision=HIGH)


def other_core(x):
    return lax.ppermute(x, "rep", [(0, 1), (1, 0)])


def side_routes(blocks, distance, outward):
    routes = []
    for i in range(blocks):
        low, high = (i - distance) % blocks, (i + distance) % blocks
        if outward:
            routes += [(i * 2, low * 2), (i * 2 + 1, high * 2 + 1)]
        else:
            routes += [(low * 2, i * 2), (high * 2 + 1, i * 2 + 1)]
    return routes


def exchange(x):
    return lax.all_to_all(x, "blk", 0, 0, tiled=True)


def tile_products(pieces, values, rows, places, valid, row_tiles):
    tile = values.shape[1]
    width = pieces.shape[1]
    picked = pieces.reshape(-1, tile, width)[places]
    zero = jnp.zeros((), picked.dtype)
    masked = [
        jnp.where((valid & (rows == r))[:, None, None], picked, zero) for r in range(row_tiles)
    ]
    product = lax.dot_general(
        values,
        jnp.concatenate(masked, axis=2),
        (((0, 2), (0, 1)), ((), ())),
        preferred_element_type=F32,
    )
    return jnp.concatenate(
        [product[:, r * width : (r + 1) * width] for r in range(row_tiles)], axis=0
    )


def parts_of(x):
    high = x.astype(BF16)
    rest = x - high.astype(F32)
    middle = rest.astype(BF16)
    return high, middle, (rest - middle.astype(F32)).astype(BF16)


def hot_dot(hot, x):
    return sum(jnp.dot(hot, part, preferred_element_type=F32) for part in parts_of(x))


def combine_kernel(sums, squares, info, info_t, near_comp, alpha, table):
    blocks = info.shape[0]
    half = alpha.shape[1]
    across = lax.broadcasted_iota(jnp.int32, (blocks, blocks), 1).astype(F32)
    down = lax.broadcasted_iota(jnp.int32, (blocks, blocks), 0).astype(F32)
    to_comp, to_run = [], []
    total = jnp.zeros((blocks, half), F32)
    count = jnp.zeros((blocks, 1), F32)
    for j in range(RUNS):
        to_comp.append((down == info_t[RUNS + j : RUNS + j + 1, :]).astype(F32).astype(BF16))
        to_run.append((across == info[:, RUNS + j : RUNS + j + 1]).astype(F32).astype(BF16))
        total += hot_dot(to_comp[j], sums[:, j * half : (j + 1) * half])
        counted = jnp.dot(to_comp[j], info[...].astype(BF16), preferred_element_type=F32)
        count += counted[:, j : j + 1]
    count = jnp.maximum(count, 1.0)
    mean = total / count
    total = jnp.zeros((blocks, half), F32)
    for j in range(RUNS):
        n = info[:, j : j + 1]
        apart = sums[:, j * half : (j + 1) * half] / jnp.maximum(n, 1.0) - hot_dot(to_run[j], mean)
        total += hot_dot(to_comp[j], squares[:, j * half : (j + 1) * half] + n * apart * apart)
    kept = (1.0 - alpha[...]) * mean
    inverse = 1.0 / jnp.sqrt(total / count + kept * kept + EPSILON)
    rows = near_comp.shape[0]
    ids = lax.broadcasted_iota(jnp.int32, (rows, blocks), 1).astype(F32)
    hot = (ids == near_comp[...]).astype(F32).astype(BF16)
    table[:rows, :] = hot_dot(hot, mean)
    table[rows:, :] = hot_dot(hot, inverse)


def forward_kernel(
    places, rows, count, starts, agg, weight_in, weight_out, table, params, values, z, hidden, proj
):
    nodes = hidden.shape[0]
    width = hidden.shape[1]
    tile = values.shape[1]
    near = table.shape[0] // 2
    node = lax.broadcasted_iota(jnp.int32, (nodes, width), 0)

    def block(k, unused):
        at = pl.ds(pl.multiple_of(k * nodes, nodes), nodes)
        first = jnp.dot(agg[at, :], weight_in[...], preferred_element_type=F32)
        mean = jnp.broadcast_to(table[pl.ds(k * RUNS, 1), :], (nodes, width))
        inverse = jnp.broadcast_to(table[pl.ds(near + k * RUNS, 1), :], (nodes, width))
        for j in range(1, RUNS):
            later = node >= starts[k * RUNS + j]
            mean = jnp.where(later, table[pl.ds(k * RUNS + j, 1), :], mean)
            inverse = jnp.where(later, table[pl.ds(near + k * RUNS + j, 1), :], inverse)
        normed = (first - params[2:3, :] * mean) * inverse
        y = params[0:1, :] * normed + params[1:2, :]
        low = (y / (1.0 + jnp.exp(-y))).astype(BF16)

        @pl.when(k == 0)
        def _():
            hidden[...] = low

        proj[at, :] = jnp.dot(low, weight_out[...], preferred_element_type=F32).astype(BF16)
        return unused

    lax.fori_loop(0, 2 * BAND + 1, block, 0)
    z[...] = jnp.zeros_like(z)

    def slot(s, unused):
        source = pl.ds(pl.multiple_of(places[s] * tile, tile), tile)
        target = pl.ds(pl.multiple_of(rows[s] * tile, tile), tile)
        z[target, :] += jnp.dot(values[s], proj[source, :], preferred_element_type=F32)
        return unused

    lax.fori_loop(0, count[0], slot, 0)


def transposed_kernel(places, rows, live, values, grads, own, near, total):
    tile = values.shape[1]
    nodes = grads.shape[0]
    total[...] = jnp.zeros_like(total)
    for s in range(values.shape[0]):

        @pl.when(live[s] > 0)
        def _():
            source = pl.ds(pl.multiple_of(rows[s] * tile, tile), tile)
            target = pl.ds(pl.multiple_of(places[s] * tile, tile), tile)
            total[target, :] += lax.dot_general(
                values[s], grads[source, :], (((0,), (0,)), ((), ())), preferred_element_type=F32
            )

    own[...] = total[:nodes, :]
    near[...] = total[nodes:, :].astype(BF16)


def call(kernel, outs, scratch, scalars, arrays, cost):
    return pl.pallas_call(
        kernel,
        out_shape=outs,
        in_specs=[pl.BlockSpec(memory_space=pltpu.SMEM)] * len(scalars)
        + [pl.BlockSpec(memory_space=pltpu.VMEM)] * len(arrays),
        out_specs=jax.tree.map(lambda _: pl.BlockSpec(memory_space=pltpu.VMEM), outs),
        scratch_shapes=scratch,
        cost_estimate=pl.CostEstimate(flops=cost, bytes_accessed=1 << 20, transcendentals=0),
        compiler_params=pltpu.CompilerParams(vmem_limit_bytes=40 << 20),
    )(*scalars, *arrays)


def silu_grad(values):
    logistic = jax.nn.sigmoid(values)
    return logistic * (1.0 + values * (1.0 - logistic))


def shards(
    node_feat,
    tile_values,
    tile_rows,
    tile_cols,
    tile_count,
    comp_ids,
    weight_in,
    weight_hidden,
    norm_params,
    cotangent,
):
    nodes_here, features = node_feat.shape
    hidden_units = weight_hidden.shape[0]
    tile = tile_values.shape[1]
    row_tiles = nodes_here // tile
    blocks = lax.axis_size("blk")
    b = lax.axis_index("blk")
    r = lax.axis_index("rep")
    half = hidden_units // 2
    items = 2 * half // blocks
    f_half = features // 2
    h_half = hidden_units // 2

    slots = jnp.arange(tile_values.shape[0], dtype=jnp.int32)
    valid = slots < tile_count[0]
    distance = (tile_cols // row_tiles - b) % blocks
    signed = jnp.where(distance > blocks // 2, distance - blocks, distance)
    signed = jnp.where(valid, signed, 0)
    within = tile_cols % row_tiles
    places = jnp.where(signed > 0, BAND + signed, -signed) * row_tiles + within
    own_side = jnp.where(signed == 0, r == 0, (signed < 0) == (r == 0))
    side_valid = valid & own_side
    side_places = jnp.where(side_valid, jnp.abs(signed) * row_tiles + within, 0)

    node = jnp.arange(nodes_here, dtype=jnp.int32)
    changed = jnp.concatenate(
        [jnp.zeros((1,), jnp.int32), (comp_ids[1:] != comp_ids[:-1]).astype(jnp.int32)]
    )
    run_of = jnp.sum(
        jnp.where(node[None, :] <= node[:, None], changed[None, :], 0), axis=1
    )
    run_ids = jnp.arange(RUNS, dtype=jnp.int32)
    run_hot = run_of[:, None] == run_ids[None, :]
    sel = run_hot.astype(F32)
    n_run = jnp.sum(sel, axis=0)
    comp_run = jnp.max(jnp.where(run_hot, comp_ids[:, None], -1), axis=0).astype(F32)
    n_safe = jnp.maximum(n_run, 1.0)[:, None]

    def run_sums(x):
        return dot(sel, x, ((0,), (0,)))

    def at_nodes(table):
        return dot(sel, table, ((1,), (0,)))

    def to_owners(columns):
        k = columns.shape[1]
        doubled = jnp.broadcast_to(columns[:, None, :], (half, 2, k))
        return doubled.reshape(blocks, items, k)

    def from_owners(x):
        k = x.shape[-1]
        return x.reshape(half, 2, k)[:, 0, :]

    def mine(x, axis):
        return lax.dynamic_slice_in_dim(x, r * half, half, axis)

    params = mine(norm_params, 2)
    column = (b * items + jnp.arange(items, dtype=jnp.int32)) // 2
    column_hot = (
        jnp.arange(half, dtype=jnp.int32)[:, None] == column[None, :]
    ).astype(F32)
    owned = dot(params.reshape(6, half), column_hot, ((1,), (0,))).reshape(2, 3, items)

    def in_order(own, other, axis):
        return jnp.where(
            r == 0,
            jnp.concatenate([own, other], axis=axis),
            jnp.concatenate([other, own], axis=axis),
        )

    def with_sides(own, near):
        near = jnp.concatenate(near, axis=0)
        return jnp.concatenate([own, in_order(near, other_core(near), 0)], axis=0)

    def fetch(x):
        return [lax.ppermute(x, AXES, side_routes(blocks, d, False)) for d in range(1, BAND + 1)]

    extended = with_sides(node_feat, fetch(node_feat))
    agg_in = tile_products(extended, tile_values, tile_rows, places, valid, row_tiles).astype(BF16)
    z_first = jnp.dot(agg_in, mine(weight_in, 1), preferred_element_type=F32)

    sums_first = run_sums(z_first)
    run_means = sums_first / n_safe
    offset = z_first - at_nodes(run_means)
    squares_first = run_sums(offset * offset)
    run_info = jnp.concatenate([n_run, comp_run])
    message = jnp.concatenate(
        [
            sums_first.reshape(-1),
            squares_first.reshape(-1),
            run_info,
            jnp.zeros((128 - 2 * RUNS,), F32),
        ]
    )
    got = exchange(jnp.broadcast_to(message[None, None, :], (blocks, 1, message.shape[0])))
    agg_near = with_sides(agg_in, fetch(agg_in))
    got = got.reshape(blocks, message.shape[0])
    info = got[:, 2 * RUNS * half : 2 * RUNS * half + 2 * RUNS]
    offsets = jnp.array([0, -1, -2, -3, 1, 2, 3], jnp.int32)
    near_info = info[(b + offsets) % blocks]
    near_n = near_info[:, :RUNS].astype(jnp.int32)
    starts = jnp.concatenate(
        [jnp.zeros((2 * BAND + 1, 1), jnp.int32), jnp.cumsum(near_n, axis=1)[:, : RUNS - 1]], axis=1
    ).reshape(-1)
    near_comp = jnp.concatenate(
        [near_info[:, RUNS:].reshape(-1), jnp.full((RUNS,), -1.0, F32)]
    ).reshape(-1, 1)
    near_rows = near_comp.shape[0]
    table = call(
        combine_kernel,
        jax.ShapeDtypeStruct((2 * near_rows, half), F32),
        [],
        [],
        [
            got[:, : RUNS * half],
            got[:, RUNS * half : 2 * RUNS * half],
            info,
            info.T,
            near_comp,
            params[0, 2:3],
        ],
        1 << 30,
    )
    both_tables = in_order(table, other_core(table), 1)
    z_second, hidden = call(
        forward_kernel,
        (
            jax.ShapeDtypeStruct((nodes_here, half), F32),
            jax.ShapeDtypeStruct((nodes_here, hidden_units), BF16),
        ),
        [pltpu.VMEM(((2 * BAND + 1) * nodes_here, half), BF16)],
        [places, tile_rows, tile_count, starts],
        [
            agg_near,
            weight_in,
            mine(weight_hidden, 1),
            both_tables,
            norm_params[0],
            tile_values,
        ],
        1 << 30,
    )
    agg_wide = agg_in.astype(F32)
    mean_first = table[:RUNS]
    inverse_first = table[near_rows : near_rows + RUNS]
    looked = at_nodes(jnp.concatenate([params[0, 2] * mean_first, inverse_first], axis=1))
    normed_first = (z_first - looked[:, :half]) * looked[:, half:]
    slope_first = params[0, 0] * looked[:, half:]
    y_first = params[0, 0] * normed_first + params[0, 1]

    def per_run(x):
        return jnp.transpose(x, (0, 2, 1)).reshape(blocks * RUNS, items)

    def per_block(x):
        return jnp.transpose(x.reshape(blocks, RUNS, items), (0, 2, 1))

    d_out = mine(cotangent, 1).astype(F32) / jnp.sqrt(F32(nodes_here * blocks))
    sums = run_sums(jnp.concatenate([z_second, d_out], axis=1))
    run_means = sums[:, :half] / n_safe
    offset = z_second - at_nodes(run_means)
    more = run_sums(jnp.concatenate([offset * offset, offset * d_out], axis=1))
    message = jnp.concatenate(
        [
            sums[:, :half],
            more[:, :half],
            sums[:, half:],
            more[:, half:],
            sums_first,
            squares_first,
            jnp.broadcast_to(run_info[:, None], (2 * RUNS, half)),
        ],
        axis=0,
    ).T
    by_run = (sel[:, :, None] * agg_wide[:, None, :]).reshape(nodes_here, RUNS * features)
    cross = dot(normed_first, by_run, ((0,), (0,)))
    cross = jnp.transpose(cross.reshape(half, RUNS, 2, f_half), (0, 2, 1, 3))
    run_feat = jnp.transpose(run_sums(agg_wide).reshape(RUNS, 2, f_half), (1, 0, 2))
    run_feat = jnp.broadcast_to(run_feat[None], (half, 2, RUNS, f_half))
    got = exchange(
        jnp.concatenate(
            [
                cross.reshape(blocks, items, RUNS * f_half),
                run_feat.reshape(blocks, items, RUNS * f_half),
                to_owners(message),
            ],
            axis=2,
        )
    )
    all_cross = got[:, :, : RUNS * f_half].reshape(blocks, items, RUNS, f_half)
    all_feat = got[:, :, RUNS * f_half : 2 * RUNS * f_half].reshape(blocks, items, RUNS, f_half)
    base = 2 * RUNS * f_half
    stats = [
        per_run(got[:, :, base + i * RUNS : base + (i + 1) * RUNS]) for i in range(7)
    ]
    all_n = stats[6]
    all_comp = got[:, 0, base + 7 * RUNS :].reshape(1, blocks * RUNS)
    comp_hot = (jnp.arange(blocks, dtype=jnp.int32)[:, None].astype(F32) == all_comp).astype(F32)

    def by_comp(x):
        return dot(comp_hot, x, ((1,), (0,)))

    def at_runs(x):
        return dot(comp_hot, x, ((0,), (0,)))

    alpha0, gamma0 = owned[0, 2], owned[0, 0]
    alpha1, gamma1 = owned[1, 2], owned[1, 0]
    firsts = by_comp(jnp.concatenate([all_n, stats[0], stats[4], stats[2]], axis=1))
    count, rows1 = firsts[:, :items], firsts[:, 3 * items :]
    mean1, mean0 = firsts[:, items : 2 * items] / count, firsts[:, 2 * items : 3 * items] / count
    run_wide = at_runs(jnp.concatenate([mean1, mean0], axis=1))
    mean1_r = run_wide[:, :items]
    n_least = jnp.maximum(all_n, 1.0)
    apart = stats[0] / n_least - mean1_r
    apart0 = stats[4] / n_least - run_wide[:, items:]
    second = by_comp(
        jnp.concatenate(
            [
                stats[1] + all_n * apart * apart,
                stats[3] + apart * stats[2],
                stats[5] + all_n * apart0 * apart0,
            ],
            axis=1,
        )
    )
    kept = (1.0 - alpha0) * mean0
    spread0 = jnp.sqrt(second[:, 2 * items :] / count + kept * kept + EPSILON)
    kept = (1.0 - alpha1) * mean1
    spread1 = jnp.sqrt(second[:, :items] / count + kept * kept + EPSILON)
    proj1 = (second[:, items : 2 * items] + kept * rows1) / spread1
    total1 = gamma1 / spread1 * (rows1 - kept * proj1 / spread1)
    grads1 = jnp.stack(
        [jnp.sum(proj1, axis=0), jnp.sum(rows1, axis=0), -jnp.sum(mean1 * total1, axis=0)], axis=1
    )
    wide = at_runs(jnp.concatenate([spread1, proj1 / count, total1 / count], axis=1))
    back = exchange(
        jnp.concatenate(
            [per_block(mean1_r)]
            + [per_block(wide[:, i * items : (i + 1) * items]) for i in range(3)],
            axis=2,
        )
    )
    back = from_owners(back).T
    mean_second = back[:RUNS]
    spread_second = jnp.where(n_run[:, None] > 0, back[RUNS : 2 * RUNS], 1.0)
    gamma, beta, alpha = params[1, 0], params[1, 1], params[1, 2]
    looked = at_nodes(
        jnp.concatenate(
            [
                alpha * mean_second,
                1.0 / spread_second,
                back[2 * RUNS : 3 * RUNS],
                alpha * back[3 * RUNS :],
            ],
            axis=1,
        )
    )
    inverse = looked[:, half : 2 * half]
    normed = (z_second - looked[:, :half]) * inverse
    out_mine = (gamma * normed + beta).astype(BF16)
    d_second = gamma * inverse * (d_out - normed * looked[:, 2 * half : 3 * half])
    d_second = (d_second - looked[:, 3 * half :]).astype(BF16)
    swapped = other_core(jnp.concatenate([out_mine, d_second], axis=1))
    node_out = in_order(out_mine, swapped[:, :half], 1)
    d_second = in_order(d_second, swapped[:, half:], 1)

    gathered, near = call(
        transposed_kernel,
        (
            jax.ShapeDtypeStruct((nodes_here, hidden_units), F32),
            jax.ShapeDtypeStruct((BAND * nodes_here, hidden_units), BF16),
        ),
        [pltpu.VMEM(((BAND + 1) * nodes_here, hidden_units), F32)],
        [side_places, tile_rows, side_valid.astype(jnp.int32)],
        [tile_values, d_second],
        1 << 28,
    )
    for d in range(1, BAND + 1):
        gathered = gathered + lax.ppermute(
            near[(d - 1) * nodes_here : d * nodes_here], AXES, side_routes(blocks, d, True)
        ).astype(F32)
    d_projected = (gathered + other_core(gathered)).astype(BF16)

    d_hidden = lax.dot_general(
        d_projected,
        mine(weight_hidden, 0),
        (((1,), (1,)), ((), ())),
        preferred_element_type=F32,
    )
    d_first_y = d_hidden * silu_grad(y_first)
    sums = run_sums(jnp.concatenate([d_first_y, d_first_y * normed_first], axis=1))
    direct = dot(slope_first * d_first_y, agg_wide, ((0,), (0,)))
    w2_part = lax.dot_general(
        mine(d_projected, 1), hidden, (((0,), (0,)), ((), ())), preferred_element_type=F32
    )
    message = jnp.concatenate([sums[:, :half].T, sums[:, half:].T], axis=1)
    got = exchange(
        jnp.concatenate(
            [
                w2_part.reshape(blocks, items, h_half),
                direct.reshape(blocks, items, f_half),
                to_owners(message),
            ],
            axis=2,
        )
    )
    w2_owned = jnp.sum(got[:, :, :h_half], axis=0)
    w1_owned = jnp.sum(got[:, :, h_half : h_half + f_half], axis=0)
    base = h_half + f_half
    run_rows, run_proj = per_run(got[:, :, base : base + RUNS]), per_run(got[:, :, base + RUNS :])
    both = by_comp(jnp.concatenate([run_rows, run_proj], axis=1))
    rows0, proj0 = both[:, :items], both[:, items:]
    total0 = gamma0 / spread0 * (rows0 - (1.0 - alpha0) * mean0 * proj0 / spread0)
    grads0 = jnp.stack(
        [jnp.sum(proj0, axis=0), jnp.sum(rows0, axis=0), -jnp.sum(mean0 * total0, axis=0)], axis=1
    )
    wide = at_runs(
        jnp.concatenate([gamma0 / spread0 * proj0 / count, alpha0 * total0 / count], axis=1)
    )
    coef_cross, coef_feat = per_block(wide[:, :items]), per_block(wide[:, items:])
    w1_owned = w1_owned - jnp.sum(
        coef_cross[..., None] * all_cross + coef_feat[..., None] * all_feat, axis=(0, 2)
    )
    final = jnp.concatenate([w2_owned, w1_owned, grads0, grads1], axis=1)
    width = final.shape[1]
    final = exchange(jnp.broadcast_to(final[None], (blocks, items, width)))
    final = final.reshape(half, 2, width)
    final = in_order(final, other_core(final), 0)
    grad_w2 = final[:, :, :h_half].reshape(hidden_units, hidden_units).T
    grad_w1 = final[:, :, h_half:base].reshape(hidden_units, features).T
    grad_norm = final[:, 0, base:].T.reshape(2, 3, hidden_units)
    return (node_out, grad_w1, grad_w2, grad_norm)


def solution(mesh):
    in_specs = (
        P("blk", None),
        P("blk", None, None),
        P("blk"),
        P("blk"),
        P("blk"),
        P("blk"),
        P(),
        P(),
        P(),
        P("blk", None),
    )
    out_specs = (P("blk", None), P(), P(), P())
    return jax.shard_map(shards, mesh=mesh, in_specs=in_specs, out_specs=out_specs, check_vma=False)
```

```python
import jax
import jax.numpy as jnp
from jax import lax
from jax.experimental import pallas as pl
from jax.experimental.pallas import tpu as pltpu
from jax.sharding import PartitionSpec as P

BAND = 3
RUNS = 4
EPSILON = 1e-05
F32 = jnp.float32
BF16 = jnp.bfloat16
HIGH = lax.Precision.HIGHEST
AXES = ("blk", "rep")


def dot(a, b, contract):
    return lax.dot_general(a, b, (contract, ((), ())), precision=HIGH)


def other_core(x):
    return lax.ppermute(x, "rep", [(0, 1), (1, 0)])


def side_routes(blocks, distance, outward):
    routes = []
    for i in range(blocks):
        low, high = (i - distance) % blocks, (i + distance) % blocks
        if outward:
            routes += [(i * 2, low * 2), (i * 2 + 1, high * 2 + 1)]
        else:
            routes += [(low * 2, i * 2), (high * 2 + 1, i * 2 + 1)]
    return routes


def exchange(x):
    return lax.all_to_all(x, "blk", 0, 0, tiled=True)


def tile_products(pieces, values, rows, places, valid, row_tiles):
    tile = values.shape[1]
    width = pieces.shape[1]
    picked = pieces.reshape(-1, tile, width)[places]
    zero = jnp.zeros((), picked.dtype)
    masked = [
        jnp.where((valid & (rows == r))[:, None, None], picked, zero) for r in range(row_tiles)
    ]
    product = lax.dot_general(
        values,
        jnp.concatenate(masked, axis=2),
        (((0, 2), (0, 1)), ((), ())),
        preferred_element_type=F32,
    )
    return jnp.concatenate(
        [product[:, r * width : (r + 1) * width] for r in range(row_tiles)], axis=0
    )


def parts_of(x):
    high = x.astype(BF16)
    rest = x - high.astype(F32)
    middle = rest.astype(BF16)
    return high, middle, (rest - middle.astype(F32)).astype(BF16)


def hot_dot(hot, x):
    return sum(jnp.dot(hot, part, preferred_element_type=F32) for part in parts_of(x))


def spread_of(total, count, mean, alpha):
    kept = (1.0 - alpha) * mean
    return jnp.sqrt(total / count + kept * kept + EPSILON)


def combine_kernel(near_block, got, alpha, table):
    each = 2 * RUNS + 1
    blocks = got.shape[0] // each
    half = got.shape[1]

    def row_of(k):
        return got[pl.ds(k, blocks, stride=each), :]

    info = row_of(2 * RUNS)
    flipped = info.T
    across = lax.broadcasted_iota(jnp.int32, (blocks, blocks), 1).astype(F32)
    down = lax.broadcasted_iota(jnp.int32, (blocks, blocks), 0).astype(F32)
    counts = info.astype(BF16)
    to_comp, to_run = [], []
    total = jnp.zeros((blocks, half), F32)
    count = jnp.zeros((blocks, 1), F32)
    for j in range(RUNS):
        to_comp.append((down == flipped[RUNS + j : RUNS + j + 1, :]).astype(F32).astype(BF16))
        to_run.append((across == info[:, RUNS + j : RUNS + j + 1]).astype(F32).astype(BF16))
        total += hot_dot(to_comp[j], row_of(j))
        counted = jnp.dot(to_comp[j], counts, preferred_element_type=F32)
        count += counted[:, j : j + 1]
    count = jnp.maximum(count, 1.0)
    mean = total / count
    total = jnp.zeros((blocks, half), F32)
    for j in range(RUNS):
        n = info[:, j : j + 1]
        apart = row_of(j) / jnp.maximum(n, 1.0) - hot_dot(to_run[j], mean)
        total += hot_dot(to_comp[j], row_of(RUNS + j) + n * apart * apart)
    inverse = 1.0 / spread_of(total, count, mean, alpha[...])
    near = near_block.shape[0]
    rows = [got[pl.ds(near_block[i] * each + 2 * RUNS, 1), :] for i in range(near)]
    info = jnp.concatenate(rows + rows[:1], axis=0)
    across = lax.broadcasted_iota(jnp.int32, (8, blocks), 1).astype(F32)
    start = jnp.zeros((8, 1), F32)
    for j in range(RUNS):
        hot = (across == info[:, RUNS + j : RUNS + j + 1]).astype(F32).astype(BF16)
        table[j * 8 : j * 8 + 8, :] = hot_dot(hot, mean)
        table[(RUNS + j) * 8 : (RUNS + j) * 8 + 8, :] = hot_dot(hot, inverse)
        table[(2 * RUNS + j) * 8 : (2 * RUNS + j) * 8 + 8, :] = jnp.broadcast_to(start, (8, half))
        start = start + info[:, j : j + 1]


def owner_hots(stats):
    blocks = stats.shape[0]
    flipped = stats[...].T
    across = lax.broadcasted_iota(jnp.int32, (blocks, blocks), 1).astype(F32)
    down = lax.broadcasted_iota(jnp.int32, (blocks, blocks), 0).astype(F32)
    to_comp = [
        (down == flipped[28 + j : 29 + j, :]).astype(F32).astype(BF16) for j in range(RUNS)
    ]
    to_run = [(across == stats[:, 28 + j : 29 + j]).astype(F32).astype(BF16) for j in range(RUNS)]
    return to_comp, to_run


def comp_sums(to_comp, x, firsts):
    lane = lax.broadcasted_iota(jnp.int32, x.shape, 1) % RUNS
    total = jnp.zeros(x.shape, F32)
    for j in range(RUNS):
        total += jnp.where(lane == j, hot_dot(to_comp[j], x), 0.0)
    return [sum(total[:, f + j : f + j + 1] for j in range(RUNS)) for f in firsts]


def in_lanes(columns, shape):
    lane = lax.broadcasted_iota(jnp.int32, shape, 1) % len(columns)
    out = jnp.broadcast_to(columns[0], shape)
    for q in range(1, len(columns)):
        out = jnp.where(lane == q, columns[q], out)
    return out


def second_owner_kernel(stats, owned, back, state):
    blocks = stats.shape[0]
    shape = (blocks, 128)
    to_comp, to_run = owner_hots(stats)
    sum1, rows1, sum0, count = comp_sums(to_comp, stats[...], (0, 8, 16, 24))
    mean1, mean0 = sum1 / count, sum0 / count
    means = in_lanes([mean1, mean0], shape)
    total = jnp.zeros(shape, F32)
    for j in range(RUNS):
        value = [stats[:, 4 * i + j : 4 * i + j + 1] for i in range(7)]
        n = value[6]
        here = hot_dot(to_run[j], means)
        apart1 = value[0] / jnp.maximum(n, 1.0) - here[:, :1]
        apart0 = value[4] / jnp.maximum(n, 1.0) - here[:, 1:2]
        x = in_lanes(
            [
                value[1] + n * apart1 * apart1,
                value[3] + apart1 * value[2],
                value[5] + n * apart0 * apart0,
            ],
            shape,
        )
        total += hot_dot(to_comp[j], x)
    gamma, alpha = owned[:, 3:4], owned[:, 5:6]
    spread0 = spread_of(total[:, 2:3], count, mean0, owned[:, 2:3])
    spread = spread_of(total[:, :1], count, mean1, alpha)
    kept = (1.0 - alpha) * mean1
    proj = (total[:, 1:2] + kept * rows1) / spread
    whole = gamma / spread * (rows1 - kept * proj / spread)
    give = in_lanes([alpha * mean1, 1.0 / spread, proj / count, alpha * whole / count], shape)
    lane = lax.broadcasted_iota(jnp.int32, shape, 1)
    out = jnp.zeros(shape, F32)
    for j in range(RUNS):
        out = jnp.where(lane // 4 == j, hot_dot(to_run[j], give), out)
    back[...] = out
    grads = [
        jnp.sum(c, axis=0, keepdims=True) for c in (proj, rows1, mean1 * whole, jnp.zeros_like(proj))
    ]
    state[...] = jnp.where(
        lane < 4,
        in_lanes([mean0, spread0, count, count], shape),
        in_lanes([grads[0], grads[1], -grads[2], grads[3]], shape),
    )


def first_owner_kernel(stats, state, owned, sums, cross, feat, final):
    blocks = stats.shape[0]
    shape = (blocks, 128)
    wide = cross.shape[1]
    f_half = wide // RUNS
    to_comp, to_run = owner_hots(stats)
    h_half = sums.shape[1] - 128
    rows, proj = comp_sums(to_comp, sums[:, h_half:], (f_half, f_half + RUNS))
    mean, spread, count = state[:, :1], state[:, 1:2], state[:, 2:3]
    gamma, alpha = owned[:, :1], owned[:, 2:3]
    whole = gamma / spread * (rows - (1.0 - alpha) * mean * proj / spread)
    give = in_lanes([gamma / spread * proj / count, alpha * whole / count], shape)
    lane = lax.broadcasted_iota(jnp.int32, (blocks, wide), 1)
    on_cross = jnp.zeros((blocks, wide), F32)
    on_feat = jnp.zeros((blocks, wide), F32)
    for j in range(RUNS):
        here = hot_dot(to_run[j], give)
        on_cross = jnp.where(lane // f_half == j, here[:, :1], on_cross)
        on_feat = jnp.where(lane // f_half == j, here[:, 1:2], on_feat)
    less = jnp.sum(on_cross * cross[...] + on_feat * feat[...], axis=0, keepdims=True)
    added = jnp.sum(sums[...], axis=0, keepdims=True)
    tail = added[:, h_half : h_half + f_half]
    for j in range(RUNS):
        tail = tail - less[:, j * f_half : (j + 1) * f_half]
    grads = [jnp.sum(c, axis=0, keepdims=True) for c in (proj, rows, mean * whole)]
    lane = lax.broadcasted_iota(jnp.int32, (1, 128 - f_half), 1)
    rest = jnp.zeros((1, 128 - f_half), F32)
    values = [grads[0], grads[1], -grads[2]] + [state[:1, 4 + q : 5 + q] for q in range(3)]
    for q in range(6):
        rest = jnp.where(lane == q, values[q], rest)
    row = jnp.concatenate([added[:, :h_half], tail, rest], axis=1)
    final[...] = jnp.broadcast_to(row, final.shape)


def forward_kernel(
    places, rows, count, agg, weight_in, weight_out, table, params, values, z, hidden, proj
):
    nodes = hidden.shape[0]
    width = hidden.shape[1]
    tile = values.shape[1]
    node = lax.broadcasted_iota(jnp.int32, (nodes, width), 0).astype(F32)

    def block(k, unused):
        at = pl.ds(pl.multiple_of(k * nodes, nodes), nodes)
        first = jnp.dot(agg[at, :], weight_in[...], preferred_element_type=F32)
        mean = jnp.broadcast_to(table[pl.ds(k, 1), :], (nodes, width))
        inverse = jnp.broadcast_to(table[pl.ds(8 * RUNS + k, 1), :], (nodes, width))
        for j in range(1, RUNS):
            later = node >= table[pl.ds(16 * RUNS + 8 * j + k, 1), :]
            mean = jnp.where(later, table[pl.ds(8 * j + k, 1), :], mean)
            inverse = jnp.where(later, table[pl.ds(8 * RUNS + 8 * j + k, 1), :], inverse)
        normed = (first - params[2:3, :] * mean) * inverse
        y = params[0:1, :] * normed + params[1:2, :]
        low = (y / (1.0 + jnp.exp(-y))).astype(BF16)

        @pl.when(k == 0)
        def _():
            hidden[...] = low

        proj[at, :] = jnp.dot(low, weight_out[...], preferred_element_type=F32).astype(BF16)
        return unused

    lax.fori_loop(0, 2 * BAND + 1, block, 0)
    z[...] = jnp.zeros_like(z)

    def slot(s, unused):
        source = pl.ds(pl.multiple_of(places[s] * tile, tile), tile)
        target = pl.ds(pl.multiple_of(rows[s] * tile, tile), tile)
        z[target, :] += jnp.dot(values[s], proj[source, :], preferred_element_type=F32)
        return unused

    lax.fori_loop(0, count[0], slot, 0)


def transposed_kernel(places, rows, live, values, grads, own, near, total):
    tile = values.shape[1]
    nodes = grads.shape[0]
    total[...] = jnp.zeros_like(total)
    for s in range(values.shape[0]):

        @pl.when(live[s] > 0)
        def _():
            source = pl.ds(pl.multiple_of(rows[s] * tile, tile), tile)
            target = pl.ds(pl.multiple_of(places[s] * tile, tile), tile)
            total[target, :] += lax.dot_general(
                values[s], grads[source, :], (((0,), (0,)), ((), ())), preferred_element_type=F32
            )

    own[...] = total[:nodes, :]
    near[...] = total[nodes:, :].astype(BF16)


def call(kernel, outs, scratch, scalars, arrays, cost):
    return pl.pallas_call(
        kernel,
        out_shape=outs,
        in_specs=[pl.BlockSpec(memory_space=pltpu.SMEM)] * len(scalars)
        + [pl.BlockSpec(memory_space=pltpu.VMEM)] * len(arrays),
        out_specs=jax.tree.map(lambda _: pl.BlockSpec(memory_space=pltpu.VMEM), outs),
        scratch_shapes=scratch,
        cost_estimate=pl.CostEstimate(flops=cost, bytes_accessed=1 << 20, transcendentals=0),
        compiler_params=pltpu.CompilerParams(vmem_limit_bytes=40 << 20),
    )(*scalars, *arrays)


def silu_grad(values):
    logistic = jax.nn.sigmoid(values)
    return logistic * (1.0 + values * (1.0 - logistic))


def shards(
    node_feat,
    tile_values,
    tile_rows,
    tile_cols,
    tile_count,
    comp_ids,
    weight_in,
    weight_hidden,
    norm_params,
    cotangent,
):
    nodes_here, features = node_feat.shape
    hidden_units = weight_hidden.shape[0]
    tile = tile_values.shape[1]
    row_tiles = nodes_here // tile
    blocks = lax.axis_size("blk")
    b = lax.axis_index("blk")
    r = lax.axis_index("rep")
    half = hidden_units // 2
    items = 2 * half // blocks
    f_half = features // 2
    h_half = hidden_units // 2

    slots = jnp.arange(tile_values.shape[0], dtype=jnp.int32)
    valid = slots < tile_count[0]
    distance = (tile_cols // row_tiles - b) % blocks
    signed = jnp.where(distance > blocks // 2, distance - blocks, distance)
    signed = jnp.where(valid, signed, 0)
    within = tile_cols % row_tiles
    places = jnp.where(signed > 0, BAND + signed, -signed) * row_tiles + within
    own_side = jnp.where(signed == 0, r == 0, (signed < 0) == (r == 0))
    side_valid = valid & own_side
    side_places = jnp.where(side_valid, jnp.abs(signed) * row_tiles + within, 0)

    node = jnp.arange(nodes_here, dtype=jnp.int32)
    changed = jnp.concatenate(
        [jnp.zeros((1,), jnp.int32), (comp_ids[1:] != comp_ids[:-1]).astype(jnp.int32)]
    )
    run_of = jnp.sum(
        jnp.where(node[None, :] <= node[:, None], changed[None, :], 0), axis=1
    )
    run_ids = jnp.arange(RUNS, dtype=jnp.int32)
    run_hot = run_of[:, None] == run_ids[None, :]
    sel = run_hot.astype(F32)
    n_run = jnp.sum(sel, axis=0)
    comp_run = jnp.max(jnp.where(run_hot, comp_ids[:, None], -1), axis=0).astype(F32)
    n_safe = jnp.maximum(n_run, 1.0)[:, None]

    def run_sums(x):
        return dot(sel, x, ((0,), (0,)))

    def at_nodes(table):
        return dot(sel, table, ((1,), (0,)))

    def to_owners(columns):
        k = columns.shape[1]
        doubled = jnp.broadcast_to(columns[:, None, :], (half, 2, k))
        return doubled.reshape(blocks, items, k)

    def from_owners(x):
        k = x.shape[-1]
        return x.reshape(half, 2, k)[:, 0, :]

    def mine(x, axis):
        return lax.dynamic_slice_in_dim(x, r * half, half, axis)

    params = mine(norm_params, 2)
    column = (b * items + jnp.arange(items, dtype=jnp.int32)) // 2
    column_hot = (
        jnp.arange(half, dtype=jnp.int32)[:, None] == column[None, :]
    ).astype(F32)
    owned = dot(params.reshape(6, half), column_hot, ((1,), (0,))).reshape(2, 3, items)

    def in_order(own, other, axis):
        return jnp.where(
            r == 0,
            jnp.concatenate([own, other], axis=axis),
            jnp.concatenate([other, own], axis=axis),
        )

    def with_sides(own, near):
        near = jnp.concatenate(near, axis=0)
        return jnp.concatenate([own, in_order(near, other_core(near), 0)], axis=0)

    def fetch(x):
        return [lax.ppermute(x, AXES, side_routes(blocks, d, False)) for d in range(1, BAND + 1)]

    extended = with_sides(node_feat, fetch(node_feat))
    agg_in = tile_products(extended, tile_values, tile_rows, places, valid, row_tiles).astype(BF16)
    z_first = jnp.dot(agg_in, mine(weight_in, 1), preferred_element_type=F32)

    sums_first = run_sums(z_first)
    run_means = sums_first / n_safe
    offset = z_first - at_nodes(run_means)
    squares_first = run_sums(offset * offset)
    run_info = jnp.concatenate([n_run, comp_run])
    message = jnp.concatenate(
        [
            sums_first.reshape(-1),
            squares_first.reshape(-1),
            run_info,
            jnp.zeros((half - 2 * RUNS,), F32),
        ]
    )
    got = exchange(jnp.broadcast_to(message[None, None, :], (blocks, 1, message.shape[0])))
    got = got.reshape(-1, half)
    agg_near = with_sides(agg_in, fetch(agg_in))
    offsets = jnp.array([0, -1, -2, -3, 1, 2, 3], jnp.int32)
    table = call(
        combine_kernel,
        jax.ShapeDtypeStruct((3 * 8 * RUNS, half), F32),
        [],
        [(b + offsets) % blocks],
        [got, params[0, 2:3]],
        1 << 30,
    )
    both_tables = in_order(table, other_core(table), 1)
    z_second, hidden = call(
        forward_kernel,
        (
            jax.ShapeDtypeStruct((nodes_here, half), F32),
            jax.ShapeDtypeStruct((nodes_here, hidden_units), BF16),
        ),
        [pltpu.VMEM(((2 * BAND + 1) * nodes_here, half), BF16)],
        [places, tile_rows, tile_count],
        [
            agg_near,
            weight_in,
            mine(weight_hidden, 1),
            both_tables,
            norm_params[0],
            tile_values,
        ],
        1 << 30,
    )
    agg_wide = agg_in.astype(F32)
    mean_first = table[: 8 * RUNS : 8]
    inverse_first = table[8 * RUNS : 16 * RUNS : 8]
    looked = at_nodes(jnp.concatenate([params[0, 2] * mean_first, inverse_first], axis=1))
    normed_first = (z_first - looked[:, :half]) * looked[:, half:]
    slope_first = params[0, 0] * looked[:, half:]
    y_first = params[0, 0] * normed_first + params[0, 1]

    run_feat = lax.all_gather(run_sums(agg_wide), "blk", axis=0, tiled=False)
    run_feat = jnp.transpose(run_feat.reshape(blocks, RUNS, 2, f_half), (2, 0, 1, 3))
    run_feat = run_feat.reshape(2, blocks, RUNS * f_half)

    def per_item(function, *args):
        if items == 1:
            return jax.tree.map(
                lambda x: x[:, None, :], function(*[x[:, 0, :] for x in args])
            )
        return jax.vmap(function, in_axes=1, out_axes=1)(*args)

    d_out = mine(cotangent, 1).astype(F32) / jnp.sqrt(F32(nodes_here * blocks))
    sums = run_sums(jnp.concatenate([z_second, d_out], axis=1))
    run_means = sums[:, :half] / n_safe
    offset = z_second - at_nodes(run_means)
    more = run_sums(jnp.concatenate([offset * offset, offset * d_out], axis=1))
    message = jnp.concatenate(
        [
            sums[:, :half],
            more[:, :half],
            sums[:, half:],
            more[:, half:],
            sums_first,
            squares_first,
            jnp.broadcast_to(run_info[:, None], (2 * RUNS, half)),
            jnp.zeros((128 - 8 * RUNS, half), F32),
        ],
        axis=0,
    ).T
    by_run = (sel[:, :, None] * agg_wide[:, None, :]).reshape(nodes_here, RUNS * features)
    cross = dot(normed_first, by_run, ((0,), (0,)))
    cross = jnp.transpose(cross.reshape(half, RUNS, 2, f_half), (0, 2, 1, 3))
    got = exchange(
        jnp.concatenate(
            [to_owners(message), cross.reshape(blocks, items, RUNS * f_half)], axis=2
        )
    )
    all_stats, all_cross = got[:, :, :128], got[:, :, 128:]
    owned = jnp.transpose(owned.reshape(6, items), (1, 0))[None]
    lanes = jax.ShapeDtypeStruct((blocks, 128), F32)

    def second_owner(stats, own):
        return tuple(call(second_owner_kernel, (lanes, lanes), [], [], [stats, own], 1 << 28))

    back, state = per_item(second_owner, all_stats, owned)
    back = from_owners(exchange(back))
    back = jnp.transpose(back[:, : 4 * RUNS].reshape(half, RUNS, 4), (1, 2, 0))
    back = jnp.where(n_run[:, None, None] > 0, back, 0.0).reshape(RUNS, 4 * half)
    looked = at_nodes(back)
    gamma, beta = params[1, 0], params[1, 1]
    inverse = looked[:, half : 2 * half]
    normed = (z_second - looked[:, :half]) * inverse
    out_mine = (gamma * normed + beta).astype(BF16)
    d_second = gamma * inverse * (d_out - normed * looked[:, 2 * half : 3 * half])
    d_second = (d_second - looked[:, 3 * half :]).astype(BF16)
    swapped = other_core(jnp.concatenate([out_mine, d_second], axis=1))
    node_out = in_order(out_mine, swapped[:, :half], 1)
    d_second = in_order(d_second, swapped[:, half:], 1)

    gathered, near = call(
        transposed_kernel,
        (
            jax.ShapeDtypeStruct((nodes_here, hidden_units), F32),
            jax.ShapeDtypeStruct((BAND * nodes_here, hidden_units), BF16),
        ),
        [pltpu.VMEM(((BAND + 1) * nodes_here, hidden_units), F32)],
        [side_places, tile_rows, side_valid.astype(jnp.int32)],
        [tile_values, d_second],
        1 << 28,
    )
    for d in range(1, BAND + 1):
        gathered = gathered + lax.ppermute(
            near[(d - 1) * nodes_here : d * nodes_here], AXES, side_routes(blocks, d, True)
        ).astype(F32)
    d_projected = (gathered + other_core(gathered)).astype(BF16)

    d_hidden = lax.dot_general(
        d_projected,
        mine(weight_hidden, 0),
        (((1,), (1,)), ((), ())),
        preferred_element_type=F32,
    )
    d_first_y = d_hidden * silu_grad(y_first)
    sums = run_sums(jnp.concatenate([d_first_y, d_first_y * normed_first], axis=1))
    direct = dot(slope_first * d_first_y, agg_wide, ((0,), (0,)))
    w2_part = lax.dot_general(
        mine(d_projected, 1), hidden, (((0,), (0,)), ((), ())), preferred_element_type=F32
    )
    message = jnp.concatenate([sums[:, :half].T, sums[:, half:].T], axis=1)
    got = exchange(
        jnp.concatenate(
            [
                w2_part.reshape(blocks, items, h_half),
                direct.reshape(blocks, items, f_half),
                to_owners(message),
                jnp.zeros((blocks, items, 128 - f_half - 2 * RUNS), F32),
            ],
            axis=2,
        )
    )
    side = (b * items + jnp.arange(items, dtype=jnp.int32)) % 2
    if items == 1:
        feat = lax.dynamic_index_in_dim(run_feat, side[0], 0, True)
    else:
        feat = run_feat[side]
    width = h_half + 128

    def first_owner(*args):
        out = jax.ShapeDtypeStruct((blocks, width), F32)
        return call(first_owner_kernel, out, [], [], list(args), 1 << 28)

    final = exchange(
        per_item(
            first_owner, all_stats, state, owned, got, all_cross, jnp.transpose(feat, (1, 0, 2))
        )
    )
    base = h_half + f_half
    final = final.reshape(half, 2, width)
    final = in_order(final, other_core(final), 0)
    grad_w2 = final[:, :, :h_half].reshape(hidden_units, hidden_units).T
    grad_w1 = final[:, :, h_half:base].reshape(hidden_units, features).T
    grad_norm = final[:, 0, base : base + 6].T.reshape(2, 3, hidden_units)
    return (node_out, grad_w1, grad_w2, grad_norm)


def solution(mesh):
    in_specs = (
        P("blk", None),
        P("blk", None, None),
        P("blk"),
        P("blk"),
        P("blk"),
        P("blk"),
        P(),
        P(),
        P(),
        P("blk", None),
    )
    out_specs = (P("blk", None), P(), P(), P())
    return jax.shard_map(shards, mesh=mesh, in_specs=in_specs, out_specs=out_specs, check_vma=False)
```

```python
import jax
import jax.numpy as jnp
from jax import lax
from jax.experimental import pallas as pl
from jax.experimental.pallas import tpu as pltpu
from jax.sharding import PartitionSpec as P

BAND = 3
RUNS = 4
EPSILON = 1e-05
F32 = jnp.float32
BF16 = jnp.bfloat16
HIGH = lax.Precision.HIGHEST
AXES = ("blk", "rep")


def dot(a, b, contract):
    return lax.dot_general(a, b, (contract, ((), ())), precision=HIGH)


def other_core(x):
    return lax.ppermute(x, "rep", [(0, 1), (1, 0)])


def side_routes(blocks, distance, outward):
    routes = []
    for i in range(blocks):
        low, high = (i - distance) % blocks, (i + distance) % blocks
        if outward:
            routes += [(i * 2, low * 2), (i * 2 + 1, high * 2 + 1)]
        else:
            routes += [(low * 2, i * 2), (high * 2 + 1, i * 2 + 1)]
    return routes


def exchange(x):
    return lax.all_to_all(x, "blk", 0, 0, tiled=True)


def tile_products(pieces, values, rows, places, valid, row_tiles):
    tile = values.shape[1]
    width = pieces.shape[1]
    picked = pieces.reshape(-1, tile, width)[places]
    zero = jnp.zeros((), picked.dtype)
    masked = [
        jnp.where((valid & (rows == r))[:, None, None], picked, zero) for r in range(row_tiles)
    ]
    product = lax.dot_general(
        values,
        jnp.concatenate(masked, axis=2),
        (((0, 2), (0, 1)), ((), ())),
        preferred_element_type=F32,
    )
    return jnp.concatenate(
        [product[:, r * width : (r + 1) * width] for r in range(row_tiles)], axis=0
    )


def parts_of(x):
    high = x.astype(BF16)
    rest = x - high.astype(F32)
    middle = rest.astype(BF16)
    return high, middle, (rest - middle.astype(F32)).astype(BF16)


def hot_dot(hot, x):
    return sum(jnp.dot(hot, part, preferred_element_type=F32) for part in parts_of(x))


def spread_of(total, count, mean, alpha):
    kept = (1.0 - alpha) * mean
    return jnp.sqrt(total / count + kept * kept + EPSILON)


def owner_hots(stats):
    blocks = stats.shape[0]
    flipped = stats[...].T
    across = lax.broadcasted_iota(jnp.int32, (blocks, blocks), 1).astype(F32)
    down = lax.broadcasted_iota(jnp.int32, (blocks, blocks), 0).astype(F32)
    to_comp = [
        (down == flipped[28 + j : 29 + j, :]).astype(F32).astype(BF16) for j in range(RUNS)
    ]
    to_run = [(across == stats[:, 28 + j : 29 + j]).astype(F32).astype(BF16) for j in range(RUNS)]
    return to_comp, to_run


def comp_sums(to_comp, x, firsts):
    lane = lax.broadcasted_iota(jnp.int32, x.shape, 1) % RUNS
    total = jnp.zeros(x.shape, F32)
    for j in range(RUNS):
        total += jnp.where(lane == j, hot_dot(to_comp[j], x), 0.0)
    return [sum(total[:, f + j : f + j + 1] for j in range(RUNS)) for f in firsts]


def in_lanes(columns, shape):
    lane = lax.broadcasted_iota(jnp.int32, shape, 1) % len(columns)
    out = jnp.broadcast_to(columns[0], shape)
    for q in range(1, len(columns)):
        out = jnp.where(lane == q, columns[q], out)
    return out


def run_columns(stats, i, j):
    return stats[:, 4 * i + j : 4 * i + j + 1]


def norm_owner_kernel(stats, owned, back, state):
    blocks = stats.shape[0]
    shape = (blocks, 128)
    lane = lax.broadcasted_iota(jnp.int32, shape, 1)
    to_comp, to_run = owner_hots(stats)
    total, count = comp_sums(to_comp, stats[...], (0, 24))
    mean = total / count
    wide = jnp.broadcast_to(mean, shape)
    total = jnp.zeros((blocks, 1), F32)
    for j in range(RUNS):
        n = run_columns(stats, 6, j)
        here = hot_dot(to_run[j], wide)[:, :1]
        apart = run_columns(stats, 0, j) / jnp.maximum(n, 1.0) - here
        x = jnp.broadcast_to(run_columns(stats, 1, j) + n * apart * apart, shape)
        total += hot_dot(to_comp[j], x)[:, :1]
    spread = spread_of(total, count, mean, owned[:, 2:3])
    give = in_lanes([mean, 1.0 / spread, mean, mean], shape)
    own = jnp.zeros(shape, F32)
    for j in range(RUNS):
        here = jnp.where(lane % 4 == 2, run_columns(stats, 6, j), hot_dot(to_run[j], give))
        own = jnp.where(lane % 16 // 4 == j, here, own)
    out = own
    for k in range(1, 2 * BAND + 1):
        away = -k if k <= BAND else k - BAND
        out = jnp.where(lane // 16 == k, pltpu.roll(own, -away % blocks, 0), out)
    back[...] = out
    state[...] = in_lanes([mean, spread, count, count], shape)


def second_owner_kernel(stats, owned, back, state):
    blocks = stats.shape[0]
    shape = (blocks, 128)
    to_comp, to_run = owner_hots(stats)
    total, rows, count = comp_sums(to_comp, stats[...], (0, 8, 24))
    mean = total / count
    wide = jnp.broadcast_to(mean, shape)
    total = jnp.zeros(shape, F32)
    for j in range(RUNS):
        value = [run_columns(stats, i, j) for i in range(4)]
        n = run_columns(stats, 6, j)
        here = hot_dot(to_run[j], wide)[:, :1]
        apart = value[0] / jnp.maximum(n, 1.0) - here
        x = in_lanes([value[1] + n * apart * apart, value[3] + apart * value[2]], shape)
        total += hot_dot(to_comp[j], x)
    gamma, alpha = owned[:, 3:4], owned[:, 5:6]
    spread = spread_of(total[:, :1], count, mean, alpha)
    kept = (1.0 - alpha) * mean
    proj = (total[:, 1:2] + kept * rows) / spread
    whole = gamma / spread * (rows - kept * proj / spread)
    give = in_lanes([alpha * mean, 1.0 / spread, proj / count, alpha * whole / count], shape)
    lane = lax.broadcasted_iota(jnp.int32, shape, 1)
    out = jnp.zeros(shape, F32)
    for j in range(RUNS):
        out = jnp.where(lane // 4 == j, hot_dot(to_run[j], give), out)
    back[...] = out
    grads = [jnp.sum(c, axis=0, keepdims=True) for c in (proj, rows, mean * whole)]
    state[...] = in_lanes([grads[0], grads[1], -grads[2], grads[0]], shape)


def first_owner_kernel(stats, state, grads_second, owned, sums, cross, feat, final):
    blocks = stats.shape[0]
    shape = (blocks, 128)
    wide = cross.shape[1]
    f_half = wide // RUNS
    to_comp, to_run = owner_hots(stats)
    h_half = sums.shape[1] - 128
    rows, proj = comp_sums(to_comp, sums[:, h_half:], (f_half, f_half + RUNS))
    mean, spread, count = state[:, :1], state[:, 1:2], state[:, 2:3]
    gamma, alpha = owned[:, :1], owned[:, 2:3]
    whole = gamma / spread * (rows - (1.0 - alpha) * mean * proj / spread)
    give = in_lanes([gamma / spread * proj / count, alpha * whole / count], shape)
    lane = lax.broadcasted_iota(jnp.int32, (blocks, wide), 1)
    on_cross = jnp.zeros((blocks, wide), F32)
    on_feat = jnp.zeros((blocks, wide), F32)
    for j in range(RUNS):
        here = hot_dot(to_run[j], give)
        on_cross = jnp.where(lane // f_half == j, here[:, :1], on_cross)
        on_feat = jnp.where(lane // f_half == j, here[:, 1:2], on_feat)
    less = jnp.sum(on_cross * cross[...] + on_feat * feat[...], axis=0, keepdims=True)
    added = jnp.sum(sums[...], axis=0, keepdims=True)
    tail = added[:, h_half : h_half + f_half]
    for j in range(RUNS):
        tail = tail - less[:, j * f_half : (j + 1) * f_half]
    grads = [jnp.sum(c, axis=0, keepdims=True) for c in (proj, rows, mean * whole)]
    lane = lax.broadcasted_iota(jnp.int32, (1, 128 - f_half), 1)
    rest = jnp.zeros((1, 128 - f_half), F32)
    values = [grads[0], grads[1], -grads[2]] + [grads_second[:1, q : q + 1] for q in range(3)]
    for q in range(6):
        rest = jnp.where(lane == q, values[q], rest)
    row = jnp.concatenate([added[:, :h_half], tail, rest], axis=1)
    final[...] = jnp.broadcast_to(row, final.shape)


def forward_kernel(
    places, rows, count, agg, weight_in, weight_out, table, params, values, z, hidden, proj
):
    nodes = hidden.shape[0]
    width = hidden.shape[1]
    tile = values.shape[1]
    node = lax.broadcasted_iota(jnp.int32, (nodes, width), 0).astype(F32)

    def block(k, unused):
        at = pl.ds(pl.multiple_of(k * nodes, nodes), nodes)
        first = jnp.dot(agg[at, :], weight_in[...], preferred_element_type=F32)
        rows_here = table[pl.ds(pl.multiple_of(k * 16, 16), 16), :]
        mean = jnp.broadcast_to(rows_here[0:1, :], (nodes, width))
        inverse = jnp.broadcast_to(rows_here[1:2, :], (nodes, width))
        start = rows_here[2:3, :]
        for j in range(1, RUNS):
            later = node >= start
            mean = jnp.where(later, rows_here[4 * j : 4 * j + 1, :], mean)
            inverse = jnp.where(later, rows_here[4 * j + 1 : 4 * j + 2, :], inverse)
            start = start + rows_here[4 * j + 2 : 4 * j + 3, :]
        normed = (first - params[2:3, :] * mean) * inverse
        y = params[0:1, :] * normed + params[1:2, :]
        low = (y / (1.0 + jnp.exp(-y))).astype(BF16)

        @pl.when(k == 0)
        def _():
            hidden[...] = low

        proj[at, :] = jnp.dot(low, weight_out[...], preferred_element_type=F32).astype(BF16)
        return unused

    lax.fori_loop(0, 2 * BAND + 1, block, 0)
    z[...] = jnp.zeros_like(z)

    def slot(s, unused):
        source = pl.ds(pl.multiple_of(places[s] * tile, tile), tile)
        target = pl.ds(pl.multiple_of(rows[s] * tile, tile), tile)
        z[target, :] += jnp.dot(values[s], proj[source, :], preferred_element_type=F32)
        return unused

    lax.fori_loop(0, count[0], slot, 0)


def transposed_kernel(places, rows, live, values, grads, own, near, total):
    tile = values.shape[1]
    nodes = grads.shape[0]
    total[...] = jnp.zeros_like(total)
    for s in range(values.shape[0]):

        @pl.when(live[s] > 0)
        def _():
            source = pl.ds(pl.multiple_of(rows[s] * tile, tile), tile)
            target = pl.ds(pl.multiple_of(places[s] * tile, tile), tile)
            total[target, :] += lax.dot_general(
                values[s], grads[source, :], (((0,), (0,)), ((), ())), preferred_element_type=F32
            )

    own[...] = total[:nodes, :]
    near[...] = total[nodes:, :].astype(BF16)


def call(kernel, outs, scratch, scalars, arrays, cost):
    return pl.pallas_call(
        kernel,
        out_shape=outs,
        in_specs=[pl.BlockSpec(memory_space=pltpu.SMEM)] * len(scalars)
        + [pl.BlockSpec(memory_space=pltpu.VMEM)] * len(arrays),
        out_specs=jax.tree.map(lambda _: pl.BlockSpec(memory_space=pltpu.VMEM), outs),
        scratch_shapes=scratch,
        cost_estimate=pl.CostEstimate(flops=cost, bytes_accessed=1 << 20, transcendentals=0),
        compiler_params=pltpu.CompilerParams(vmem_limit_bytes=40 << 20),
    )(*scalars, *arrays)


def silu_grad(values):
    logistic = jax.nn.sigmoid(values)
    return logistic * (1.0 + values * (1.0 - logistic))


def shards(
    node_feat,
    tile_values,
    tile_rows,
    tile_cols,
    tile_count,
    comp_ids,
    weight_in,
    weight_hidden,
    norm_params,
    cotangent,
):
    nodes_here, features = node_feat.shape
    hidden_units = weight_hidden.shape[0]
    tile = tile_values.shape[1]
    row_tiles = nodes_here // tile
    blocks = lax.axis_size("blk")
    b = lax.axis_index("blk")
    r = lax.axis_index("rep")
    half = hidden_units // 2
    items = 2 * half // blocks
    f_half = features // 2
    h_half = hidden_units // 2

    slots = jnp.arange(tile_values.shape[0], dtype=jnp.int32)
    valid = slots < tile_count[0]
    distance = (tile_cols // row_tiles - b) % blocks
    signed = jnp.where(distance > blocks // 2, distance - blocks, distance)
    signed = jnp.where(valid, signed, 0)
    within = tile_cols % row_tiles
    places = jnp.where(signed > 0, BAND + signed, -signed) * row_tiles + within
    own_side = jnp.where(signed == 0, r == 0, (signed < 0) == (r == 0))
    side_valid = valid & own_side
    side_places = jnp.where(side_valid, jnp.abs(signed) * row_tiles + within, 0)

    node = jnp.arange(nodes_here, dtype=jnp.int32)
    changed = jnp.concatenate(
        [jnp.zeros((1,), jnp.int32), (comp_ids[1:] != comp_ids[:-1]).astype(jnp.int32)]
    )
    run_of = jnp.sum(
        jnp.where(node[None, :] <= node[:, None], changed[None, :], 0), axis=1
    )
    run_ids = jnp.arange(RUNS, dtype=jnp.int32)
    run_hot = run_of[:, None] == run_ids[None, :]
    sel = run_hot.astype(F32)
    n_run = jnp.sum(sel, axis=0)
    comp_run = jnp.max(jnp.where(run_hot, comp_ids[:, None], -1), axis=0).astype(F32)
    n_safe = jnp.maximum(n_run, 1.0)[:, None]

    def run_sums(x):
        return dot(sel, x, ((0,), (0,)))

    def at_nodes(table):
        return dot(sel, table, ((1,), (0,)))

    def to_owners(columns):
        k = columns.shape[1]
        doubled = jnp.broadcast_to(columns[:, None, :], (half, 2, k))
        return doubled.reshape(blocks, items, k)

    def from_owners(x):
        k = x.shape[-1]
        return x.reshape(half, 2, k)[:, 0, :]

    def mine(x, axis):
        return lax.dynamic_slice_in_dim(x, r * half, half, axis)

    params = mine(norm_params, 2)
    column = (b * items + jnp.arange(items, dtype=jnp.int32)) // 2
    column_hot = (
        jnp.arange(half, dtype=jnp.int32)[:, None] == column[None, :]
    ).astype(F32)
    owned = dot(params.reshape(6, half), column_hot, ((1,), (0,))).reshape(2, 3, items)

    def in_order(own, other, axis):
        return jnp.where(
            r == 0,
            jnp.concatenate([own, other], axis=axis),
            jnp.concatenate([other, own], axis=axis),
        )

    def with_sides(own, near):
        near = jnp.concatenate(near, axis=0)
        return jnp.concatenate([own, in_order(near, other_core(near), 0)], axis=0)

    def fetch(x):
        return [lax.ppermute(x, AXES, side_routes(blocks, d, False)) for d in range(1, BAND + 1)]

    extended = with_sides(node_feat, fetch(node_feat))
    agg_in = tile_products(extended, tile_values, tile_rows, places, valid, row_tiles).astype(BF16)
    z_first = jnp.dot(agg_in, mine(weight_in, 1), preferred_element_type=F32)

    agg_wide = agg_in.astype(F32)
    sums_first = run_sums(jnp.concatenate([z_first, agg_wide], axis=1))
    run_feat = sums_first[:, half:]
    sums_first = sums_first[:, :half]
    run_means = sums_first / n_safe
    offset = z_first - at_nodes(run_means)
    squares_first = run_sums(offset * offset)
    run_info = jnp.broadcast_to(jnp.concatenate([n_run, comp_run])[:, None], (2 * RUNS, half))
    filler = jnp.zeros((128 - 8 * RUNS, half), F32)
    message = jnp.concatenate(
        [sums_first, squares_first, jnp.zeros((4 * RUNS, half), F32), run_info, filler], axis=0
    ).T
    run_feat = jnp.transpose(run_feat.reshape(RUNS, 2, f_half), (1, 0, 2))
    run_feat = jnp.broadcast_to(
        run_feat.reshape(1, 2, RUNS * f_half), (half, 2, RUNS * f_half)
    ).reshape(blocks, items, RUNS * f_half)
    got = exchange(jnp.concatenate([to_owners(message), run_feat], axis=2))
    agg_near = with_sides(agg_in, fetch(agg_in))
    first_stats, all_feat = got[:, :, :128], got[:, :, 128:]
    owned = jnp.transpose(owned.reshape(6, items), (1, 0))[None]
    lanes = jax.ShapeDtypeStruct((blocks, 128), F32)

    def per_item(function, *args):
        if items == 1:
            return jax.tree.map(
                lambda x: x[:, None, :], function(*[x[:, 0, :] for x in args])
            )
        return jax.vmap(function, in_axes=1, out_axes=1)(*args)

    def norm_owner(stats, own):
        return tuple(call(norm_owner_kernel, (lanes, lanes), [], [], [stats, own], 1 << 28))

    back, state_first = per_item(norm_owner, first_stats, owned)
    table = from_owners(exchange(back)).T
    both_tables = in_order(table, other_core(table), 1)
    z_second, hidden = call(
        forward_kernel,
        (
            jax.ShapeDtypeStruct((nodes_here, half), F32),
            jax.ShapeDtypeStruct((nodes_here, hidden_units), BF16),
        ),
        [pltpu.VMEM(((2 * BAND + 1) * nodes_here, half), BF16)],
        [places, tile_rows, tile_count],
        [
            agg_near,
            weight_in,
            mine(weight_hidden, 1),
            both_tables,
            norm_params[0],
            tile_values,
        ],
        1 << 30,
    )
    mean_first = table[0 : 4 * RUNS : 4]
    inverse_first = jnp.where(n_run[:, None] > 0, table[1 : 4 * RUNS : 4], 0.0)
    looked = at_nodes(jnp.concatenate([params[0, 2] * mean_first, inverse_first], axis=1))
    normed_first = (z_first - looked[:, :half]) * looked[:, half:]
    slope_first = params[0, 0] * looked[:, half:]
    y_first = params[0, 0] * normed_first + params[0, 1]

    d_out = mine(cotangent, 1).astype(F32) / jnp.sqrt(F32(nodes_here * blocks))
    sums = run_sums(jnp.concatenate([z_second, d_out], axis=1))
    run_means = sums[:, :half] / n_safe
    offset = z_second - at_nodes(run_means)
    more = run_sums(jnp.concatenate([offset * offset, offset * d_out], axis=1))
    message = jnp.concatenate(
        [
            sums[:, :half],
            more[:, :half],
            sums[:, half:],
            more[:, half:],
            jnp.zeros((2 * RUNS, half), F32),
            run_info,
            filler,
        ],
        axis=0,
    ).T
    by_run = (sel[:, :, None] * agg_wide[:, None, :]).reshape(nodes_here, RUNS * features)
    cross = dot(normed_first, by_run, ((0,), (0,)))
    cross = jnp.transpose(cross.reshape(half, RUNS, 2, f_half), (0, 2, 1, 3))
    got = exchange(
        jnp.concatenate(
            [to_owners(message), cross.reshape(blocks, items, RUNS * f_half)], axis=2
        )
    )
    all_stats, all_cross = got[:, :, :128], got[:, :, 128:]
    def second_owner(stats, own):
        return tuple(call(second_owner_kernel, (lanes, lanes), [], [], [stats, own], 1 << 28))

    back, state = per_item(second_owner, all_stats, owned)
    back = from_owners(exchange(back))
    back = jnp.transpose(back[:, : 4 * RUNS].reshape(half, RUNS, 4), (1, 2, 0))
    back = jnp.where(n_run[:, None, None] > 0, back, 0.0).reshape(RUNS, 4 * half)
    looked = at_nodes(back)
    gamma, beta = params[1, 0], params[1, 1]
    inverse = looked[:, half : 2 * half]
    normed = (z_second - looked[:, :half]) * inverse
    out_mine = (gamma * normed + beta).astype(BF16)
    d_second = gamma * inverse * (d_out - normed * looked[:, 2 * half : 3 * half])
    d_second = (d_second - looked[:, 3 * half :]).astype(BF16)
    swapped = other_core(jnp.concatenate([out_mine, d_second], axis=1))
    node_out = in_order(out_mine, swapped[:, :half], 1)
    d_second = in_order(d_second, swapped[:, half:], 1)

    gathered, near = call(
        transposed_kernel,
        (
            jax.ShapeDtypeStruct((nodes_here, hidden_units), F32),
            jax.ShapeDtypeStruct((BAND * nodes_here, hidden_units), BF16),
        ),
        [pltpu.VMEM(((BAND + 1) * nodes_here, hidden_units), F32)],
        [side_places, tile_rows, side_valid.astype(jnp.int32)],
        [tile_values, d_second],
        1 << 28,
    )
    for d in range(1, BAND + 1):
        gathered = gathered + lax.ppermute(
            near[(d - 1) * nodes_here : d * nodes_here], AXES, side_routes(blocks, d, True)
        ).astype(F32)
    d_projected = (gathered + other_core(gathered)).astype(BF16)

    d_hidden = lax.dot_general(
        d_projected,
        mine(weight_hidden, 0),
        (((1,), (1,)), ((), ())),
        preferred_element_type=F32,
    )
    d_first_y = d_hidden * silu_grad(y_first)
    sums = run_sums(jnp.concatenate([d_first_y, d_first_y * normed_first], axis=1))
    direct = dot(slope_first * d_first_y, agg_wide, ((0,), (0,)))
    w2_part = lax.dot_general(
        mine(d_projected, 1), hidden, (((0,), (0,)), ((), ())), preferred_element_type=F32
    )
    message = jnp.concatenate([sums[:, :half].T, sums[:, half:].T], axis=1)
    got = exchange(
        jnp.concatenate(
            [
                w2_part.reshape(blocks, items, h_half),
                direct.reshape(blocks, items, f_half),
                to_owners(message),
                jnp.zeros((blocks, items, 128 - f_half - 2 * RUNS), F32),
            ],
            axis=2,
        )
    )
    width = h_half + 128

    def first_owner(*args):
        out = jax.ShapeDtypeStruct((blocks, width), F32)
        return call(first_owner_kernel, out, [], [], list(args), 1 << 28)

    final = exchange(
        per_item(
            first_owner, all_stats, state_first, state, owned, got, all_cross, all_feat
        )
    )
    base = h_half + f_half
    final = final.reshape(half, 2, width)
    final = in_order(final, other_core(final), 0)
    grad_w2 = final[:, :, :h_half].reshape(hidden_units, hidden_units).T
    grad_w1 = final[:, :, h_half:base].reshape(hidden_units, features).T
    grad_norm = final[:, 0, base : base + 6].T.reshape(2, 3, hidden_units)
    return (node_out, grad_w1, grad_w2, grad_norm)


def solution(mesh):
    in_specs = (
        P("blk", None),
        P("blk", None, None),
        P("blk"),
        P("blk"),
        P("blk"),
        P("blk"),
        P(),
        P(),
        P(),
        P("blk", None),
    )
    out_specs = (P("blk", None), P(), P(), P())
    return jax.shard_map(shards, mesh=mesh, in_specs=in_specs, out_specs=out_specs, check_vma=False)
```

```python
import jax
import jax.numpy as jnp
from jax import lax
from jax.experimental import pallas as pl
from jax.experimental.pallas import tpu as pltpu
from jax.sharding import PartitionSpec as P

BAND = 3
RUNS = 4
EPSILON = 1e-05
F32 = jnp.float32
BF16 = jnp.bfloat16
HIGH = lax.Precision.HIGHEST
AXES = ("blk", "rep")


def dot(a, b, contract):
    return lax.dot_general(a, b, (contract, ((), ())), precision=HIGH)


def other_core(x):
    return lax.ppermute(x, "rep", [(0, 1), (1, 0)])


def side_routes(blocks, distance, outward):
    routes = []
    for i in range(blocks):
        low, high = (i - distance) % blocks, (i + distance) % blocks
        if outward:
            routes += [(i * 2, low * 2), (i * 2 + 1, high * 2 + 1)]
        else:
            routes += [(low * 2, i * 2), (high * 2 + 1, i * 2 + 1)]
    return routes


def exchange(x):
    return lax.all_to_all(x, "blk", 0, 0, tiled=True)


def tile_products(pieces, values, rows, places, valid, row_tiles):
    tile = values.shape[1]
    width = pieces.shape[1]
    picked = pieces.reshape(-1, tile, width)[places]
    zero = jnp.zeros((), picked.dtype)
    masked = [
        jnp.where((valid & (rows == r))[:, None, None], picked, zero) for r in range(row_tiles)
    ]
    product = lax.dot_general(
        values,
        jnp.concatenate(masked, axis=2),
        (((0, 2), (0, 1)), ((), ())),
        preferred_element_type=F32,
    )
    return jnp.concatenate(
        [product[:, r * width : (r + 1) * width] for r in range(row_tiles)], axis=0
    )


def parts_of(x):
    high = x.astype(BF16)
    rest = x - high.astype(F32)
    middle = rest.astype(BF16)
    return high, middle, (rest - middle.astype(F32)).astype(BF16)


def hot_dot(hot, x):
    return sum(jnp.dot(hot, part, preferred_element_type=F32) for part in parts_of(x))


def spread_of(total, count, mean, alpha):
    kept = (1.0 - alpha) * mean
    return jnp.sqrt(total / count + kept * kept + EPSILON)


def owner_hots(stats):
    blocks = stats.shape[0]
    flipped = stats[...].T
    across = lax.broadcasted_iota(jnp.int32, (blocks, blocks), 1).astype(F32)
    down = lax.broadcasted_iota(jnp.int32, (blocks, blocks), 0).astype(F32)
    to_comp = [
        (down == flipped[28 + j : 29 + j, :]).astype(F32).astype(BF16) for j in range(RUNS)
    ]
    to_run = [(across == stats[:, 28 + j : 29 + j]).astype(F32).astype(BF16) for j in range(RUNS)]
    return to_comp, to_run


def comp_sums(to_comp, x, firsts):
    lane = lax.broadcasted_iota(jnp.int32, x.shape, 1) % RUNS
    total = jnp.zeros(x.shape, F32)
    for j in range(RUNS):
        total += jnp.where(lane == j, hot_dot(to_comp[j], x), 0.0)
    return [sum(total[:, f + j : f + j + 1] for j in range(RUNS)) for f in firsts]


def in_lanes(columns, shape):
    lane = lax.broadcasted_iota(jnp.int32, shape, 1) % len(columns)
    out = jnp.broadcast_to(columns[0], shape)
    for q in range(1, len(columns)):
        out = jnp.where(lane == q, columns[q], out)
    return out


def run_columns(stats, i, j):
    return stats[:, 4 * i + j : 4 * i + j + 1]


def norm_owner_kernel(stats, owned, back, state):
    blocks = stats.shape[0]
    shape = (blocks, 128)
    lane = lax.broadcasted_iota(jnp.int32, shape, 1)
    to_comp, to_run = owner_hots(stats)
    total, count = comp_sums(to_comp, stats[...], (0, 24))
    mean = total / count
    wide = jnp.broadcast_to(mean, shape)
    total = jnp.zeros((blocks, 1), F32)
    for j in range(RUNS):
        n = run_columns(stats, 6, j)
        here = hot_dot(to_run[j], wide)[:, :1]
        apart = run_columns(stats, 0, j) / jnp.maximum(n, 1.0) - here
        x = jnp.broadcast_to(run_columns(stats, 1, j) + n * apart * apart, shape)
        total += hot_dot(to_comp[j], x)[:, :1]
    spread = spread_of(total, count, mean, owned[:, 2:3])
    give = in_lanes([mean, 1.0 / spread, mean, mean], shape)
    own = jnp.zeros(shape, F32)
    for j in range(RUNS):
        here = jnp.where(lane % 4 == 2, run_columns(stats, 6, j), hot_dot(to_run[j], give))
        own = jnp.where(lane % 16 // 4 == j, here, own)
    out = own
    for k in range(1, 2 * BAND + 1):
        away = -k if k <= BAND else k - BAND
        out = jnp.where(lane // 16 == k, pltpu.roll(own, -away % blocks, 0), out)
    back[...] = out
    state[...] = in_lanes([mean, spread, count, count], shape)


def second_owner_kernel(stats, owned, back, state):
    blocks = stats.shape[0]
    shape = (blocks, 128)
    to_comp, to_run = owner_hots(stats)
    total, rows, count = comp_sums(to_comp, stats[...], (0, 8, 24))
    mean = total / count
    wide = jnp.broadcast_to(mean, shape)
    total = jnp.zeros(shape, F32)
    for j in range(RUNS):
        value = [run_columns(stats, i, j) for i in range(4)]
        n = run_columns(stats, 6, j)
        here = hot_dot(to_run[j], wide)[:, :1]
        apart = value[0] / jnp.maximum(n, 1.0) - here
        x = in_lanes([value[1] + n * apart * apart, value[3] + apart * value[2]], shape)
        total += hot_dot(to_comp[j], x)
    gamma, alpha = owned[:, 3:4], owned[:, 5:6]
    spread = spread_of(total[:, :1], count, mean, alpha)
    kept = (1.0 - alpha) * mean
    proj = (total[:, 1:2] + kept * rows) / spread
    whole = gamma / spread * (rows - kept * proj / spread)
    give = in_lanes([alpha * mean, 1.0 / spread, proj / count, alpha * whole / count], shape)
    lane = lax.broadcasted_iota(jnp.int32, shape, 1)
    out = jnp.zeros(shape, F32)
    for j in range(RUNS):
        out = jnp.where(lane // 4 == j, hot_dot(to_run[j], give), out)
    back[...] = out
    grads = [jnp.sum(c, axis=0, keepdims=True) for c in (proj, rows, mean * whole)]
    state[...] = in_lanes([grads[0], grads[1], -grads[2], grads[0]], shape)


def first_owner_kernel(stats, state, grads_second, owned, sums, cross, feat, final):
    blocks = stats.shape[0]
    shape = (blocks, 128)
    wide = cross.shape[1]
    f_half = wide // RUNS
    to_comp, to_run = owner_hots(stats)
    h_half = sums.shape[1] - 128
    rows, proj = comp_sums(to_comp, sums[:, h_half:], (f_half, f_half + RUNS))
    mean, spread, count = state[:, :1], state[:, 1:2], state[:, 2:3]
    gamma, alpha = owned[:, :1], owned[:, 2:3]
    whole = gamma / spread * (rows - (1.0 - alpha) * mean * proj / spread)
    give = in_lanes([gamma / spread * proj / count, alpha * whole / count], shape)
    lane = lax.broadcasted_iota(jnp.int32, (blocks, wide), 1)
    on_cross = jnp.zeros((blocks, wide), F32)
    on_feat = jnp.zeros((blocks, wide), F32)
    for j in range(RUNS):
        here = hot_dot(to_run[j], give)
        on_cross = jnp.where(lane // f_half == j, here[:, :1], on_cross)
        on_feat = jnp.where(lane // f_half == j, here[:, 1:2], on_feat)
    less = jnp.sum(on_cross * cross[...] + on_feat * feat[...], axis=0, keepdims=True)
    added = jnp.sum(sums[...], axis=0, keepdims=True)
    tail = added[:, h_half : h_half + f_half]
    for j in range(RUNS):
        tail = tail - less[:, j * f_half : (j + 1) * f_half]
    grads = [jnp.sum(c, axis=0, keepdims=True) for c in (proj, rows, mean * whole)]
    lane = lax.broadcasted_iota(jnp.int32, (1, 128 - f_half), 1)
    rest = jnp.zeros((1, 128 - f_half), F32)
    values = [grads[0], grads[1], -grads[2]] + [grads_second[:1, q : q + 1] for q in range(3)]
    for q in range(6):
        rest = jnp.where(lane == q, values[q], rest)
    row = jnp.concatenate([added[:, :h_half], tail, rest], axis=1)
    final[...] = jnp.broadcast_to(row, final.shape)


def forward_kernel(
    places,
    rows,
    count,
    core,
    agg,
    weight_in,
    weight_out,
    own,
    other,
    params,
    values,
    z,
    hidden,
    normed_own,
    y_own,
    slope_own,
    proj,
    table,
):
    nodes = hidden.shape[0]
    width = hidden.shape[1]
    half = width // 2
    lower = core[0] == 0
    mine = own[pl.ds(0, half, stride=2), :].T
    theirs = other[pl.ds(0, half, stride=2), :].T
    table[:, :half] = jnp.where(lower, mine, theirs)
    table[:, half:] = jnp.where(lower, theirs, mine)

    def own_half(x):
        return jnp.where(lower, x[:, :half], x[:, half:])

    tile = values.shape[1]
    node = lax.broadcasted_iota(jnp.int32, (nodes, width), 0).astype(F32)

    def block(k, unused):
        at = pl.ds(pl.multiple_of(k * nodes, nodes), nodes)
        first = jnp.dot(agg[at, :], weight_in[...], preferred_element_type=F32)
        rows_here = table[pl.ds(pl.multiple_of(k * 16, 16), 16), :]
        mean = jnp.broadcast_to(rows_here[0:1, :], (nodes, width))
        inverse = jnp.broadcast_to(rows_here[1:2, :], (nodes, width))
        start = rows_here[2:3, :]
        for j in range(1, RUNS):
            later = node >= start
            mean = jnp.where(later, rows_here[4 * j : 4 * j + 1, :], mean)
            inverse = jnp.where(later, rows_here[4 * j + 1 : 4 * j + 2, :], inverse)
            start = start + rows_here[4 * j + 2 : 4 * j + 3, :]
        normed = (first - params[2:3, :] * mean) * inverse
        y = params[0:1, :] * normed + params[1:2, :]
        low = (y / (1.0 + jnp.exp(-y))).astype(BF16)

        @pl.when(k == 0)
        def _():
            hidden[...] = low
            normed_own[...] = own_half(normed)
            y_own[...] = own_half(y)
            slope_own[...] = own_half(params[0:1, :] * inverse)

        proj[at, :] = jnp.dot(low, weight_out[...], preferred_element_type=F32).astype(BF16)
        return unused

    lax.fori_loop(0, 2 * BAND + 1, block, 0)
    z[...] = jnp.zeros_like(z)

    def slot(s, unused):
        source = pl.ds(pl.multiple_of(places[s] * tile, tile), tile)
        target = pl.ds(pl.multiple_of(rows[s] * tile, tile), tile)
        z[target, :] += jnp.dot(values[s], proj[source, :], preferred_element_type=F32)
        return unused

    lax.fori_loop(0, count[0], slot, 0)


def transposed_kernel(places, rows, live, values, grads, own, near, total):
    tile = values.shape[1]
    nodes = grads.shape[0]
    total[...] = jnp.zeros_like(total)
    for s in range(values.shape[0]):

        @pl.when(live[s] > 0)
        def _():
            source = pl.ds(pl.multiple_of(rows[s] * tile, tile), tile)
            target = pl.ds(pl.multiple_of(places[s] * tile, tile), tile)
            total[target, :] += lax.dot_general(
                values[s], grads[source, :], (((0,), (0,)), ((), ())), preferred_element_type=F32
            )

    own[...] = total[:nodes, :]
    near[...] = total[nodes:, :].astype(BF16)


def final_kernel(core, own, other, grad_w1, grad_w2, grad_norm):
    half = own.shape[0] // 4
    lower = core[0] == 0
    parts = []
    for ref in (own, other):
        second = [ref[pl.ds(2 * h, half, stride=4), :].T for h in range(2)]
        first = [ref[pl.ds(2 * h + 1, half, stride=4), :].T for h in range(2)]
        f_half = grad_w1.shape[0] // 2
        parts.append(
            (
                jnp.concatenate([x[:f_half, :] for x in first], axis=0),
                jnp.concatenate(second, axis=0),
                first[0][f_half : f_half + 8, :],
            )
        )
    for out, mine, theirs in zip((grad_w1, grad_w2), *[p[:2] for p in parts]):
        out[:, :half] = jnp.where(lower, mine, theirs)
        out[:, half:] = jnp.where(lower, theirs, mine)
    for i in range(2):
        mine, theirs = [p[2][3 * i : 3 * i + 3, :] for p in parts]
        grad_norm[i, :, :half] = jnp.where(lower, mine, theirs)
        grad_norm[i, :, half:] = jnp.where(lower, theirs, mine)


def call(kernel, outs, scratch, scalars, arrays, cost):
    return pl.pallas_call(
        kernel,
        out_shape=outs,
        in_specs=[pl.BlockSpec(memory_space=pltpu.SMEM)] * len(scalars)
        + [pl.BlockSpec(memory_space=pltpu.VMEM)] * len(arrays),
        out_specs=jax.tree.map(lambda _: pl.BlockSpec(memory_space=pltpu.VMEM), outs),
        scratch_shapes=scratch,
        cost_estimate=pl.CostEstimate(flops=cost, bytes_accessed=1 << 20, transcendentals=0),
        compiler_params=pltpu.CompilerParams(vmem_limit_bytes=40 << 20),
    )(*scalars, *arrays)


def silu_grad(values):
    logistic = jax.nn.sigmoid(values)
    return logistic * (1.0 + values * (1.0 - logistic))


def shards(
    node_feat,
    tile_values,
    tile_rows,
    tile_cols,
    tile_count,
    comp_ids,
    weight_in,
    weight_hidden,
    norm_params,
    cotangent,
):
    nodes_here, features = node_feat.shape
    hidden_units = weight_hidden.shape[0]
    tile = tile_values.shape[1]
    row_tiles = nodes_here // tile
    blocks = lax.axis_size("blk")
    b = lax.axis_index("blk")
    r = lax.axis_index("rep")
    half = hidden_units // 2
    items = 2 * half // blocks
    f_half = features // 2
    h_half = hidden_units // 2

    slots = jnp.arange(tile_values.shape[0], dtype=jnp.int32)
    valid = slots < tile_count[0]
    distance = (tile_cols // row_tiles - b) % blocks
    signed = jnp.where(distance > blocks // 2, distance - blocks, distance)
    signed = jnp.where(valid, signed, 0)
    within = tile_cols % row_tiles
    places = jnp.where(signed > 0, BAND + signed, -signed) * row_tiles + within
    own_side = jnp.where(signed == 0, r == 0, (signed < 0) == (r == 0))
    side_valid = valid & own_side
    side_places = jnp.where(side_valid, jnp.abs(signed) * row_tiles + within, 0)

    node = jnp.arange(nodes_here, dtype=jnp.int32)
    changed = jnp.concatenate(
        [jnp.zeros((1,), jnp.int32), (comp_ids[1:] != comp_ids[:-1]).astype(jnp.int32)]
    )
    run_of = jnp.sum(
        jnp.where(node[None, :] <= node[:, None], changed[None, :], 0), axis=1
    )
    run_ids = jnp.arange(RUNS, dtype=jnp.int32)
    run_hot = run_of[:, None] == run_ids[None, :]
    sel = run_hot.astype(F32)
    n_run = jnp.sum(sel, axis=0)
    comp_run = jnp.max(jnp.where(run_hot, comp_ids[:, None], -1), axis=0).astype(F32)
    n_safe = jnp.maximum(n_run, 1.0)[:, None]

    def run_sums(x):
        return dot(sel, x, ((0,), (0,)))

    def at_nodes(table):
        return dot(sel, table, ((1,), (0,)))

    def to_owners(columns):
        k = columns.shape[1]
        doubled = jnp.broadcast_to(columns[:, None, :], (half, 2, k))
        return doubled.reshape(blocks, items, k)

    def from_owners(x):
        k = x.shape[-1]
        return x.reshape(half, 2, k)[:, 0, :]

    def mine(x, axis):
        return lax.dynamic_slice_in_dim(x, r * half, half, axis)

    params = mine(norm_params, 2)
    column = (b * items + jnp.arange(items, dtype=jnp.int32)) // 2
    column_hot = (
        jnp.arange(half, dtype=jnp.int32)[:, None] == column[None, :]
    ).astype(F32)
    owned = dot(params.reshape(6, half), column_hot, ((1,), (0,))).reshape(2, 3, items)

    def in_order(own, other, axis):
        return jnp.where(
            r == 0,
            jnp.concatenate([own, other], axis=axis),
            jnp.concatenate([other, own], axis=axis),
        )

    def with_sides(own, near):
        near = jnp.concatenate(near, axis=0)
        return jnp.concatenate([own, in_order(near, other_core(near), 0)], axis=0)

    def fetch(x):
        return [lax.ppermute(x, AXES, side_routes(blocks, d, False)) for d in range(1, BAND + 1)]

    extended = with_sides(node_feat, fetch(node_feat))
    agg_in = tile_products(extended, tile_values, tile_rows, places, valid, row_tiles).astype(BF16)
    z_first = jnp.dot(agg_in, mine(weight_in, 1), preferred_element_type=F32)

    agg_wide = agg_in.astype(F32)
    sums_first = run_sums(jnp.concatenate([z_first, agg_wide], axis=1))
    run_feat = sums_first[:, half:]
    sums_first = sums_first[:, :half]
    run_means = sums_first / n_safe
    offset = z_first - at_nodes(run_means)
    squares_first = run_sums(offset * offset)
    run_info = jnp.broadcast_to(jnp.concatenate([n_run, comp_run])[:, None], (2 * RUNS, half))
    filler = jnp.zeros((128 - 8 * RUNS, half), F32)
    message = jnp.concatenate(
        [sums_first, squares_first, jnp.zeros((4 * RUNS, half), F32), run_info, filler], axis=0
    ).T
    run_feat = jnp.transpose(run_feat.reshape(RUNS, 2, f_half), (1, 0, 2))
    run_feat = jnp.broadcast_to(
        run_feat.reshape(1, 2, RUNS * f_half), (half, 2, RUNS * f_half)
    ).reshape(blocks, items, RUNS * f_half)
    got = exchange(jnp.concatenate([to_owners(message), run_feat], axis=2))
    agg_pieces = fetch(agg_in)
    first_stats, all_feat = got[:, :, :128], got[:, :, 128:]
    owned = jnp.transpose(owned.reshape(6, items), (1, 0))[None]
    lanes = jax.ShapeDtypeStruct((blocks, 128), F32)

    def per_item(function, *args):
        if items == 1:
            return jax.tree.map(
                lambda x: x[:, None, :], function(*[x[:, 0, :] for x in args])
            )
        return jax.vmap(function, in_axes=1, out_axes=1)(*args)

    def norm_owner(stats, own):
        return tuple(call(norm_owner_kernel, (lanes, lanes), [], [], [stats, own], 1 << 28))

    back, state_first = per_item(norm_owner, first_stats, owned)
    ready = back[0, 0, 2] >= 0.0
    agg_near = with_sides(agg_in, [jnp.where(ready, x, jnp.zeros_like(x)) for x in agg_pieces])
    table = exchange(back).reshape(2 * half, 128)
    near_blocks = 2 * BAND + 1
    core = jnp.reshape(r, (1,))
    own_wide = jax.ShapeDtypeStruct((nodes_here, half), F32)
    z_second, hidden, normed_first, y_first, slope_first = call(
        forward_kernel,
        (
            own_wide,
            jax.ShapeDtypeStruct((nodes_here, hidden_units), BF16),
            own_wide,
            own_wide,
            own_wide,
        ),
        [
            pltpu.VMEM((near_blocks * nodes_here, half), BF16),
            pltpu.VMEM((128, hidden_units), F32),
        ],
        [places, tile_rows, tile_count, core],
        [
            agg_near,
            weight_in,
            mine(weight_hidden, 1),
            table,
            other_core(table),
            norm_params[0],
            tile_values,
        ],
        1 << 30,
    )

    d_out = mine(cotangent, 1).astype(F32) / jnp.sqrt(F32(nodes_here * blocks))
    sums = run_sums(jnp.concatenate([z_second, d_out], axis=1))
    run_means = sums[:, :half] / n_safe
    offset = z_second - at_nodes(run_means)
    more = run_sums(jnp.concatenate([offset * offset, offset * d_out], axis=1))
    message = jnp.concatenate(
        [
            sums[:, :half],
            more[:, :half],
            sums[:, half:],
            more[:, half:],
            jnp.zeros((2 * RUNS, half), F32),
            run_info,
            filler,
        ],
        axis=0,
    ).T
    by_run = (sel[:, :, None] * agg_wide[:, None, :]).reshape(nodes_here, RUNS * features)
    cross = dot(normed_first, by_run, ((0,), (0,)))
    cross = jnp.transpose(cross.reshape(half, RUNS, 2, f_half), (0, 2, 1, 3))
    got = exchange(
        jnp.concatenate(
            [to_owners(message), cross.reshape(blocks, items, RUNS * f_half)], axis=2
        )
    )
    all_stats, all_cross = got[:, :, :128], got[:, :, 128:]
    def second_owner(stats, own):
        return tuple(call(second_owner_kernel, (lanes, lanes), [], [], [stats, own], 1 << 28))

    back, state = per_item(second_owner, all_stats, owned)
    back = from_owners(exchange(back))
    back = jnp.transpose(back[:, : 4 * RUNS].reshape(half, RUNS, 4), (1, 2, 0))
    back = jnp.where(n_run[:, None, None] > 0, back, 0.0).reshape(RUNS, 4 * half)
    looked = at_nodes(back)
    gamma, beta = params[1, 0], params[1, 1]
    inverse = looked[:, half : 2 * half]
    normed = (z_second - looked[:, :half]) * inverse
    out_mine = (gamma * normed + beta).astype(BF16)
    d_second = gamma * inverse * (d_out - normed * looked[:, 2 * half : 3 * half])
    d_second = (d_second - looked[:, 3 * half :]).astype(BF16)
    swapped = other_core(jnp.concatenate([out_mine, d_second], axis=1))
    node_out = in_order(out_mine, swapped[:, :half], 1)
    d_second = in_order(d_second, swapped[:, half:], 1)

    gathered, near = call(
        transposed_kernel,
        (
            jax.ShapeDtypeStruct((nodes_here, hidden_units), F32),
            jax.ShapeDtypeStruct((BAND * nodes_here, hidden_units), BF16),
        ),
        [pltpu.VMEM(((BAND + 1) * nodes_here, hidden_units), F32)],
        [side_places, tile_rows, side_valid.astype(jnp.int32)],
        [tile_values, d_second],
        1 << 28,
    )
    for d in range(1, BAND + 1):
        gathered = gathered + lax.ppermute(
            near[(d - 1) * nodes_here : d * nodes_here], AXES, side_routes(blocks, d, True)
        ).astype(F32)
    d_projected = (gathered + other_core(gathered)).astype(BF16)

    d_hidden = lax.dot_general(
        d_projected,
        mine(weight_hidden, 0),
        (((1,), (1,)), ((), ())),
        preferred_element_type=F32,
    )
    d_first_y = d_hidden * silu_grad(y_first)
    sums = run_sums(jnp.concatenate([d_first_y, d_first_y * normed_first], axis=1))
    direct = dot(slope_first * d_first_y, agg_wide, ((0,), (0,)))
    w2_part = lax.dot_general(
        mine(d_projected, 1), hidden, (((0,), (0,)), ((), ())), preferred_element_type=F32
    )
    message = jnp.concatenate([sums[:, :half].T, sums[:, half:].T], axis=1)
    got = exchange(
        jnp.concatenate(
            [
                w2_part.reshape(blocks, items, h_half),
                direct.reshape(blocks, items, f_half),
                to_owners(message),
                jnp.zeros((blocks, items, 128 - f_half - 2 * RUNS), F32),
            ],
            axis=2,
        )
    )
    width = h_half + 128

    def first_owner(*args):
        out = jax.ShapeDtypeStruct((blocks, width), F32)
        return call(first_owner_kernel, out, [], [], list(args), 1 << 28)

    final = exchange(
        per_item(
            first_owner, all_stats, state_first, state, owned, got, all_cross, all_feat
        )
    )
    final = final.reshape(4 * half, 128)
    grad_w1, grad_w2, grad_norm = call(
        final_kernel,
        (
            jax.ShapeDtypeStruct((features, hidden_units), F32),
            jax.ShapeDtypeStruct((hidden_units, hidden_units), F32),
            jax.ShapeDtypeStruct((2, 3, hidden_units), F32),
        ),
        [],
        [core],
        [final, other_core(final)],
        1 << 20,
    )
    return (node_out, grad_w1, grad_w2, grad_norm)


def solution(mesh):
    in_specs = (
        P("blk", None),
        P("blk", None, None),
        P("blk"),
        P("blk"),
        P("blk"),
        P("blk"),
        P(),
        P(),
        P(),
        P("blk", None),
    )
    out_specs = (P("blk", None), P(), P(), P())
    return jax.shard_map(shards, mesh=mesh, in_specs=in_specs, out_specs=out_specs, check_vma=False)
```

```python
import jax
import jax.numpy as jnp
from jax import lax
from jax.experimental import pallas as pl
from jax.experimental.pallas import tpu as pltpu
from jax.sharding import PartitionSpec as P

BAND = 3
RUNS = 4
EPSILON = 1e-05
F32 = jnp.float32
BF16 = jnp.bfloat16
HIGH = lax.Precision.HIGHEST
AXES = ("blk", "rep")


def dot(a, b, contract):
    return lax.dot_general(a, b, (contract, ((), ())), precision=HIGH)


def other_core(x):
    return lax.ppermute(x, "rep", [(0, 1), (1, 0)])


def side_routes(blocks, distance, outward):
    routes = []
    for i in range(blocks):
        low, high = (i - distance) % blocks, (i + distance) % blocks
        if outward:
            routes += [(i * 2, low * 2), (i * 2 + 1, high * 2 + 1)]
        else:
            routes += [(low * 2, i * 2), (high * 2 + 1, i * 2 + 1)]
    return routes


def exchange(x):
    return lax.all_to_all(x, "blk", 0, 0, tiled=True)


def tile_products(pieces, values, rows, places, valid, row_tiles):
    tile = values.shape[1]
    width = pieces.shape[1]
    picked = pieces.reshape(-1, tile, width)[places]
    zero = jnp.zeros((), picked.dtype)
    masked = [
        jnp.where((valid & (rows == r))[:, None, None], picked, zero) for r in range(row_tiles)
    ]
    product = lax.dot_general(
        values,
        jnp.concatenate(masked, axis=2),
        (((0, 2), (0, 1)), ((), ())),
        preferred_element_type=F32,
    )
    return jnp.concatenate(
        [product[:, r * width : (r + 1) * width] for r in range(row_tiles)], axis=0
    )


def parts_of(x):
    high = x.astype(BF16)
    rest = x - high.astype(F32)
    middle = rest.astype(BF16)
    return high, middle, (rest - middle.astype(F32)).astype(BF16)


def hot_dot(hot, x):
    return sum(jnp.dot(hot, part, preferred_element_type=F32) for part in parts_of(x))


def spread_of(total, count, mean, alpha):
    kept = (1.0 - alpha) * mean
    return jnp.sqrt(total / count + kept * kept + EPSILON)


def owner_hots(stats):
    blocks = stats.shape[0]
    flipped = stats.T
    across = lax.broadcasted_iota(jnp.int32, (blocks, blocks), 1).astype(F32)
    down = lax.broadcasted_iota(jnp.int32, (blocks, blocks), 0).astype(F32)
    to_comp = [
        (down == flipped[28 + j : 29 + j, :]).astype(F32).astype(BF16) for j in range(RUNS)
    ]
    to_run = [(across == stats[:, 28 + j : 29 + j]).astype(F32).astype(BF16) for j in range(RUNS)]
    return to_comp, to_run


def comp_sums(to_comp, x, firsts):
    lane = lax.broadcasted_iota(jnp.int32, x.shape, 1) % RUNS
    total = jnp.zeros(x.shape, F32)
    for j in range(RUNS):
        total += jnp.where(lane == j, hot_dot(to_comp[j], x), 0.0)
    return [sum(total[:, f + j : f + j + 1] for j in range(RUNS)) for f in firsts]


def in_lanes(columns, shape):
    lane = lax.broadcasted_iota(jnp.int32, shape, 1) % len(columns)
    out = jnp.broadcast_to(columns[0], shape)
    for q in range(1, len(columns)):
        out = jnp.where(lane == q, columns[q], out)
    return out


def run_columns(stats, i, j):
    return stats[:, 4 * i + j : 4 * i + j + 1]


def norm_owner_kernel(stats, owned, back, state):
    blocks = stats.shape[0] // 3
    stats = stats[pl.ds(0, blocks, stride=3), :]
    shape = (blocks, 128)
    lane = lax.broadcasted_iota(jnp.int32, shape, 1)
    to_comp, to_run = owner_hots(stats)
    total, count = comp_sums(to_comp, stats, (0, 24))
    mean = total / count
    wide = jnp.broadcast_to(mean, shape)
    total = jnp.zeros((blocks, 1), F32)
    for j in range(RUNS):
        n = run_columns(stats, 6, j)
        here = hot_dot(to_run[j], wide)[:, :1]
        apart = run_columns(stats, 0, j) / jnp.maximum(n, 1.0) - here
        x = jnp.broadcast_to(run_columns(stats, 1, j) + n * apart * apart, shape)
        total += hot_dot(to_comp[j], x)[:, :1]
    spread = spread_of(total, count, mean, owned[:, 2:3])
    give = in_lanes([mean, 1.0 / spread, mean, mean], shape)
    own = jnp.zeros(shape, F32)
    for j in range(RUNS):
        here = jnp.where(lane % 4 == 2, run_columns(stats, 6, j), hot_dot(to_run[j], give))
        own = jnp.where(lane % 16 // 4 == j, here, own)
    out = own
    for k in range(1, 2 * BAND + 1):
        away = -k if k <= BAND else k - BAND
        out = jnp.where(lane // 16 == k, pltpu.roll(own, -away % blocks, 0), out)
    back[...] = out
    state[...] = in_lanes([mean, spread, count, count], shape)


def second_owner_kernel(stats, owned, back, state):
    blocks = stats.shape[0] // 3
    stats = stats[pl.ds(0, blocks, stride=3), :]
    shape = (blocks, 128)
    to_comp, to_run = owner_hots(stats)
    total, rows, count = comp_sums(to_comp, stats, (0, 8, 24))
    mean = total / count
    wide = jnp.broadcast_to(mean, shape)
    total = jnp.zeros(shape, F32)
    for j in range(RUNS):
        value = [run_columns(stats, i, j) for i in range(4)]
        n = run_columns(stats, 6, j)
        here = hot_dot(to_run[j], wide)[:, :1]
        apart = value[0] / jnp.maximum(n, 1.0) - here
        x = in_lanes([value[1] + n * apart * apart, value[3] + apart * value[2]], shape)
        total += hot_dot(to_comp[j], x)
    gamma, alpha = owned[:, 3:4], owned[:, 5:6]
    spread = spread_of(total[:, :1], count, mean, alpha)
    kept = (1.0 - alpha) * mean
    proj = (total[:, 1:2] + kept * rows) / spread
    whole = gamma / spread * (rows - kept * proj / spread)
    give = in_lanes([alpha * mean, 1.0 / spread, proj / count, alpha * whole / count], shape)
    lane = lax.broadcasted_iota(jnp.int32, shape, 1)
    out = jnp.zeros(shape, F32)
    for j in range(RUNS):
        out = jnp.where(lane // 4 == j, hot_dot(to_run[j], give), out)
    back[...] = out
    grads = [jnp.sum(c, axis=0, keepdims=True) for c in (proj, rows, mean * whole)]
    state[...] = in_lanes([grads[0], grads[1], -grads[2], grads[0]], shape)


def first_owner_kernel(first, second, state, grads_second, owned, sums, final):
    blocks = first.shape[0] // 3
    shape = (blocks, 128)
    stats = first[pl.ds(0, blocks, stride=3), :]
    feat = [first[pl.ds(1 + t, blocks, stride=3), :] for t in range(2)]
    cross = [second[pl.ds(1 + t, blocks, stride=3), :] for t in range(2)]
    f_half = 64
    to_comp, to_run = owner_hots(stats)
    h_half = sums.shape[1] - 128
    rows, proj = comp_sums(to_comp, sums[:, h_half:], (f_half, f_half + RUNS))
    mean, spread, count = state[:, :1], state[:, 1:2], state[:, 2:3]
    gamma, alpha = owned[:, :1], owned[:, 2:3]
    whole = gamma / spread * (rows - (1.0 - alpha) * mean * proj / spread)
    give = in_lanes([gamma / spread * proj / count, alpha * whole / count], shape)
    lane = lax.broadcasted_iota(jnp.int32, shape, 1)
    less = jnp.zeros((1, 128), F32)
    for t in range(2):
        here = [hot_dot(to_run[2 * t + j], give) for j in range(2)]
        on_cross = jnp.where(lane < f_half, here[0][:, :1], here[1][:, :1])
        on_feat = jnp.where(lane < f_half, here[0][:, 1:2], here[1][:, 1:2])
        less += jnp.sum(on_cross * cross[t] + on_feat * feat[t], axis=0, keepdims=True)
    added = jnp.sum(sums[...], axis=0, keepdims=True)
    tail = added[:, h_half : h_half + f_half]
    tail = tail - less[:, :f_half] - less[:, f_half:]
    grads = [jnp.sum(c, axis=0, keepdims=True) for c in (proj, rows, mean * whole)]
    lane = lax.broadcasted_iota(jnp.int32, (1, 128 - f_half), 1)
    rest = jnp.zeros((1, 128 - f_half), F32)
    values = [grads[0], grads[1], -grads[2]] + [grads_second[:1, q : q + 1] for q in range(3)]
    for q in range(6):
        rest = jnp.where(lane == q, values[q], rest)
    row = jnp.concatenate([added[:, :h_half], tail, rest], axis=1)
    final[...] = jnp.broadcast_to(row, final.shape)


def run_hots(run_row, run_column, agg):
    rows = lax.broadcasted_iota(jnp.int32, (8, run_row.shape[1]), 0).astype(F32)
    hot = (rows == run_row[...]).astype(F32).astype(BF16)
    at = run_column[...]

    def to_nodes(table):
        out = jnp.broadcast_to(table[0:1, :], agg.shape)
        for j in range(1, RUNS):
            out = jnp.where(at == float(j), table[j : j + 1, :], out)
        return out

    return hot, to_nodes


def store_message(message, stats, wide):
    half = message.shape[0] // 6
    lines = jnp.concatenate(stats, axis=0).T
    for h in range(2):
        message[pl.ds(3 * h, half, stride=6), :] = lines
        for t in range(2):
            message[pl.ds(3 * h + 1 + t, half, stride=6), :] = wide(h, t)


def first_kernel(
    places, rows, count, own, near, other, values, weight, run_row, run_column, info, agg, message, all_, total
):
    nodes = own.shape[0]
    tile = values.shape[1]
    half = weight.shape[1]
    all_[:nodes, :] = own[...]
    all_[nodes : nodes + near.shape[0], :] = near[...]
    all_[nodes + near.shape[0] :, :] = other[...]
    total[...] = jnp.zeros_like(total)

    def slot(s, unused):
        source = pl.ds(pl.multiple_of(places[s] * tile, tile), tile)
        target = pl.ds(pl.multiple_of(rows[s] * tile, tile), tile)
        total[target, :] += jnp.dot(values[s], all_[source, :], preferred_element_type=F32)
        return unused

    lax.fori_loop(0, count[0], slot, 0)
    low = total[...].astype(BF16)
    agg[...] = low
    z = jnp.dot(low, weight[...], preferred_element_type=F32)
    hot, to_nodes = run_hots(run_row, run_column, z)
    sums = hot_dot(hot, z)
    offset = z - to_nodes(sums[:RUNS, :] / jnp.maximum(info[:RUNS, :], 1.0))
    squares = hot_dot(hot, offset * offset)
    feat = jnp.dot(hot, low, preferred_element_type=F32)
    f_half = feat.shape[1] // 2

    def wide(h, t):
        line = [feat[2 * t + j : 2 * t + j + 1, h * f_half : (h + 1) * f_half] for j in range(2)]
        return jnp.broadcast_to(jnp.concatenate(line, axis=1), (half, 2 * f_half))

    stats = [sums[:RUNS, :], squares[:RUNS, :], jnp.zeros((4 * RUNS, half), F32), info[...]]
    store_message(message, stats + [jnp.zeros((128 - 8 * RUNS, half), F32)], wide)


def forward_kernel(
    places,
    rows,
    count,
    core,
    agg,
    weight_in,
    weight_out,
    own,
    other,
    params,
    values,
    run_row,
    run_column,
    info,
    d_out,
    z,
    message,
    hidden,
    normed_own,
    y_own,
    slope_own,
    proj,
    table,
):
    nodes = hidden.shape[0]
    width = hidden.shape[1]
    half = width // 2
    lower = core[0] == 0
    mine = own[pl.ds(0, half, stride=2), :].T
    theirs = other[pl.ds(0, half, stride=2), :].T
    table[:, :half] = jnp.where(lower, mine, theirs)
    table[:, half:] = jnp.where(lower, theirs, mine)

    def own_half(x):
        return jnp.where(lower, x[:, :half], x[:, half:])

    tile = values.shape[1]
    node = lax.broadcasted_iota(jnp.int32, (nodes, width), 0).astype(F32)

    def block(k, unused):
        at = pl.ds(pl.multiple_of(k * nodes, nodes), nodes)
        first = jnp.dot(agg[at, :], weight_in[...], preferred_element_type=F32)
        rows_here = table[pl.ds(pl.multiple_of(k * 16, 16), 16), :]
        mean = jnp.broadcast_to(rows_here[0:1, :], (nodes, width))
        inverse = jnp.broadcast_to(rows_here[1:2, :], (nodes, width))
        start = rows_here[2:3, :]
        for j in range(1, RUNS):
            later = node >= start
            mean = jnp.where(later, rows_here[4 * j : 4 * j + 1, :], mean)
            inverse = jnp.where(later, rows_here[4 * j + 1 : 4 * j + 2, :], inverse)
            start = start + rows_here[4 * j + 2 : 4 * j + 3, :]
        normed = (first - params[2:3, :] * mean) * inverse
        y = params[0:1, :] * normed + params[1:2, :]
        low = (y / (1.0 + jnp.exp(-y))).astype(BF16)

        @pl.when(k == 0)
        def _():
            hidden[...] = low
            normed_own[...] = own_half(normed)
            y_own[...] = own_half(y)
            slope_own[...] = own_half(params[0:1, :] * inverse)

        proj[at, :] = jnp.dot(low, weight_out[...], preferred_element_type=F32).astype(BF16)
        return unused

    lax.fori_loop(0, 2 * BAND + 1, block, 0)
    z[...] = jnp.zeros_like(z)

    def slot(s, unused):
        source = pl.ds(pl.multiple_of(places[s] * tile, tile), tile)
        target = pl.ds(pl.multiple_of(rows[s] * tile, tile), tile)
        z[target, :] += jnp.dot(values[s], proj[source, :], preferred_element_type=F32)
        return unused

    lax.fori_loop(0, count[0], slot, 0)
    hot, to_nodes = run_hots(run_row, run_column, z)
    sums = hot_dot(hot, z[...])
    offset = z[...] - to_nodes(sums[:RUNS, :] / jnp.maximum(info[:RUNS, :], 1.0))
    stats = [sums, hot_dot(hot, offset * offset), hot_dot(hot, d_out[...])]
    stats = [x[:RUNS, :] for x in stats + [hot_dot(hot, offset * d_out[...])]]
    stats += [jnp.zeros((2 * RUNS, half), F32), info[...]]
    flipped = parts_of(normed_own[...].T)
    cross = []
    for j in range(RUNS):
        here = jnp.where(run_column[...] == float(j), agg[:nodes, :].astype(F32), 0.0).astype(BF16)
        cross.append(sum(jnp.dot(x, here, preferred_element_type=F32) for x in flipped))
    f_half = cross[0].shape[1] // 2

    def wide(h, t):
        return jnp.concatenate(
            [cross[2 * t + j][:, h * f_half : (h + 1) * f_half] for j in range(2)], axis=1
        )

    store_message(message, stats + [jnp.zeros((128 - 8 * RUNS, half), F32)], wide)


def transposed_kernel(places, rows, live, values, grads, own, near, total):
    tile = values.shape[1]
    nodes = grads.shape[0]
    total[...] = jnp.zeros_like(total)
    for s in range(values.shape[0]):

        @pl.when(live[s] > 0)
        def _():
            source = pl.ds(pl.multiple_of(rows[s] * tile, tile), tile)
            target = pl.ds(pl.multiple_of(places[s] * tile, tile), tile)
            total[target, :] += lax.dot_general(
                values[s], grads[source, :], (((0,), (0,)), ((), ())), preferred_element_type=F32
            )

    own[...] = total[:nodes, :]
    near[...] = total[nodes:, :].astype(BF16)


def final_kernel(core, own, other, grad_w1, grad_w2, grad_norm):
    half = own.shape[0] // 4
    lower = core[0] == 0
    parts = []
    for ref in (own, other):
        second = [ref[pl.ds(2 * h, half, stride=4), :].T for h in range(2)]
        first = [ref[pl.ds(2 * h + 1, half, stride=4), :].T for h in range(2)]
        f_half = grad_w1.shape[0] // 2
        parts.append(
            (
                jnp.concatenate([x[:f_half, :] for x in first], axis=0),
                jnp.concatenate(second, axis=0),
                first[0][f_half : f_half + 8, :],
            )
        )
    for out, mine, theirs in zip((grad_w1, grad_w2), *[p[:2] for p in parts]):
        out[:, :half] = jnp.where(lower, mine, theirs)
        out[:, half:] = jnp.where(lower, theirs, mine)
    for i in range(2):
        mine, theirs = [p[2][3 * i : 3 * i + 3, :] for p in parts]
        grad_norm[i, :, :half] = jnp.where(lower, mine, theirs)
        grad_norm[i, :, half:] = jnp.where(lower, theirs, mine)


def call(kernel, outs, scratch, scalars, arrays, cost):
    return pl.pallas_call(
        kernel,
        out_shape=outs,
        in_specs=[pl.BlockSpec(memory_space=pltpu.SMEM)] * len(scalars)
        + [pl.BlockSpec(memory_space=pltpu.VMEM)] * len(arrays),
        out_specs=jax.tree.map(lambda _: pl.BlockSpec(memory_space=pltpu.VMEM), outs),
        scratch_shapes=scratch,
        cost_estimate=pl.CostEstimate(flops=cost, bytes_accessed=1 << 20, transcendentals=0),
        compiler_params=pltpu.CompilerParams(vmem_limit_bytes=40 << 20),
    )(*scalars, *arrays)


def silu_grad(values):
    logistic = jax.nn.sigmoid(values)
    return logistic * (1.0 + values * (1.0 - logistic))


def shards(
    node_feat,
    tile_values,
    tile_rows,
    tile_cols,
    tile_count,
    comp_ids,
    weight_in,
    weight_hidden,
    norm_params,
    cotangent,
):
    nodes_here, features = node_feat.shape
    hidden_units = weight_hidden.shape[0]
    tile = tile_values.shape[1]
    row_tiles = nodes_here // tile
    blocks = lax.axis_size("blk")
    b = lax.axis_index("blk")
    r = lax.axis_index("rep")
    half = hidden_units // 2
    items = 2 * half // blocks
    f_half = features // 2
    h_half = hidden_units // 2

    slots = jnp.arange(tile_values.shape[0], dtype=jnp.int32)
    valid = slots < tile_count[0]
    distance = (tile_cols // row_tiles - b) % blocks
    signed = jnp.where(distance > blocks // 2, distance - blocks, distance)
    signed = jnp.where(valid, signed, 0)
    within = tile_cols % row_tiles
    places = jnp.where(signed > 0, BAND + signed, -signed) * row_tiles + within
    own_side = jnp.where(signed == 0, r == 0, (signed < 0) == (r == 0))
    side_valid = valid & own_side
    side_places = jnp.where(side_valid, jnp.abs(signed) * row_tiles + within, 0)

    node = jnp.arange(nodes_here, dtype=jnp.int32)
    changed = jnp.concatenate(
        [jnp.zeros((1,), jnp.int32), (comp_ids[1:] != comp_ids[:-1]).astype(jnp.int32)]
    )
    run_of = jnp.sum(
        jnp.where(node[None, :] <= node[:, None], changed[None, :], 0), axis=1
    )
    run_ids = jnp.arange(RUNS, dtype=jnp.int32)
    run_hot = run_of[:, None] == run_ids[None, :]
    sel = run_hot.astype(F32)
    n_run = jnp.sum(sel, axis=0)
    comp_run = jnp.max(jnp.where(run_hot, comp_ids[:, None], -1), axis=0).astype(F32)

    def run_sums(x):
        return dot(sel, x, ((0,), (0,)))

    def at_nodes(table):
        return dot(sel, table, ((1,), (0,)))

    def to_owners(columns):
        k = columns.shape[1]
        doubled = jnp.broadcast_to(columns[:, None, :], (half, 2, k))
        return doubled.reshape(blocks, items, k)

    def from_owners(x):
        k = x.shape[-1]
        return x.reshape(half, 2, k)[:, 0, :]

    def mine(x, axis):
        return lax.dynamic_slice_in_dim(x, r * half, half, axis)

    params = mine(norm_params, 2)
    column = (b * items + jnp.arange(items, dtype=jnp.int32)) // 2
    column_hot = (
        jnp.arange(half, dtype=jnp.int32)[:, None] == column[None, :]
    ).astype(F32)
    owned = dot(params.reshape(6, half), column_hot, ((1,), (0,))).reshape(2, 3, items)

    def in_order(own, other, axis):
        return jnp.where(
            r == 0,
            jnp.concatenate([own, other], axis=axis),
            jnp.concatenate([other, own], axis=axis),
        )

    def with_sides(own, near):
        near = jnp.concatenate(near, axis=0)
        return jnp.concatenate([own, in_order(near, other_core(near), 0)], axis=0)

    def fetch(x):
        return [lax.ppermute(x, AXES, side_routes(blocks, d, False)) for d in range(1, BAND + 1)]

    run_row, run_column = run_of.astype(F32)[None, :], run_of.astype(F32)[:, None]
    run_info = jnp.broadcast_to(jnp.concatenate([n_run, comp_run])[:, None], (2 * RUNS, half))
    near_feat = jnp.concatenate(fetch(node_feat), axis=0)
    sided = jnp.where(
        signed == 0, 0, jnp.where((signed < 0) == (r == 0), 0, BAND) + jnp.abs(signed)
    )
    wide_message = jax.ShapeDtypeStruct((6 * half, 128), F32)
    agg_in, message = call(
        first_kernel,
        (jax.ShapeDtypeStruct((nodes_here, features), BF16), wide_message),
        [
            pltpu.VMEM(((2 * BAND + 1) * nodes_here, features), BF16),
            pltpu.VMEM((nodes_here, features), F32),
        ],
        [sided * row_tiles + within, tile_rows, tile_count],
        [
            node_feat,
            near_feat,
            other_core(near_feat),
            tile_values,
            mine(weight_in, 1),
            run_row,
            run_column,
            run_info,
        ],
        1 << 28,
    )
    agg_wide = agg_in.astype(F32)
    got_first = exchange(message.reshape(blocks, items, 384))
    agg_pieces = fetch(agg_in)
    owned = jnp.transpose(owned.reshape(6, items), (1, 0))[None]
    lanes = jax.ShapeDtypeStruct((blocks, 128), F32)

    def per_item(function, *args):
        if items == 1:
            return jax.tree.map(
                lambda x: x[:, None, :], function(*[x[:, 0, :] for x in args])
            )
        return jax.vmap(function, in_axes=1, out_axes=1)(*args)

    def lines(x):
        return x.reshape(3 * blocks, 128)

    def norm_owner(stats, own):
        return tuple(call(norm_owner_kernel, (lanes, lanes), [], [], [lines(stats), own], 1 << 28))

    back, state_first = per_item(norm_owner, got_first, owned)
    ready = back[0, 0, 2] >= 0.0
    agg_near = with_sides(agg_in, [jnp.where(ready, x, jnp.zeros_like(x)) for x in agg_pieces])
    table = exchange(back).reshape(2 * half, 128)
    near_blocks = 2 * BAND + 1
    core = jnp.reshape(r, (1,))
    d_out = mine(cotangent, 1).astype(F32) / jnp.sqrt(F32(nodes_here * blocks))
    own_wide = jax.ShapeDtypeStruct((nodes_here, half), F32)
    z_second, message, hidden, normed_first, y_first, slope_first = call(
        forward_kernel,
        (
            own_wide,
            wide_message,
            jax.ShapeDtypeStruct((nodes_here, hidden_units), BF16),
            own_wide,
            own_wide,
            own_wide,
        ),
        [
            pltpu.VMEM((near_blocks * nodes_here, half), BF16),
            pltpu.VMEM((128, hidden_units), F32),
        ],
        [places, tile_rows, tile_count, core],
        [
            agg_near,
            weight_in,
            mine(weight_hidden, 1),
            table,
            other_core(table),
            norm_params[0],
            tile_values,
            run_row,
            run_column,
            run_info,
            d_out,
        ],
        1 << 30,
    )

    got_second = exchange(message.reshape(blocks, items, 384))

    def second_owner(stats, own):
        return tuple(call(second_owner_kernel, (lanes, lanes), [], [], [lines(stats), own], 1 << 28))

    back, state = per_item(second_owner, got_second, owned)
    back = from_owners(exchange(back))
    back = jnp.transpose(back[:, : 4 * RUNS].reshape(half, RUNS, 4), (1, 2, 0))
    back = jnp.where(n_run[:, None, None] > 0, back, 0.0).reshape(RUNS, 4 * half)
    looked = at_nodes(back)
    gamma, beta = params[1, 0], params[1, 1]
    inverse = looked[:, half : 2 * half]
    normed = (z_second - looked[:, :half]) * inverse
    out_mine = (gamma * normed + beta).astype(BF16)
    d_second = gamma * inverse * (d_out - normed * looked[:, 2 * half : 3 * half])
    d_second = (d_second - looked[:, 3 * half :]).astype(BF16)
    swapped = other_core(jnp.concatenate([out_mine, d_second], axis=1))
    node_out = in_order(out_mine, swapped[:, :half], 1)
    d_second = in_order(d_second, swapped[:, half:], 1)

    gathered, near = call(
        transposed_kernel,
        (
            jax.ShapeDtypeStruct((nodes_here, hidden_units), F32),
            jax.ShapeDtypeStruct((BAND * nodes_here, hidden_units), BF16),
        ),
        [pltpu.VMEM(((BAND + 1) * nodes_here, hidden_units), F32)],
        [side_places, tile_rows, side_valid.astype(jnp.int32)],
        [tile_values, d_second],
        1 << 28,
    )
    for d in range(1, BAND + 1):
        gathered = gathered + lax.ppermute(
            near[(d - 1) * nodes_here : d * nodes_here], AXES, side_routes(blocks, d, True)
        ).astype(F32)
    d_projected = (gathered + other_core(gathered)).astype(BF16)

    d_hidden = lax.dot_general(
        d_projected,
        mine(weight_hidden, 0),
        (((1,), (1,)), ((), ())),
        preferred_element_type=F32,
    )
    d_first_y = d_hidden * silu_grad(y_first)
    sums = run_sums(jnp.concatenate([d_first_y, d_first_y * normed_first], axis=1))
    direct = dot(slope_first * d_first_y, agg_wide, ((0,), (0,)))
    w2_part = lax.dot_general(
        mine(d_projected, 1), hidden, (((0,), (0,)), ((), ())), preferred_element_type=F32
    )
    message = jnp.concatenate([sums[:, :half].T, sums[:, half:].T], axis=1)
    got = exchange(
        jnp.concatenate(
            [
                w2_part.reshape(blocks, items, h_half),
                direct.reshape(blocks, items, f_half),
                to_owners(message),
                jnp.zeros((blocks, items, 128 - f_half - 2 * RUNS), F32),
            ],
            axis=2,
        )
    )
    width = h_half + 128

    def first_owner(first, second, *args):
        out = jax.ShapeDtypeStruct((blocks, width), F32)
        return call(first_owner_kernel, out, [], [], [lines(first), lines(second), *args], 1 << 28)

    final = exchange(
        per_item(
            first_owner, got_first, got_second, state_first, state, owned, got
        )
    )
    final = final.reshape(4 * half, 128)
    grad_w1, grad_w2, grad_norm = call(
        final_kernel,
        (
            jax.ShapeDtypeStruct((features, hidden_units), F32),
            jax.ShapeDtypeStruct((hidden_units, hidden_units), F32),
            jax.ShapeDtypeStruct((2, 3, hidden_units), F32),
        ),
        [],
        [core],
        [final, other_core(final)],
        1 << 20,
    )
    return (node_out, grad_w1, grad_w2, grad_norm)


def solution(mesh):
    in_specs = (
        P("blk", None),
        P("blk", None, None),
        P("blk"),
        P("blk"),
        P("blk"),
        P("blk"),
        P(),
        P(),
        P(),
        P("blk", None),
    )
    out_specs = (P("blk", None), P(), P(), P())
    return jax.shard_map(shards, mesh=mesh, in_specs=in_specs, out_specs=out_specs, check_vma=False)
```

```python
import jax
import jax.numpy as jnp
from jax import lax
from jax.experimental import pallas as pl
from jax.experimental.pallas import tpu as pltpu
from jax.sharding import PartitionSpec as P

BAND = 3
RUNS = 4
EPSILON = 1e-05
F32 = jnp.float32
BF16 = jnp.bfloat16
HIGH = lax.Precision.HIGHEST
AXES = ("blk", "rep")


def dot(a, b, contract):
    return lax.dot_general(a, b, (contract, ((), ())), precision=HIGH)


def other_core(x):
    return lax.ppermute(x, "rep", [(0, 1), (1, 0)])


def side_routes(blocks, distance, outward):
    routes = []
    for i in range(blocks):
        low, high = (i - distance) % blocks, (i + distance) % blocks
        if outward:
            routes += [(i * 2, low * 2), (i * 2 + 1, high * 2 + 1)]
        else:
            routes += [(low * 2, i * 2), (high * 2 + 1, i * 2 + 1)]
    return routes


def exchange(x):
    return lax.all_to_all(x, "blk", 0, 0, tiled=True)


def tile_products(pieces, values, rows, places, valid, row_tiles):
    tile = values.shape[1]
    width = pieces.shape[1]
    picked = pieces.reshape(-1, tile, width)[places]
    zero = jnp.zeros((), picked.dtype)
    masked = [
        jnp.where((valid & (rows == r))[:, None, None], picked, zero) for r in range(row_tiles)
    ]
    product = lax.dot_general(
        values,
        jnp.concatenate(masked, axis=2),
        (((0, 2), (0, 1)), ((), ())),
        preferred_element_type=F32,
    )
    return jnp.concatenate(
        [product[:, r * width : (r + 1) * width] for r in range(row_tiles)], axis=0
    )


def parts_of(x):
    high = x.astype(BF16)
    rest = x - high.astype(F32)
    middle = rest.astype(BF16)
    return high, middle, (rest - middle.astype(F32)).astype(BF16)


def hot_dot(hot, x):
    return sum(jnp.dot(hot, part, preferred_element_type=F32) for part in parts_of(x))


def spread_of(total, count, mean, alpha):
    kept = (1.0 - alpha) * mean
    return jnp.sqrt(total / count + kept * kept + EPSILON)


def owner_hots(stats):
    blocks = stats.shape[0]
    flipped = stats.T
    across = lax.broadcasted_iota(jnp.int32, (blocks, blocks), 1).astype(F32)
    down = lax.broadcasted_iota(jnp.int32, (blocks, blocks), 0).astype(F32)
    to_comp = [
        (down == flipped[28 + j : 29 + j, :]).astype(F32).astype(BF16) for j in range(RUNS)
    ]
    to_run = [(across == stats[:, 28 + j : 29 + j]).astype(F32).astype(BF16) for j in range(RUNS)]
    return to_comp, to_run


def comp_sums(to_comp, x, firsts):
    lane = lax.broadcasted_iota(jnp.int32, x.shape, 1) % RUNS
    total = jnp.zeros(x.shape, F32)
    for j in range(RUNS):
        total += jnp.where(lane == j, hot_dot(to_comp[j], x), 0.0)
    return [sum(total[:, f + j : f + j + 1] for j in range(RUNS)) for f in firsts]


def in_lanes(columns, shape):
    lane = lax.broadcasted_iota(jnp.int32, shape, 1) % len(columns)
    out = jnp.broadcast_to(columns[0], shape)
    for q in range(1, len(columns)):
        out = jnp.where(lane == q, columns[q], out)
    return out


def run_columns(stats, i, j):
    return stats[:, 4 * i + j : 4 * i + j + 1]


def norm_owner_kernel(stats, owned, arrived_first, arrived_second, back, state, ready):
    blocks = stats.shape[0] // 3
    stats = stats[pl.ds(0, blocks, stride=3), :]
    shape = (blocks, 128)
    lane = lax.broadcasted_iota(jnp.int32, shape, 1)
    to_comp, to_run = owner_hots(stats)
    total, count = comp_sums(to_comp, stats, (0, 24))
    mean = total / count
    wide = jnp.broadcast_to(mean, shape)
    total = jnp.zeros((blocks, 1), F32)
    for j in range(RUNS):
        n = run_columns(stats, 6, j)
        here = hot_dot(to_run[j], wide)[:, :1]
        apart = run_columns(stats, 0, j) / jnp.maximum(n, 1.0) - here
        x = jnp.broadcast_to(run_columns(stats, 1, j) + n * apart * apart, shape)
        total += hot_dot(to_comp[j], x)[:, :1]
    spread = spread_of(total, count, mean, owned[:, 2:3])
    give = in_lanes([mean, 1.0 / spread, mean, mean], shape)
    own = jnp.zeros(shape, F32)
    for j in range(RUNS):
        here = jnp.where(lane % 4 == 2, run_columns(stats, 6, j), hot_dot(to_run[j], give))
        own = jnp.where(lane % 16 // 4 == j, here, own)
    out = own
    for k in range(1, 2 * BAND + 1):
        away = -k if k <= BAND else k - BAND
        out = jnp.where(lane // 16 == k, pltpu.roll(own, -away % blocks, 0), out)
    back[...] = out
    state[...] = in_lanes([mean, spread, count, count], shape)
    ready[...] = jnp.broadcast_to((count[:1, :] >= 0.0).astype(F32), ready.shape).astype(BF16)


def second_owner_kernel(stats, owned, back, state):
    blocks = stats.shape[0] // 3
    stats = stats[pl.ds(0, blocks, stride=3), :]
    shape = (blocks, 128)
    to_comp, to_run = owner_hots(stats)
    total, rows, count = comp_sums(to_comp, stats, (0, 8, 24))
    mean = total / count
    wide = jnp.broadcast_to(mean, shape)
    total = jnp.zeros(shape, F32)
    for j in range(RUNS):
        value = [run_columns(stats, i, j) for i in range(4)]
        n = run_columns(stats, 6, j)
        here = hot_dot(to_run[j], wide)[:, :1]
        apart = value[0] / jnp.maximum(n, 1.0) - here
        x = in_lanes([value[1] + n * apart * apart, value[3] + apart * value[2]], shape)
        total += hot_dot(to_comp[j], x)
    gamma, alpha = owned[:, 3:4], owned[:, 5:6]
    spread = spread_of(total[:, :1], count, mean, alpha)
    kept = (1.0 - alpha) * mean
    proj = (total[:, 1:2] + kept * rows) / spread
    whole = gamma / spread * (rows - kept * proj / spread)
    give = in_lanes([alpha * mean, 1.0 / spread, proj / count, alpha * whole / count], shape)
    lane = lax.broadcasted_iota(jnp.int32, shape, 1)
    out = jnp.zeros(shape, F32)
    for j in range(RUNS):
        out = jnp.where(lane // 4 == j, hot_dot(to_run[j], give), out)
    back[...] = out
    grads = [jnp.sum(c, axis=0, keepdims=True) for c in (proj, rows, mean * whole)]
    state[...] = in_lanes([grads[0], grads[1], -grads[2], grads[0]], shape)


def first_owner_kernel(first, second, state, grads_second, owned, sums, final):
    blocks = first.shape[0] // 3
    shape = (blocks, 128)
    stats = first[pl.ds(0, blocks, stride=3), :]
    feat = [first[pl.ds(1 + t, blocks, stride=3), :] for t in range(2)]
    cross = [second[pl.ds(1 + t, blocks, stride=3), :] for t in range(2)]
    f_half = 64
    to_comp, to_run = owner_hots(stats)
    h_half = sums.shape[1] - 128
    rows, proj = comp_sums(to_comp, sums[:, h_half:], (f_half, f_half + RUNS))
    mean, spread, count = state[:, :1], state[:, 1:2], state[:, 2:3]
    gamma, alpha = owned[:, :1], owned[:, 2:3]
    whole = gamma / spread * (rows - (1.0 - alpha) * mean * proj / spread)
    give = in_lanes([gamma / spread * proj / count, alpha * whole / count], shape)
    lane = lax.broadcasted_iota(jnp.int32, shape, 1)
    less = jnp.zeros((1, 128), F32)
    for t in range(2):
        here = [hot_dot(to_run[2 * t + j], give) for j in range(2)]
        on_cross = jnp.where(lane < f_half, here[0][:, :1], here[1][:, :1])
        on_feat = jnp.where(lane < f_half, here[0][:, 1:2], here[1][:, 1:2])
        less += jnp.sum(on_cross * cross[t] + on_feat * feat[t], axis=0, keepdims=True)
    added = jnp.sum(sums[...], axis=0, keepdims=True)
    tail = added[:, h_half : h_half + f_half]
    tail = tail - less[:, :f_half] - less[:, f_half:]
    grads = [jnp.sum(c, axis=0, keepdims=True) for c in (proj, rows, mean * whole)]
    lane = lax.broadcasted_iota(jnp.int32, (1, 128 - f_half), 1)
    rest = jnp.zeros((1, 128 - f_half), F32)
    values = [grads[0], grads[1], -grads[2]] + [grads_second[:1, q : q + 1] for q in range(3)]
    for q in range(6):
        rest = jnp.where(lane == q, values[q], rest)
    row = jnp.concatenate([added[:, :h_half], tail, rest], axis=1)
    final[...] = jnp.broadcast_to(row, final.shape)


def run_hots(run_row, run_column, agg):
    rows = lax.broadcasted_iota(jnp.int32, (8, run_row.shape[1]), 0).astype(F32)
    hot = (rows == run_row[...]).astype(F32).astype(BF16)
    at = run_column[...]

    def to_nodes(table):
        out = jnp.broadcast_to(table[0:1, :], agg.shape)
        for j in range(1, RUNS):
            out = jnp.where(at == float(j), table[j : j + 1, :], out)
        return out

    return hot, to_nodes


def store_message(message, stats, wide):
    half = message.shape[0] // 6
    lines = jnp.concatenate(stats, axis=0).T
    for h in range(2):
        message[pl.ds(3 * h, half, stride=6), :] = lines
        for t in range(2):
            message[pl.ds(3 * h + 1 + t, half, stride=6), :] = wide(h, t)


def first_kernel(
    places, rows, count, own, near, other, values, weight, run_row, run_column, info, agg, message, all_, total
):
    nodes = own.shape[0]
    tile = values.shape[1]
    half = weight.shape[1]
    all_[:nodes, :] = own[...]
    all_[nodes : nodes + near.shape[0], :] = near[...]
    all_[nodes + near.shape[0] :, :] = other[...]
    total[...] = jnp.zeros_like(total)

    def slot(s, unused):
        source = pl.ds(pl.multiple_of(places[s] * tile, tile), tile)
        target = pl.ds(pl.multiple_of(rows[s] * tile, tile), tile)
        total[target, :] += jnp.dot(values[s], all_[source, :], preferred_element_type=F32)
        return unused

    lax.fori_loop(0, count[0], slot, 0)
    low = total[...].astype(BF16)
    agg[...] = low
    z = jnp.dot(low, weight[...], preferred_element_type=F32)
    hot, to_nodes = run_hots(run_row, run_column, z)
    sums = hot_dot(hot, z)
    offset = z - to_nodes(sums[:RUNS, :] / jnp.maximum(info[:RUNS, :], 1.0))
    squares = hot_dot(hot, offset * offset)
    feat = jnp.dot(hot, low, preferred_element_type=F32)
    f_half = feat.shape[1] // 2

    def wide(h, t):
        line = [feat[2 * t + j : 2 * t + j + 1, h * f_half : (h + 1) * f_half] for j in range(2)]
        return jnp.broadcast_to(jnp.concatenate(line, axis=1), (half, 2 * f_half))

    stats = [sums[:RUNS, :], squares[:RUNS, :], jnp.zeros((4 * RUNS, half), F32), info[...]]
    store_message(message, stats + [jnp.zeros((128 - 8 * RUNS, half), F32)], wide)


def forward_kernel(
    places,
    rows,
    count,
    core,
    agg,
    near,
    far,
    weight_in,
    weight_out,
    own,
    other,
    params,
    values,
    run_row,
    run_column,
    info,
    d_out,
    z,
    message,
    hidden,
    normed_own,
    y_own,
    slope_own,
    proj,
    table,
    all_,
):
    nodes = hidden.shape[0]
    width = hidden.shape[1]
    half = width // 2
    lower = core[0] == 0
    mine = own[pl.ds(0, half, stride=2), :].T
    theirs = other[pl.ds(0, half, stride=2), :].T
    table[:, :half] = jnp.where(lower, mine, theirs)
    table[:, half:] = jnp.where(lower, theirs, mine)

    all_[:nodes, :] = agg[...]
    all_[nodes : nodes + near.shape[0], :] = near[...]
    all_[nodes + near.shape[0] :, :] = far[...]

    def own_half(x):
        return jnp.where(lower, x[:, :half], x[:, half:])

    tile = values.shape[1]
    node = lax.broadcasted_iota(jnp.int32, (nodes, width), 0).astype(F32)

    def block(k, unused):
        at = pl.ds(pl.multiple_of(k * nodes, nodes), nodes)
        first = jnp.dot(all_[at, :], weight_in[...], preferred_element_type=F32)
        swapped = jnp.where(k == 0, 0, jnp.where(k <= BAND, k + BAND, k - BAND))
        here = jnp.where(lower, k, swapped)
        rows_here = table[pl.ds(pl.multiple_of(here * 16, 16), 16), :]
        mean = jnp.broadcast_to(rows_here[0:1, :], (nodes, width))
        inverse = jnp.broadcast_to(rows_here[1:2, :], (nodes, width))
        start = rows_here[2:3, :]
        for j in range(1, RUNS):
            later = node >= start
            mean = jnp.where(later, rows_here[4 * j : 4 * j + 1, :], mean)
            inverse = jnp.where(later, rows_here[4 * j + 1 : 4 * j + 2, :], inverse)
            start = start + rows_here[4 * j + 2 : 4 * j + 3, :]
        normed = (first - params[2:3, :] * mean) * inverse
        y = params[0:1, :] * normed + params[1:2, :]
        low = (y / (1.0 + jnp.exp(-y))).astype(BF16)

        @pl.when(k == 0)
        def _():
            hidden[...] = low
            normed_own[...] = own_half(normed)
            y_own[...] = own_half(y)
            slope_own[...] = own_half(params[0:1, :] * inverse)

        proj[at, :] = jnp.dot(low, weight_out[...], preferred_element_type=F32).astype(BF16)
        return unused

    lax.fori_loop(0, 2 * BAND + 1, block, 0)
    z[...] = jnp.zeros_like(z)

    def slot(s, unused):
        source = pl.ds(pl.multiple_of(places[s] * tile, tile), tile)
        target = pl.ds(pl.multiple_of(rows[s] * tile, tile), tile)
        z[target, :] += jnp.dot(values[s], proj[source, :], preferred_element_type=F32)
        return unused

    lax.fori_loop(0, count[0], slot, 0)
    hot, to_nodes = run_hots(run_row, run_column, z)
    sums = hot_dot(hot, z[...])
    offset = z[...] - to_nodes(sums[:RUNS, :] / jnp.maximum(info[:RUNS, :], 1.0))
    stats = [sums, hot_dot(hot, offset * offset), hot_dot(hot, d_out[...])]
    stats = [x[:RUNS, :] for x in stats + [hot_dot(hot, offset * d_out[...])]]
    stats += [jnp.zeros((2 * RUNS, half), F32), info[...]]
    flipped = parts_of(normed_own[...].T)
    cross = []
    for j in range(RUNS):
        here = jnp.where(run_column[...] == float(j), agg[...].astype(F32), 0.0).astype(BF16)
        cross.append(sum(jnp.dot(x, here, preferred_element_type=F32) for x in flipped))
    f_half = cross[0].shape[1] // 2

    def wide(h, t):
        return jnp.concatenate(
            [cross[2 * t + j][:, h * f_half : (h + 1) * f_half] for j in range(2)], axis=1
        )

    store_message(message, stats + [jnp.zeros((128 - 8 * RUNS, half), F32)], wide)


def transposed_kernel(places, rows, live, values, grads, own, near, total):
    tile = values.shape[1]
    nodes = grads.shape[0]
    total[...] = jnp.zeros_like(total)
    for s in range(values.shape[0]):

        @pl.when(live[s] > 0)
        def _():
            source = pl.ds(pl.multiple_of(rows[s] * tile, tile), tile)
            target = pl.ds(pl.multiple_of(places[s] * tile, tile), tile)
            total[target, :] += lax.dot_general(
                values[s], grads[source, :], (((0,), (0,)), ((), ())), preferred_element_type=F32
            )

    own[...] = total[:nodes, :]
    near[...] = total[nodes:, :].astype(BF16)


def final_kernel(core, own, other, grad_w1, grad_w2, grad_norm):
    half = own.shape[0] // 4
    lower = core[0] == 0
    parts = []
    for ref in (own, other):
        second = [ref[pl.ds(2 * h, half, stride=4), :].T for h in range(2)]
        first = [ref[pl.ds(2 * h + 1, half, stride=4), :].T for h in range(2)]
        f_half = grad_w1.shape[0] // 2
        parts.append(
            (
                jnp.concatenate([x[:f_half, :] for x in first], axis=0),
                jnp.concatenate(second, axis=0),
                first[0][f_half : f_half + 8, :],
            )
        )
    for out, mine, theirs in zip((grad_w1, grad_w2), *[p[:2] for p in parts]):
        out[:, :half] = jnp.where(lower, mine, theirs)
        out[:, half:] = jnp.where(lower, theirs, mine)
    for i in range(2):
        mine, theirs = [p[2][3 * i : 3 * i + 3, :] for p in parts]
        grad_norm[i, :, :half] = jnp.where(lower, mine, theirs)
        grad_norm[i, :, half:] = jnp.where(lower, theirs, mine)


def call(kernel, outs, scratch, scalars, arrays, cost):
    return pl.pallas_call(
        kernel,
        out_shape=outs,
        in_specs=[pl.BlockSpec(memory_space=pltpu.SMEM)] * len(scalars)
        + [pl.BlockSpec(memory_space=pltpu.VMEM)] * len(arrays),
        out_specs=jax.tree.map(lambda _: pl.BlockSpec(memory_space=pltpu.VMEM), outs),
        scratch_shapes=scratch,
        cost_estimate=pl.CostEstimate(flops=cost, bytes_accessed=1 << 20, transcendentals=0),
        compiler_params=pltpu.CompilerParams(vmem_limit_bytes=40 << 20),
    )(*scalars, *arrays)


def silu_grad(values):
    logistic = jax.nn.sigmoid(values)
    return logistic * (1.0 + values * (1.0 - logistic))


def shards(
    node_feat,
    tile_values,
    tile_rows,
    tile_cols,
    tile_count,
    comp_ids,
    weight_in,
    weight_hidden,
    norm_params,
    cotangent,
):
    nodes_here, features = node_feat.shape
    hidden_units = weight_hidden.shape[0]
    tile = tile_values.shape[1]
    row_tiles = nodes_here // tile
    blocks = lax.axis_size("blk")
    b = lax.axis_index("blk")
    r = lax.axis_index("rep")
    half = hidden_units // 2
    items = 2 * half // blocks
    f_half = features // 2
    h_half = hidden_units // 2

    slots = jnp.arange(tile_values.shape[0], dtype=jnp.int32)
    valid = slots < tile_count[0]
    distance = (tile_cols // row_tiles - b) % blocks
    signed = jnp.where(distance > blocks // 2, distance - blocks, distance)
    signed = jnp.where(valid, signed, 0)
    within = tile_cols % row_tiles
    places = jnp.where(signed > 0, BAND + signed, -signed) * row_tiles + within
    own_side = jnp.where(signed == 0, r == 0, (signed < 0) == (r == 0))
    side_valid = valid & own_side
    side_places = jnp.where(side_valid, jnp.abs(signed) * row_tiles + within, 0)

    node = jnp.arange(nodes_here, dtype=jnp.int32)
    changed = jnp.concatenate(
        [jnp.zeros((1,), jnp.int32), (comp_ids[1:] != comp_ids[:-1]).astype(jnp.int32)]
    )
    run_of = jnp.sum(
        jnp.where(node[None, :] <= node[:, None], changed[None, :], 0), axis=1
    )
    run_ids = jnp.arange(RUNS, dtype=jnp.int32)
    run_hot = run_of[:, None] == run_ids[None, :]
    sel = run_hot.astype(F32)
    n_run = jnp.sum(sel, axis=0)
    comp_run = jnp.max(jnp.where(run_hot, comp_ids[:, None], -1), axis=0).astype(F32)

    def run_sums(x):
        return dot(sel, x, ((0,), (0,)))

    def at_nodes(table):
        return dot(sel, table, ((1,), (0,)))

    def to_owners(columns):
        k = columns.shape[1]
        doubled = jnp.broadcast_to(columns[:, None, :], (half, 2, k))
        return doubled.reshape(blocks, items, k)

    def from_owners(x):
        k = x.shape[-1]
        return x.reshape(half, 2, k)[:, 0, :]

    def mine(x, axis):
        return lax.dynamic_slice_in_dim(x, r * half, half, axis)

    params = mine(norm_params, 2)
    column = (b * items + jnp.arange(items, dtype=jnp.int32)) // 2
    column_hot = (
        jnp.arange(half, dtype=jnp.int32)[:, None] == column[None, :]
    ).astype(F32)
    owned = dot(params.reshape(6, half), column_hot, ((1,), (0,))).reshape(2, 3, items)

    def in_order(own, other, axis):
        return jnp.where(
            r == 0,
            jnp.concatenate([own, other], axis=axis),
            jnp.concatenate([other, own], axis=axis),
        )

    def fetch(x):
        return [lax.ppermute(x, AXES, side_routes(blocks, d, False)) for d in range(1, BAND + 1)]

    run_row, run_column = run_of.astype(F32)[None, :], run_of.astype(F32)[:, None]
    run_info = jnp.broadcast_to(jnp.concatenate([n_run, comp_run])[:, None], (2 * RUNS, half))
    near_feat = jnp.concatenate(fetch(node_feat), axis=0)
    sided = jnp.where(
        signed == 0, 0, jnp.where((signed < 0) == (r == 0), 0, BAND) + jnp.abs(signed)
    )
    wide_message = jax.ShapeDtypeStruct((6 * half, 128), F32)
    agg_in, message = call(
        first_kernel,
        (jax.ShapeDtypeStruct((nodes_here, features), BF16), wide_message),
        [
            pltpu.VMEM(((2 * BAND + 1) * nodes_here, features), BF16),
            pltpu.VMEM((nodes_here, features), F32),
        ],
        [sided * row_tiles + within, tile_rows, tile_count],
        [
            node_feat,
            near_feat,
            other_core(near_feat),
            tile_values,
            mine(weight_in, 1),
            run_row,
            run_column,
            run_info,
        ],
        1 << 28,
    )
    agg_wide = agg_in.astype(F32)
    got_first = exchange(message.reshape(blocks, items, 384))
    agg_pieces = fetch(agg_in)
    owned = jnp.transpose(owned.reshape(6, items), (1, 0))[None]
    lanes = jax.ShapeDtypeStruct((blocks, 128), F32)

    def per_item(function, *args):
        if items == 1:
            return jax.tree.map(
                lambda x: x[:, None, :], function(*[x[:, 0, :] for x in args])
            )
        return jax.vmap(function, in_axes=1, out_axes=1)(*args)

    def lines(x):
        return x.reshape(3 * blocks, 128)

    def norm_owner(stats, own):
        flag = jax.ShapeDtypeStruct((16, 128), BF16)
        outs = (lanes, lanes, flag)
        return tuple(call(norm_owner_kernel, outs, [], [], [lines(stats), own, *agg_pieces[:2]], 1 << 28))

    back, state_first, ready = per_item(norm_owner, got_first, owned)
    ready = jnp.tile(ready[:, 0, :features], (nodes_here // 16, 1))
    near_agg = jnp.concatenate([x * ready for x in agg_pieces], axis=0)
    table = exchange(back).reshape(2 * half, 128)
    near_blocks = 2 * BAND + 1
    core = jnp.reshape(r, (1,))
    d_out = mine(cotangent, 1).astype(F32) / jnp.sqrt(F32(nodes_here * blocks))
    own_wide = jax.ShapeDtypeStruct((nodes_here, half), F32)
    z_second, message, hidden, normed_first, y_first, slope_first = call(
        forward_kernel,
        (
            own_wide,
            wide_message,
            jax.ShapeDtypeStruct((nodes_here, hidden_units), BF16),
            own_wide,
            own_wide,
            own_wide,
        ),
        [
            pltpu.VMEM((near_blocks * nodes_here, half), BF16),
            pltpu.VMEM((128, hidden_units), F32),
            pltpu.VMEM((near_blocks * nodes_here, features), BF16),
        ],
        [sided * row_tiles + within, tile_rows, tile_count, core],
        [
            agg_in,
            near_agg,
            other_core(near_agg),
            weight_in,
            mine(weight_hidden, 1),
            table,
            other_core(table),
            norm_params[0],
            tile_values,
            run_row,
            run_column,
            run_info,
            d_out,
        ],
        1 << 30,
    )

    got_second = exchange(message.reshape(blocks, items, 384))

    def second_owner(stats, own):
        return tuple(call(second_owner_kernel, (lanes, lanes), [], [], [lines(stats), own], 1 << 28))

    back, state = per_item(second_owner, got_second, owned)
    back = from_owners(exchange(back))
    back = jnp.transpose(back[:, : 4 * RUNS].reshape(half, RUNS, 4), (1, 2, 0))
    back = jnp.where(n_run[:, None, None] > 0, back, 0.0).reshape(RUNS, 4 * half)
    looked = at_nodes(back)
    gamma, beta = params[1, 0], params[1, 1]
    inverse = looked[:, half : 2 * half]
    normed = (z_second - looked[:, :half]) * inverse
    out_mine = (gamma * normed + beta).astype(BF16)
    d_second = gamma * inverse * (d_out - normed * looked[:, 2 * half : 3 * half])
    d_second = (d_second - looked[:, 3 * half :]).astype(BF16)
    swapped = other_core(jnp.concatenate([out_mine, d_second], axis=1))
    node_out = in_order(out_mine, swapped[:, :half], 1)
    d_second = in_order(d_second, swapped[:, half:], 1)

    gathered, near = call(
        transposed_kernel,
        (
            jax.ShapeDtypeStruct((nodes_here, hidden_units), F32),
            jax.ShapeDtypeStruct((BAND * nodes_here, hidden_units), BF16),
        ),
        [pltpu.VMEM(((BAND + 1) * nodes_here, hidden_units), F32)],
        [side_places, tile_rows, side_valid.astype(jnp.int32)],
        [tile_values, d_second],
        1 << 28,
    )
    for d in range(1, BAND + 1):
        gathered = gathered + lax.ppermute(
            near[(d - 1) * nodes_here : d * nodes_here], AXES, side_routes(blocks, d, True)
        ).astype(F32)
    d_projected = (gathered + other_core(gathered)).astype(BF16)

    d_hidden = lax.dot_general(
        d_projected,
        mine(weight_hidden, 0),
        (((1,), (1,)), ((), ())),
        preferred_element_type=F32,
    )
    d_first_y = d_hidden * silu_grad(y_first)
    sums = run_sums(jnp.concatenate([d_first_y, d_first_y * normed_first], axis=1))
    direct = dot(slope_first * d_first_y, agg_wide, ((0,), (0,)))
    w2_part = lax.dot_general(
        mine(d_projected, 1), hidden, (((0,), (0,)), ((), ())), preferred_element_type=F32
    )
    message = jnp.concatenate([sums[:, :half].T, sums[:, half:].T], axis=1)
    got = exchange(
        jnp.concatenate(
            [
                w2_part.reshape(blocks, items, h_half),
                direct.reshape(blocks, items, f_half),
                to_owners(message),
                jnp.zeros((blocks, items, 128 - f_half - 2 * RUNS), F32),
            ],
            axis=2,
        )
    )
    width = h_half + 128

    def first_owner(first, second, *args):
        out = jax.ShapeDtypeStruct((blocks, width), F32)
        return call(first_owner_kernel, out, [], [], [lines(first), lines(second), *args], 1 << 28)

    final = exchange(
        per_item(
            first_owner, got_first, got_second, state_first, state, owned, got
        )
    )
    final = final.reshape(4 * half, 128)
    grad_w1, grad_w2, grad_norm = call(
        final_kernel,
        (
            jax.ShapeDtypeStruct((features, hidden_units), F32),
            jax.ShapeDtypeStruct((hidden_units, hidden_units), F32),
            jax.ShapeDtypeStruct((2, 3, hidden_units), F32),
        ),
        [],
        [core],
        [final, other_core(final)],
        1 << 20,
    )
    return (node_out, grad_w1, grad_w2, grad_norm)


def solution(mesh):
    in_specs = (
        P("blk", None),
        P("blk", None, None),
        P("blk"),
        P("blk"),
        P("blk"),
        P("blk"),
        P(),
        P(),
        P(),
        P("blk", None),
    )
    out_specs = (P("blk", None), P(), P(), P())
    return jax.shard_map(shards, mesh=mesh, in_specs=in_specs, out_specs=out_specs, check_vma=False)
```

```python
import jax
import jax.numpy as jnp
from jax import lax
from jax.experimental import pallas as pl
from jax.experimental.pallas import tpu as pltpu
from jax.sharding import PartitionSpec as P

BAND = 3
RUNS = 4
EPSILON = 1e-05
F32 = jnp.float32
BF16 = jnp.bfloat16
HIGH = lax.Precision.HIGHEST
AXES = ("blk", "rep")


def dot(a, b, contract):
    return lax.dot_general(a, b, (contract, ((), ())), precision=HIGH)


def other_core(x):
    return lax.ppermute(x, "rep", [(0, 1), (1, 0)])


def side_routes(blocks, distance, outward):
    routes = []
    for i in range(blocks):
        low, high = (i - distance) % blocks, (i + distance) % blocks
        if outward:
            routes += [(i * 2, low * 2), (i * 2 + 1, high * 2 + 1)]
        else:
            routes += [(low * 2, i * 2), (high * 2 + 1, i * 2 + 1)]
    return routes


def exchange(x):
    return lax.all_to_all(x, "blk", 0, 0, tiled=True)


def tile_products(pieces, values, rows, places, valid, row_tiles):
    tile = values.shape[1]
    width = pieces.shape[1]
    picked = pieces.reshape(-1, tile, width)[places]
    zero = jnp.zeros((), picked.dtype)
    masked = [
        jnp.where((valid & (rows == r))[:, None, None], picked, zero) for r in range(row_tiles)
    ]
    product = lax.dot_general(
        values,
        jnp.concatenate(masked, axis=2),
        (((0, 2), (0, 1)), ((), ())),
        preferred_element_type=F32,
    )
    return jnp.concatenate(
        [product[:, r * width : (r + 1) * width] for r in range(row_tiles)], axis=0
    )


def parts_of(x):
    high = x.astype(BF16)
    rest = x - high.astype(F32)
    middle = rest.astype(BF16)
    return high, middle, (rest - middle.astype(F32)).astype(BF16)


def hot_dot(hot, x):
    return sum(jnp.dot(hot, part, preferred_element_type=F32) for part in parts_of(x))


def spread_of(total, count, mean, alpha):
    kept = (1.0 - alpha) * mean
    return jnp.sqrt(total / count + kept * kept + EPSILON)


def owner_hots(stats):
    blocks = stats.shape[0]
    flipped = stats.T
    across = lax.broadcasted_iota(jnp.int32, (blocks, blocks), 1).astype(F32)
    down = lax.broadcasted_iota(jnp.int32, (blocks, blocks), 0).astype(F32)
    to_comp = [
        (down == flipped[28 + j : 29 + j, :]).astype(F32).astype(BF16) for j in range(RUNS)
    ]
    to_run = [(across == stats[:, 28 + j : 29 + j]).astype(F32).astype(BF16) for j in range(RUNS)]
    return to_comp, to_run


def comp_sums(to_comp, x, firsts):
    lane = lax.broadcasted_iota(jnp.int32, x.shape, 1) % RUNS
    total = jnp.zeros(x.shape, F32)
    for j in range(RUNS):
        total += jnp.where(lane == j, hot_dot(to_comp[j], x), 0.0)
    return [sum(total[:, f + j : f + j + 1] for j in range(RUNS)) for f in firsts]


def in_lanes(columns, shape):
    lane = lax.broadcasted_iota(jnp.int32, shape, 1) % len(columns)
    out = jnp.broadcast_to(columns[0], shape)
    for q in range(1, len(columns)):
        out = jnp.where(lane == q, columns[q], out)
    return out


def run_columns(stats, i, j):
    return stats[:, 4 * i + j : 4 * i + j + 1]


def norm_owner_kernel(stats, owned, lowest, middle, highest, back, state, ready):
    blocks = stats.shape[0] // 3
    stats = stats[pl.ds(0, blocks, stride=3), :]
    shape = (blocks, 128)
    lane = lax.broadcasted_iota(jnp.int32, shape, 1)
    to_comp, to_run = owner_hots(stats)
    total, count = comp_sums(to_comp, stats, (0, 24))
    mean = total / count
    wide = jnp.broadcast_to(mean, shape)
    total = jnp.zeros((blocks, 1), F32)
    for j in range(RUNS):
        n = run_columns(stats, 6, j)
        here = hot_dot(to_run[j], wide)[:, :1]
        apart = run_columns(stats, 0, j) / jnp.maximum(n, 1.0) - here
        x = jnp.broadcast_to(run_columns(stats, 1, j) + n * apart * apart, shape)
        total += hot_dot(to_comp[j], x)[:, :1]
    spread = spread_of(total, count, mean, owned[:, 2:3])
    give = in_lanes([mean, 1.0 / spread, mean, mean], shape)
    own = jnp.zeros(shape, F32)
    for j in range(RUNS):
        here = jnp.where(lane % 4 == 2, run_columns(stats, 6, j), hot_dot(to_run[j], give))
        own = jnp.where(lane % 16 // 4 == j, here, own)
    out = own
    for k in range(1, 2 * BAND + 1):
        away = -k if k <= BAND else k - BAND
        out = jnp.where(lane // 16 == k, pltpu.roll(own, -away % blocks, 0), out)
    back[...] = out
    state[...] = in_lanes([mean, spread, count, count], shape)
    ready[...] = jnp.broadcast_to((count[:1, :] >= 0.0).astype(F32), ready.shape).astype(BF16)


def second_owner_kernel(stats, owned, back, state):
    blocks = stats.shape[0] // 3
    stats = stats[pl.ds(0, blocks, stride=3), :]
    shape = (blocks, 128)
    to_comp, to_run = owner_hots(stats)
    total, rows, count = comp_sums(to_comp, stats, (0, 8, 24))
    mean = total / count
    wide = jnp.broadcast_to(mean, shape)
    total = jnp.zeros(shape, F32)
    for j in range(RUNS):
        value = [run_columns(stats, i, j) for i in range(4)]
        n = run_columns(stats, 6, j)
        here = hot_dot(to_run[j], wide)[:, :1]
        apart = value[0] / jnp.maximum(n, 1.0) - here
        x = in_lanes([value[1] + n * apart * apart, value[3] + apart * value[2]], shape)
        total += hot_dot(to_comp[j], x)
    gamma, alpha = owned[:, 3:4], owned[:, 5:6]
    spread = spread_of(total[:, :1], count, mean, alpha)
    kept = (1.0 - alpha) * mean
    proj = (total[:, 1:2] + kept * rows) / spread
    whole = gamma / spread * (rows - kept * proj / spread)
    give = in_lanes([alpha * mean, 1.0 / spread, proj / count, alpha * whole / count], shape)
    lane = lax.broadcasted_iota(jnp.int32, shape, 1)
    out = jnp.zeros(shape, F32)
    for j in range(RUNS):
        out = jnp.where(lane // 4 == j, hot_dot(to_run[j], give), out)
    back[...] = out
    grads = [jnp.sum(c, axis=0, keepdims=True) for c in (proj, rows, mean * whole)]
    state[...] = in_lanes([grads[0], grads[1], -grads[2], grads[0]], shape)


def first_owner_kernel(first, second, state, grads_second, owned, sums, final):
    blocks = first.shape[0] // 3
    shape = (blocks, 128)
    stats = first[pl.ds(0, blocks, stride=3), :]
    feat = [first[pl.ds(1 + t, blocks, stride=3), :] for t in range(2)]
    cross = [second[pl.ds(1 + t, blocks, stride=3), :] for t in range(2)]
    f_half = 64
    to_comp, to_run = owner_hots(stats)
    h_half = sums.shape[1] - 128
    rows, proj = comp_sums(to_comp, sums[:, h_half:], (f_half, f_half + RUNS))
    mean, spread, count = state[:, :1], state[:, 1:2], state[:, 2:3]
    gamma, alpha = owned[:, :1], owned[:, 2:3]
    whole = gamma / spread * (rows - (1.0 - alpha) * mean * proj / spread)
    give = in_lanes([gamma / spread * proj / count, alpha * whole / count], shape)
    lane = lax.broadcasted_iota(jnp.int32, shape, 1)
    less = jnp.zeros((1, 128), F32)
    for t in range(2):
        here = [hot_dot(to_run[2 * t + j], give) for j in range(2)]
        on_cross = jnp.where(lane < f_half, here[0][:, :1], here[1][:, :1])
        on_feat = jnp.where(lane < f_half, here[0][:, 1:2], here[1][:, 1:2])
        less += jnp.sum(on_cross * cross[t] + on_feat * feat[t], axis=0, keepdims=True)
    added = jnp.sum(sums[...], axis=0, keepdims=True)
    tail = added[:, h_half : h_half + f_half]
    tail = tail - less[:, :f_half] - less[:, f_half:]
    grads = [jnp.sum(c, axis=0, keepdims=True) for c in (proj, rows, mean * whole)]
    lane = lax.broadcasted_iota(jnp.int32, (1, 128 - f_half), 1)
    rest = jnp.zeros((1, 128 - f_half), F32)
    values = [grads[0], grads[1], -grads[2]] + [grads_second[:1, q : q + 1] for q in range(3)]
    for q in range(6):
        rest = jnp.where(lane == q, values[q], rest)
    row = jnp.concatenate([added[:, :h_half], tail, rest], axis=1)
    final[...] = jnp.broadcast_to(row, final.shape)


def run_hots(run_row, run_column, agg):
    rows = lax.broadcasted_iota(jnp.int32, (8, run_row.shape[1]), 0).astype(F32)
    hot = (rows == run_row[...]).astype(F32).astype(BF16)
    at = run_column[...]

    def to_nodes(table):
        out = jnp.broadcast_to(table[0:1, :], agg.shape)
        for j in range(1, RUNS):
            out = jnp.where(at == float(j), table[j : j + 1, :], out)
        return out

    return hot, to_nodes


def store_message(message, stats, wide):
    half = message.shape[0] // 6
    lines = jnp.concatenate(stats, axis=0).T
    for h in range(2):
        message[pl.ds(3 * h, half, stride=6), :] = lines
        for t in range(2):
            message[pl.ds(3 * h + 1 + t, half, stride=6), :] = wide(h, t)


def first_kernel(
    places, rows, count, own, near, other, values, weight, run_row, run_column, info, agg, message, all_, total
):
    nodes = own.shape[0]
    tile = values.shape[1]
    half = weight.shape[1]
    all_[:nodes, :] = own[...]
    all_[nodes : nodes + near.shape[0], :] = near[...]
    all_[nodes + near.shape[0] :, :] = other[...]
    total[...] = jnp.zeros_like(total)

    def slot(s, unused):
        source = pl.ds(pl.multiple_of(places[s] * tile, tile), tile)
        target = pl.ds(pl.multiple_of(rows[s] * tile, tile), tile)
        total[target, :] += jnp.dot(values[s], all_[source, :], preferred_element_type=F32)
        return unused

    lax.fori_loop(0, count[0], slot, 0)
    low = total[...].astype(BF16)
    agg[...] = low
    z = jnp.dot(low, weight[...], preferred_element_type=F32)
    hot, to_nodes = run_hots(run_row, run_column, z)
    sums = hot_dot(hot, z)
    offset = z - to_nodes(sums[:RUNS, :] / jnp.maximum(info[:RUNS, :], 1.0))
    squares = hot_dot(hot, offset * offset)
    feat = jnp.dot(hot, low, preferred_element_type=F32)
    f_half = feat.shape[1] // 2

    def wide(h, t):
        line = [feat[2 * t + j : 2 * t + j + 1, h * f_half : (h + 1) * f_half] for j in range(2)]
        return jnp.broadcast_to(jnp.concatenate(line, axis=1), (half, 2 * f_half))

    stats = [sums[:RUNS, :], squares[:RUNS, :], jnp.zeros((4 * RUNS, half), F32), info[...]]
    store_message(message, stats + [jnp.zeros((128 - 8 * RUNS, half), F32)], wide)


def forward_kernel(
    places,
    rows,
    count,
    core,
    agg,
    near,
    far,
    weight_in,
    weight_out,
    own,
    other,
    params,
    values,
    run_row,
    run_column,
    info,
    d_out,
    z,
    message,
    hidden,
    normed_own,
    y_own,
    slope_own,
    proj,
    table,
    all_,
):
    nodes = hidden.shape[0]
    width = hidden.shape[1]
    half = width // 2
    lower = core[0] == 0
    mine = own[pl.ds(0, half, stride=2), :].T
    theirs = other[pl.ds(0, half, stride=2), :].T
    table[:, :half] = jnp.where(lower, mine, theirs)
    table[:, half:] = jnp.where(lower, theirs, mine)

    all_[:nodes, :] = agg[...]
    all_[nodes : nodes + near.shape[0], :] = near[...]
    all_[nodes + near.shape[0] :, :] = far[...]

    def own_half(x):
        return jnp.where(lower, x[:, :half], x[:, half:])

    tile = values.shape[1]
    node = lax.broadcasted_iota(jnp.int32, (nodes, width), 0).astype(F32)

    def block(k, unused):
        at = pl.ds(pl.multiple_of(k * nodes, nodes), nodes)
        first = jnp.dot(all_[at, :], weight_in[...], preferred_element_type=F32)
        swapped = jnp.where(k == 0, 0, jnp.where(k <= BAND, k + BAND, k - BAND))
        here = jnp.where(lower, k, swapped)
        rows_here = table[pl.ds(pl.multiple_of(here * 16, 16), 16), :]
        mean = jnp.broadcast_to(rows_here[0:1, :], (nodes, width))
        inverse = jnp.broadcast_to(rows_here[1:2, :], (nodes, width))
        start = rows_here[2:3, :]
        for j in range(1, RUNS):
            later = node >= start
            mean = jnp.where(later, rows_here[4 * j : 4 * j + 1, :], mean)
            inverse = jnp.where(later, rows_here[4 * j + 1 : 4 * j + 2, :], inverse)
            start = start + rows_here[4 * j + 2 : 4 * j + 3, :]
        normed = (first - params[2:3, :] * mean) * inverse
        y = params[0:1, :] * normed + params[1:2, :]
        low = (y / (1.0 + jnp.exp(-y))).astype(BF16)

        @pl.when(k == 0)
        def _():
            hidden[...] = low
            normed_own[...] = own_half(normed)
            y_own[...] = own_half(y)
            slope_own[...] = own_half(params[0:1, :] * inverse)

        proj[at, :] = jnp.dot(low, weight_out[...], preferred_element_type=F32).astype(BF16)
        return unused

    lax.fori_loop(0, 2 * BAND + 1, block, 0)
    z[...] = jnp.zeros_like(z)

    def slot(s, unused):
        source = pl.ds(pl.multiple_of(places[s] * tile, tile), tile)
        target = pl.ds(pl.multiple_of(rows[s] * tile, tile), tile)
        z[target, :] += jnp.dot(values[s], proj[source, :], preferred_element_type=F32)
        return unused

    lax.fori_loop(0, count[0], slot, 0)
    hot, to_nodes = run_hots(run_row, run_column, z)
    sums = hot_dot(hot, z[...])
    offset = z[...] - to_nodes(sums[:RUNS, :] / jnp.maximum(info[:RUNS, :], 1.0))
    stats = [sums, hot_dot(hot, offset * offset), hot_dot(hot, d_out[...])]
    stats = [x[:RUNS, :] for x in stats + [hot_dot(hot, offset * d_out[...])]]
    stats += [jnp.zeros((2 * RUNS, half), F32), info[...]]
    flipped = parts_of(normed_own[...].T)
    cross = []
    for j in range(RUNS):
        here = jnp.where(run_column[...] == float(j), agg[...].astype(F32), 0.0).astype(BF16)
        cross.append(sum(jnp.dot(x, here, preferred_element_type=F32) for x in flipped))
    f_half = cross[0].shape[1] // 2

    def wide(h, t):
        return jnp.concatenate(
            [cross[2 * t + j][:, h * f_half : (h + 1) * f_half] for j in range(2)], axis=1
        )

    store_message(message, stats + [jnp.zeros((128 - 8 * RUNS, half), F32)], wide)


def transposed_kernel(places, rows, live, values, grads, own, near, total):
    tile = values.shape[1]
    nodes = grads.shape[0]
    total[...] = jnp.zeros_like(total)
    for s in range(values.shape[0]):

        @pl.when(live[s] > 0)
        def _():
            source = pl.ds(pl.multiple_of(rows[s] * tile, tile), tile)
            target = pl.ds(pl.multiple_of(places[s] * tile, tile), tile)
            total[target, :] += lax.dot_general(
                values[s], grads[source, :], (((0,), (0,)), ((), ())), preferred_element_type=F32
            )

    own[...] = total[:nodes, :]
    near[...] = total[nodes:, :].astype(BF16)


def final_kernel(core, own, other, grad_w1, grad_w2, grad_norm):
    half = own.shape[0] // 4
    lower = core[0] == 0
    parts = []
    for ref in (own, other):
        second = [ref[pl.ds(2 * h, half, stride=4), :].T for h in range(2)]
        first = [ref[pl.ds(2 * h + 1, half, stride=4), :].T for h in range(2)]
        f_half = grad_w1.shape[0] // 2
        parts.append(
            (
                jnp.concatenate([x[:f_half, :] for x in first], axis=0),
                jnp.concatenate(second, axis=0),
                first[0][f_half : f_half + 8, :],
            )
        )
    for out, mine, theirs in zip((grad_w1, grad_w2), *[p[:2] for p in parts]):
        out[:, :half] = jnp.where(lower, mine, theirs)
        out[:, half:] = jnp.where(lower, theirs, mine)
    for i in range(2):
        mine, theirs = [p[2][3 * i : 3 * i + 3, :] for p in parts]
        grad_norm[i, :, :half] = jnp.where(lower, mine, theirs)
        grad_norm[i, :, half:] = jnp.where(lower, theirs, mine)


def call(kernel, outs, scratch, scalars, arrays, cost):
    return pl.pallas_call(
        kernel,
        out_shape=outs,
        in_specs=[pl.BlockSpec(memory_space=pltpu.SMEM)] * len(scalars)
        + [pl.BlockSpec(memory_space=pltpu.VMEM)] * len(arrays),
        out_specs=jax.tree.map(lambda _: pl.BlockSpec(memory_space=pltpu.VMEM), outs),
        scratch_shapes=scratch,
        cost_estimate=pl.CostEstimate(flops=cost, bytes_accessed=1 << 20, transcendentals=0),
        compiler_params=pltpu.CompilerParams(vmem_limit_bytes=40 << 20),
    )(*scalars, *arrays)


def silu_grad(values):
    logistic = jax.nn.sigmoid(values)
    return logistic * (1.0 + values * (1.0 - logistic))


def shards(
    node_feat,
    tile_values,
    tile_rows,
    tile_cols,
    tile_count,
    comp_ids,
    weight_in,
    weight_hidden,
    norm_params,
    cotangent,
):
    nodes_here, features = node_feat.shape
    hidden_units = weight_hidden.shape[0]
    tile = tile_values.shape[1]
    row_tiles = nodes_here // tile
    blocks = lax.axis_size("blk")
    b = lax.axis_index("blk")
    r = lax.axis_index("rep")
    half = hidden_units // 2
    items = 2 * half // blocks
    f_half = features // 2
    h_half = hidden_units // 2

    slots = jnp.arange(tile_values.shape[0], dtype=jnp.int32)
    valid = slots < tile_count[0]
    distance = (tile_cols // row_tiles - b) % blocks
    signed = jnp.where(distance > blocks // 2, distance - blocks, distance)
    signed = jnp.where(valid, signed, 0)
    within = tile_cols % row_tiles
    places = jnp.where(signed > 0, BAND + signed, -signed) * row_tiles + within
    own_side = jnp.where(signed == 0, r == 0, (signed < 0) == (r == 0))
    side_valid = valid & own_side
    side_places = jnp.where(side_valid, jnp.abs(signed) * row_tiles + within, 0)

    node = jnp.arange(nodes_here, dtype=jnp.int32)
    changed = jnp.concatenate(
        [jnp.zeros((1,), jnp.int32), (comp_ids[1:] != comp_ids[:-1]).astype(jnp.int32)]
    )
    run_of = jnp.sum(
        jnp.where(node[None, :] <= node[:, None], changed[None, :], 0), axis=1
    )
    run_ids = jnp.arange(RUNS, dtype=jnp.int32)
    run_hot = run_of[:, None] == run_ids[None, :]
    sel = run_hot.astype(F32)
    n_run = jnp.sum(sel, axis=0)
    comp_run = jnp.max(jnp.where(run_hot, comp_ids[:, None], -1), axis=0).astype(F32)

    def run_sums(x):
        return dot(sel, x, ((0,), (0,)))

    def at_nodes(table):
        return dot(sel, table, ((1,), (0,)))

    def to_owners(columns):
        k = columns.shape[1]
        doubled = jnp.broadcast_to(columns[:, None, :], (half, 2, k))
        return doubled.reshape(blocks, items, k)

    def from_owners(x):
        k = x.shape[-1]
        return x.reshape(half, 2, k)[:, 0, :]

    def mine(x, axis):
        return lax.dynamic_slice_in_dim(x, r * half, half, axis)

    params = mine(norm_params, 2)
    column = (b * items + jnp.arange(items, dtype=jnp.int32)) // 2
    column_hot = (
        jnp.arange(half, dtype=jnp.int32)[:, None] == column[None, :]
    ).astype(F32)
    owned = dot(params.reshape(6, half), column_hot, ((1,), (0,))).reshape(2, 3, items)

    def in_order(own, other, axis):
        return jnp.where(
            r == 0,
            jnp.concatenate([own, other], axis=axis),
            jnp.concatenate([other, own], axis=axis),
        )

    def fetch(x):
        return [lax.ppermute(x, AXES, side_routes(blocks, d, False)) for d in range(1, BAND + 1)]

    run_row, run_column = run_of.astype(F32)[None, :], run_of.astype(F32)[:, None]
    run_info = jnp.broadcast_to(jnp.concatenate([n_run, comp_run])[:, None], (2 * RUNS, half))
    near_feat = jnp.concatenate(fetch(node_feat), axis=0)
    sided = jnp.where(
        signed == 0, 0, jnp.where((signed < 0) == (r == 0), 0, BAND) + jnp.abs(signed)
    )
    wide_message = jax.ShapeDtypeStruct((6 * half, 128), F32)
    agg_in, message = call(
        first_kernel,
        (jax.ShapeDtypeStruct((nodes_here, features), BF16), wide_message),
        [
            pltpu.VMEM(((2 * BAND + 1) * nodes_here, features), BF16),
            pltpu.VMEM((nodes_here, features), F32),
        ],
        [sided * row_tiles + within, tile_rows, tile_count],
        [
            node_feat,
            near_feat,
            other_core(near_feat),
            tile_values,
            mine(weight_in, 1),
            run_row,
            run_column,
            run_info,
        ],
        1 << 28,
    )
    agg_wide = agg_in.astype(F32)
    got_first = exchange(message.reshape(blocks, items, 384))
    agg_pieces = fetch(agg_in)
    owned = jnp.transpose(owned.reshape(6, items), (1, 0))[None]
    lanes = jax.ShapeDtypeStruct((blocks, 128), F32)

    def per_item(function, *args):
        if items == 1:
            return jax.tree.map(
                lambda x: x[:, None, :], function(*[x[:, 0, :] for x in args])
            )
        return jax.vmap(function, in_axes=1, out_axes=1)(*args)

    def lines(x):
        return x.reshape(3 * blocks, 128)

    def norm_owner(stats, own):
        flag = jax.ShapeDtypeStruct((16, 128), BF16)
        outs = (lanes, lanes, flag)
        return tuple(call(norm_owner_kernel, outs, [], [], [lines(stats), own, *agg_pieces], 1 << 28))

    back, state_first, ready = per_item(norm_owner, got_first, owned)
    ready = jnp.tile(ready[:, 0, :features], (nodes_here // 16, 1))
    near_agg = jnp.concatenate([x * ready for x in agg_pieces], axis=0)
    table = exchange(back).reshape(2 * half, 128)
    near_blocks = 2 * BAND + 1
    core = jnp.reshape(r, (1,))
    d_out = mine(cotangent, 1).astype(F32) / jnp.sqrt(F32(nodes_here * blocks))
    own_wide = jax.ShapeDtypeStruct((nodes_here, half), F32)
    z_second, message, hidden, normed_first, y_first, slope_first = call(
        forward_kernel,
        (
            own_wide,
            wide_message,
            jax.ShapeDtypeStruct((nodes_here, hidden_units), BF16),
            own_wide,
            own_wide,
            own_wide,
        ),
        [
            pltpu.VMEM((near_blocks * nodes_here, half), BF16),
            pltpu.VMEM((128, hidden_units), F32),
            pltpu.VMEM((near_blocks * nodes_here, features), BF16),
        ],
        [sided * row_tiles + within, tile_rows, tile_count, core],
        [
            agg_in,
            near_agg,
            other_core(near_agg),
            weight_in,
            mine(weight_hidden, 1),
            table,
            other_core(table),
            norm_params[0],
            tile_values,
            run_row,
            run_column,
            run_info,
            d_out,
        ],
        1 << 30,
    )

    got_second = exchange(message.reshape(blocks, items, 384))

    def second_owner(stats, own):
        return tuple(call(second_owner_kernel, (lanes, lanes), [], [], [lines(stats), own], 1 << 28))

    back, state = per_item(second_owner, got_second, owned)
    back = from_owners(exchange(back))
    back = jnp.transpose(back[:, : 4 * RUNS].reshape(half, RUNS, 4), (1, 2, 0))
    back = jnp.where(n_run[:, None, None] > 0, back, 0.0).reshape(RUNS, 4 * half)
    looked = at_nodes(back)
    gamma, beta = params[1, 0], params[1, 1]
    inverse = looked[:, half : 2 * half]
    normed = (z_second - looked[:, :half]) * inverse
    out_mine = (gamma * normed + beta).astype(BF16)
    d_second = gamma * inverse * (d_out - normed * looked[:, 2 * half : 3 * half])
    d_second = (d_second - looked[:, 3 * half :]).astype(BF16)
    swapped = other_core(jnp.concatenate([out_mine, d_second], axis=1))
    node_out = in_order(out_mine, swapped[:, :half], 1)
    d_second = in_order(d_second, swapped[:, half:], 1)

    gathered, near = call(
        transposed_kernel,
        (
            jax.ShapeDtypeStruct((nodes_here, hidden_units), F32),
            jax.ShapeDtypeStruct((BAND * nodes_here, hidden_units), BF16),
        ),
        [pltpu.VMEM(((BAND + 1) * nodes_here, hidden_units), F32)],
        [side_places, tile_rows, side_valid.astype(jnp.int32)],
        [tile_values, d_second],
        1 << 28,
    )
    for d in range(1, BAND + 1):
        gathered = gathered + lax.ppermute(
            near[(d - 1) * nodes_here : d * nodes_here], AXES, side_routes(blocks, d, True)
        ).astype(F32)
    d_projected = (gathered + other_core(gathered)).astype(BF16)

    d_hidden = lax.dot_general(
        d_projected,
        mine(weight_hidden, 0),
        (((1,), (1,)), ((), ())),
        preferred_element_type=F32,
    )
    d_first_y = d_hidden * silu_grad(y_first)
    sums = run_sums(jnp.concatenate([d_first_y, d_first_y * normed_first], axis=1))
    direct = dot(slope_first * d_first_y, agg_wide, ((0,), (0,)))
    w2_part = lax.dot_general(
        mine(d_projected, 1), hidden, (((0,), (0,)), ((), ())), preferred_element_type=F32
    )
    message = jnp.concatenate([sums[:, :half].T, sums[:, half:].T], axis=1)
    got = exchange(
        jnp.concatenate(
            [
                w2_part.reshape(blocks, items, h_half),
                direct.reshape(blocks, items, f_half),
                to_owners(message),
                jnp.zeros((blocks, items, 128 - f_half - 2 * RUNS), F32),
            ],
            axis=2,
        )
    )
    width = h_half + 128

    def first_owner(first, second, *args):
        out = jax.ShapeDtypeStruct((blocks, width), F32)
        return call(first_owner_kernel, out, [], [], [lines(first), lines(second), *args], 1 << 28)

    final = exchange(
        per_item(
            first_owner, got_first, got_second, state_first, state, owned, got
        )
    )
    final = final.reshape(4 * half, 128)
    grad_w1, grad_w2, grad_norm = call(
        final_kernel,
        (
            jax.ShapeDtypeStruct((features, hidden_units), F32),
            jax.ShapeDtypeStruct((hidden_units, hidden_units), F32),
            jax.ShapeDtypeStruct((2, 3, hidden_units), F32),
        ),
        [],
        [core],
        [final, other_core(final)],
        1 << 20,
    )
    return (node_out, grad_w1, grad_w2, grad_norm)


def solution(mesh):
    in_specs = (
        P("blk", None),
        P("blk", None, None),
        P("blk"),
        P("blk"),
        P("blk"),
        P("blk"),
        P(),
        P(),
        P(),
        P("blk", None),
    )
    out_specs = (P("blk", None), P(), P(), P())
    return jax.shard_map(shards, mesh=mesh, in_specs=in_specs, out_specs=out_specs, check_vma=False)
```
